32 devices in a mesh: seq: 8 (over z, x), grp: 4 (over y, core).
Axes of the slice: x: 2, y: 2, z: 4, core: 2. Of those that a mesh axis runs over, the one named last changes fastest.
Arguments:
- dec_in: bfloat16 [64, 256, 768], P(('seq', 'grp')), may hold values from -6 to 6
- memory: bfloat16 [64, 896, 768], P('grp', 'seq'), may hold values from -6 to 6
- cotangent: bfloat16 [64, 256, 768], P(('seq', 'grp')), may hold values from -6 to 6
- dec_len: int32 [64], P(('seq', 'grp')), may hold values from 1 to 256, as said below
- task_prefix: int32 [64], P(('seq', 'grp')), may hold values from 0 to 128
- owner: int32 [4, 16], replicated, may hold values from 0 to 15, each once within a row
- mem_len: int32 [64], replicated, may hold values from 224 to 896, as said below
- self_norm_gain: bfloat16 [768], replicated, may hold values from 0.5 to 1.5
- self_norm_shift: bfloat16 [768], replicated, may hold values from -1.75 to 1.75
- self_qkv: bfloat16 [768, 2304], replicated, may hold values from -0.21875 to 0.21875
- self_q_bias: bfloat16 [768], replicated, may hold values from -1.75 to 1.75
- self_v_bias: bfloat16 [768], replicated, may hold values from -1.75 to 1.75
- rel_bias_table: bfloat16 [64, 12], replicated, may hold values from -6 to 6
- self_head_gain: bfloat16 [12], replicated, may hold values from 0.5 to 1.5
- self_mix_gain: bfloat16 [768], replicated, may hold values from 0.5 to 1.5
- self_mix_shift: bfloat16 [768], replicated, may hold values from -1.75 to 1.75
- self_out: bfloat16 [768, 768], replicated, may hold values from -0.21875 to 0.21875
- self_out_bias: bfloat16 [768], replicated, may hold values from -1.75 to 1.75
- cross_norm_gain: bfloat16 [768], replicated, may hold values from 0.5 to 1.5
- cross_norm_shift: bfloat16 [768], replicated, may hold values from -1.75 to 1.75
- cross_q: bfloat16 [768, 768], replicated, may hold values from -0.21875 to 0.21875
- cross_q_bias: bfloat16 [768], replicated, may hold values from -1.75 to 1.75
- cross_kv: bfloat16 [768, 1536], replicated, may hold values from -0.21875 to 0.21875
- cross_v_bias: bfloat16 [768], replicated, may hold values from -1.75 to 1.75
- cross_head_gain: bfloat16 [12], replicated, may hold values from 0.5 to 1.5
- cross_mix_gain: bfloat16 [768], replicated, may hold values from 0.5 to 1.5
- cross_mix_shift: bfloat16 [768], replicated, may hold values from -1.75 to 1.75
- cross_out: bfloat16 [768, 768], replicated, may hold values from -0.21875 to 0.21875
- cross_out_bias: bfloat16 [768], replicated, may hold values from -1.75 to 1.75
- ffn_norm_gain: bfloat16 [768], replicated, may hold values from 0.5 to 1.5
- ffn_norm_shift: bfloat16 [768], replicated, may hold values from -1.75 to 1.75
- ffn_in: bfloat16 [768, 3072], replicated, may hold values from -0.21875 to 0.21875
- ffn_in_bias: bfloat16 [3072], replicated, may hold values from -1.75 to 1.75
- ffn_mid_gain: bfloat16 [3072], replicated, may hold values from 0.5 to 1.5
- ffn_mid_shift: bfloat16 [3072], replicated, may hold values from -1.75 to 1.75
- ffn_out: bfloat16 [3072, 768], replicated, may hold values from -0.109375 to 0.109375
- ffn_out_bias: bfloat16 [768], replicated, may hold values from -1.75 to 1.75
Outputs:
- out: bfloat16 [64, 256, 768], P(('seq', 'grp'))
- grad_dec_in: bfloat16 [64, 256, 768], P(('seq', 'grp'))
- grad_memory: bfloat16 [64, 896, 768], P('grp', 'seq')
- grad_self_norm_gain: float32 [768], P('grp')
- grad_self_norm_shift: float32 [768], P('grp')
- grad_self_qkv: float32 [768, 2304], P('grp')
- grad_self_q_bias: float32 [768], P('grp')
- grad_self_v_bias: float32 [768], P('grp')
- grad_rel_bias_table: float32 [64, 12], P('grp')
- grad_self_head_gain: float32 [12], P('grp')
- grad_self_mix_gain: float32 [768], P('grp')
- grad_self_mix_shift: float32 [768], P('grp')
- grad_self_out: float32 [768, 768], P('grp')
- grad_self_out_bias: float32 [768], P('grp')
- grad_cross_norm_gain: float32 [768], P('grp')
- grad_cross_norm_shift: float32 [768], P('grp')
- grad_cross_q: float32 [768, 768], P('grp')
- grad_cross_q_bias: float32 [768], P('grp')
- grad_cross_kv: float32 [768, 1536], P('grp')
- grad_cross_v_bias: float32 [768], P('grp')
- grad_cross_head_gain: float32 [12], P('grp')
- grad_cross_mix_gain: float32 [768], P('grp')
- grad_cross_mix_shift: float32 [768], P('grp')
- grad_cross_out: float32 [768, 768], P('grp')
- grad_cross_out_bias: float32 [768], P('grp')
- grad_ffn_norm_gain: float32 [768], P('grp')
- grad_ffn_norm_shift: float32 [768], P('grp')
- grad_ffn_in: float32 [768, 3072], P('grp')
- grad_ffn_in_bias: float32 [3072], P('grp')
- grad_ffn_mid_gain: float32 [3072], P('grp')
- grad_ffn_mid_shift: float32 [3072], P('grp')
- grad_ffn_out: float32 [3072, 768], P('grp')
- grad_ffn_out_bias: float32 [768], P('grp')
The draws below stay inside these ranges and needn't reach their ends.
Inputs may be any that keep to these rules, and one draw needn't show every extreme that they name: `dec_len`: in every draw some item has exactly 256 decoder tokens. `mem_len`: in every draw one memory item of each group of 16 has all 896 tokens valid.
All inputs are finite; a program needn't handle non-finite values.
Results may differ from the reference program's by a relative error of at most 0.018.
Values may be sent and summed in bfloat16 or wider, within the bound.
No kernel may reach another device: no remote copies, remote signals or barrier semaphores. Data moves between devices by JAX's collectives and lax.ppermute only.
A program may use at most 256 MiB of HBM per device.

```python
import math
import jax
import jax.numpy as jnp
from jax import lax

D = 768
H = 12
HD = 64
FF = 3072
NB = 64
LMAX = 256
MEM = 896
ITEM_DEV = 2
ITEMS_GRP = 16
GROUPS = 4
ITEMS = 64


def draw_dec_len(key, part):
    key = jax.random.fold_in(key, 11)
    first, second = jax.random.split(key)
    lengths = jax.random.randint(first, (ITEMS,), 1, LMAX + 1)
    picks = jax.random.randint(second, (GROUPS,), 0, ITEMS_GRP)
    return lengths.at[jnp.arange(GROUPS) * ITEMS_GRP + picks].set(LMAX).astype(jnp.int32)


def draw_mem_len(key, part):
    key = jax.random.fold_in(key, 23)
    first, second = jax.random.split(key)
    lengths = jax.random.randint(first, (ITEMS,), MEM // 4, MEM + 1)
    picks = jax.random.randint(second, (GROUPS,), 0, ITEMS_GRP)
    return lengths.at[jnp.arange(GROUPS) * ITEMS_GRP + picks].set(MEM).astype(jnp.int32)


def with_ends(values, rng, low, high):
    longest = values.shape.index(max(values.shape))
    spots = []
    for shift in (0, 1):
        where = [jax.random.randint(jax.random.fold_in(rng, axis), (), 0, length) for axis, length in enumerate(values.shape)]
        where[longest] = (where[longest] + shift) % values.shape[longest]
        spots.append(tuple(where))
    return values.at[spots[0]].set(low).at[spots[1]].set(high)


def level_of(own_key, shape, shards, smallest, high):
    def one(position, shards_of):
        draws = jax.random.uniform(jax.random.fold_in(jax.random.fold_in(own_key, 6), position), (shards_of,), jnp.float32, smallest / len(shards), high / len(shards))
        return jnp.repeat(jnp.exp(draws), shape[position] // shards_of).reshape((-1,) + (1,) * (len(shape) - position - 1))

    loudness = one(*shards[0])
    for cut in shards[1:]:
        loudness = loudness * one(*cut)
    return loudness


def noise(stream_key, extent, scale, limit, cuts=(), kind=jnp.bfloat16):
    array = jax.random.normal(stream_key, extent, jnp.float32) * scale
    if len(cuts) > 0:
        array = level_of(stream_key, extent, cuts, -0.22, 0.18) * array
    return jnp.clip(array, min=-limit, max=limit).astype(kind)


def setup_inputs(seed: int = 0) -> dict:
    seeds = jax.random.split(jax.random.key(seed), 38)
    return {
        "dec_in": noise(seeds[0], (ITEMS, LMAX, D), 1.0, 6.0, ((0, 32),)),
        "memory": noise(seeds[1], (ITEMS, MEM, D), 1.0, 6.0, ((0, 4), (1, 8))),
        "cotangent": noise(seeds[2], (ITEMS, LMAX, D), 1.0, 6.0, ((0, 32),)),
        "dec_len": draw_dec_len(jax.random.fold_in(seeds[37], 71), 0),
        "task_prefix": with_ends(jax.random.randint(seeds[4], (ITEMS,), 0, LMAX // 2 + 1), jax.random.fold_in(seeds[4], 1), 0, (LMAX // 2 + 1) - 1).astype(jnp.int32),
        "owner": jax.vmap(lambda own: jax.random.permutation(own, ITEMS_GRP))(jax.random.split(seeds[5], GROUPS)).reshape((GROUPS, ITEMS_GRP)).astype(jnp.int32),
        "mem_len": draw_mem_len(jax.random.fold_in(seeds[37], 71), 0),
        "self_norm_gain": jnp.clip(1.0 + 0.1 * jax.random.normal(seeds[7], (D,), jnp.float32), 0.5, 1.5).astype(jnp.bfloat16),
        "self_norm_shift": noise(seeds[8], (D,), 0.3, 1.75),
        "self_qkv": noise(seeds[9], (D, 3 * D), D ** -0.5, 0.21875),
        "self_q_bias": noise(seeds[10], (D,), 0.3, 1.75),
        "self_v_bias": noise(seeds[11], (D,), 0.3, 1.75),
        "rel_bias_table": noise(seeds[12], (NB, H), 1.0, 6.0),
        "self_head_gain": jnp.clip(1.0 + 0.1 * jax.random.normal(seeds[13], (H,), jnp.float32), 0.5, 1.5).astype(jnp.bfloat16),
        "self_mix_gain": jnp.clip(1.0 + 0.1 * jax.random.normal(seeds[14], (D,), jnp.float32), 0.5, 1.5).astype(jnp.bfloat16),
        "self_mix_shift": noise(seeds[15], (D,), 0.3, 1.75),
        "self_out": noise(seeds[16], (D, D), D ** -0.5, 0.21875),
        "self_out_bias": noise(seeds[17], (D,), 0.3, 1.75),
        "cross_norm_gain": jnp.clip(1.0 + 0.1 * jax.random.normal(seeds[18], (D,), jnp.float32), 0.5, 1.5).astype(jnp.bfloat16),
        "cross_norm_shift": noise(seeds[19], (D,), 0.3, 1.75),
        "cross_q": noise(seeds[20], (D, D), D ** -0.5, 0.21875),
        "cross_q_bias": noise(seeds[21], (D,), 0.3, 1.75),
        "cross_kv": noise(seeds[22], (D, 2 * D), D ** -0.5, 0.21875),
        "cross_v_bias": noise(seeds[23], (D,), 0.3, 1.75),
        "cross_head_gain": jnp.clip(1.0 + 0.1 * jax.random.normal(seeds[24], (H,), jnp.float32), 0.5, 1.5).astype(jnp.bfloat16),
        "cross_mix_gain": jnp.clip(1.0 + 0.1 * jax.random.normal(seeds[25], (D,), jnp.float32), 0.5, 1.5).astype(jnp.bfloat16),
        "cross_mix_shift": noise(seeds[26], (D,), 0.3, 1.75),
        "cross_out": noise(seeds[27], (D, D), D ** -0.5, 0.21875),
        "cross_out_bias": noise(seeds[28], (D,), 0.3, 1.75),
        "ffn_norm_gain": jnp.clip(1.0 + 0.1 * jax.random.normal(seeds[29], (D,), jnp.float32), 0.5, 1.5).astype(jnp.bfloat16),
        "ffn_norm_shift": noise(seeds[30], (D,), 0.3, 1.75),
        "ffn_in": noise(seeds[31], (D, FF), D ** -0.5, 0.21875),
        "ffn_in_bias": noise(seeds[32], (FF,), 0.3, 1.75),
        "ffn_mid_gain": jnp.clip(1.0 + 0.1 * jax.random.normal(seeds[33], (FF,), jnp.float32), 0.5, 1.5).astype(jnp.bfloat16),
        "ffn_mid_shift": noise(seeds[34], (FF,), 0.3, 1.75),
        "ffn_out": noise(seeds[35], (FF, D), FF ** -0.5, 0.109375),
        "ffn_out_bias": noise(seeds[36], (D,), 0.3, 1.75),
    }


@jax.custom_vjp
def low(v):
    return lax.optimization_barrier(v.astype(jnp.bfloat16)).astype(jnp.float32)

@jax.custom_vjp
def low_back(v):
    return v

def low_keep(v):
    return (low(v), None)

def low_pass(kept, grad):
    return (grad,)

def back_keep(v):
    return (v, None)

def back_low(kept, grad):
    return (low(grad),)
low.defvjp(low_keep, low_pass)
low_back.defvjp(back_keep, back_low)
EPSILON = 1e-05
PRECISE = lax.Precision.HIGHEST

def layer_norm(values, scaling, offset):
    average = lax.optimization_barrier(jnp.mean(values, axis=-1, keepdims=True))
    centered = values - average
    spread = lax.optimization_barrier(jnp.mean(centered * centered, axis=-1, keepdims=True))
    return centered * lax.rsqrt(spread + EPSILON) * scaling + offset

def matmul(left, right):
    return jnp.dot(left, right, precision=PRECISE, preferred_element_type=jnp.float32)

def split_heads(tensor):
    return tensor.reshape(tensor.shape[0], tensor.shape[1], H, HD)

def attention(queries, keys, values, bias, allowed):
    scores = jnp.einsum('gqhd,gkhd->ghqk', queries, keys, precision=PRECISE) * (1.0 / math.sqrt(HD))
    scores = low_back(scores + bias)
    scores = jnp.where(allowed[:, None], scores, -1000000000.0)
    probs = low(jax.nn.softmax(scores, axis=-1))
    mixed = jnp.einsum('ghqk,gkhd->gqhd', probs, values, precision=PRECISE)
    return low_back(mixed)

def serving_items(owner):
    groups, per_group = owner.shape
    group_ids = jnp.arange(groups, dtype=jnp.int32)[:, None]
    decoder_ids = (owner // ITEM_DEV * groups + group_ids) * ITEM_DEV + owner % ITEM_DEV
    memory_ids = jnp.arange(groups * per_group, dtype=jnp.int32)
    return jnp.zeros((groups * per_group,), jnp.int32).at[decoder_ids.reshape(-1)].set(memory_ids)

def block_forward(pieces, params, rel_bias):
    dec_rows, mem_rows, lengths, prefixes, mem_counts = pieces
    self_norm_gain, self_norm_shift, self_qkv, self_q_bias, self_v_bias, rel_bias_table, self_head_gain, self_mix_gain, self_mix_shift, self_out, self_out_bias, cross_norm_gain, cross_norm_shift, cross_q, cross_q_bias, cross_kv, cross_v_bias, cross_head_gain, cross_mix_gain, cross_mix_shift, cross_out, cross_out_bias, ffn_norm_gain, ffn_norm_shift, ffn_in, ffn_in_bias, ffn_mid_gain, ffn_mid_shift, ffn_out, ffn_out_bias = params
    count = dec_rows.shape[0]
    positions = jnp.arange(LMAX, dtype=jnp.int32)
    key_pos = positions[None, None, :]
    query_pos = positions[None, :, None]
    self_allowed = (key_pos < lengths[:, None, None]) & ((key_pos <= query_pos) | (key_pos < prefixes[:, None, None]))
    normed = low(layer_norm(dec_rows, self_norm_gain, self_norm_shift))
    projected = matmul(normed, self_qkv)
    queries = low(low_back(projected[..., :D] + self_q_bias))
    keys = low(low_back(projected[..., D:2 * D]))
    values = low(low_back(projected[..., 2 * D:] + self_v_bias))
    mixed = attention(split_heads(queries), split_heads(keys), split_heads(values), rel_bias, self_allowed)
    scaled = (mixed * self_head_gain[:, None]).reshape(count, LMAX, D)
    branch = low(layer_norm(scaled, self_mix_gain, self_mix_shift))
    after_self = dec_rows + low_back(matmul(branch, self_out) + self_out_bias)
    normed = low(layer_norm(after_self, cross_norm_gain, cross_norm_shift))
    queries = low(low_back(matmul(normed, cross_q) + cross_q_bias))
    memory_kv = matmul(mem_rows, cross_kv)
    keys = low(low_back(memory_kv[..., :D]))
    values = low(low_back(memory_kv[..., D:] + cross_v_bias))
    cross_allowed = jnp.broadcast_to(jnp.arange(MEM, dtype=jnp.int32)[None, None, :] < mem_counts[:, None, None], (count, LMAX, MEM))
    mixed = attention(split_heads(queries), split_heads(keys), split_heads(values), 0.0, cross_allowed)
    scaled = (mixed * cross_head_gain[:, None]).reshape(count, LMAX, D)
    branch = low(layer_norm(scaled, cross_mix_gain, cross_mix_shift))
    after_cross = after_self + low_back(matmul(branch, cross_out) + cross_out_bias)
    normed = low(layer_norm(after_cross, ffn_norm_gain, ffn_norm_shift))
    hidden = low_back(matmul(normed, ffn_in) + ffn_in_bias)
    activated = jax.nn.gelu(hidden, approximate=False)
    branch = low(layer_norm(activated, ffn_mid_gain, ffn_mid_shift))
    return after_cross + low_back(matmul(branch, ffn_out) + ffn_out_bias)

def forward(decoder, memory_all, params, dec_len, task_prefix, mem_len, mem_of):
    positions = jnp.arange(LMAX, dtype=jnp.int32)
    buckets = jnp.clip(positions[None, :] - positions[:, None], -(NB // 2), NB // 2 - 1) + NB // 2
    rel_bias = jnp.transpose(params[5][buckets], (2, 0, 1))
    memory_dec = memory_all[mem_of]
    counts_dec = mem_len[mem_of]
    size = math.gcd(ITEMS, 16)
    blocks = ITEMS // size

    def one_block(pieces):
        return block_forward(pieces, params, rel_bias)
    result = lax.map(jax.checkpoint(one_block), (decoder.reshape(blocks, size, LMAX, D), memory_dec.reshape(blocks, size, MEM, D), dec_len.reshape(blocks, size), task_prefix.reshape(blocks, size), counts_dec.reshape(blocks, size)))
    return result.reshape(ITEMS, LMAX, D)

def reference(dec_in, memory, cotangent, dec_len, task_prefix, owner, mem_len, self_norm_gain, self_norm_shift, self_qkv, self_q_bias, self_v_bias, rel_bias_table, self_head_gain, self_mix_gain, self_mix_shift, self_out, self_out_bias, cross_norm_gain, cross_norm_shift, cross_q, cross_q_bias, cross_kv, cross_v_bias, cross_head_gain, cross_mix_gain, cross_mix_shift, cross_out, cross_out_bias, ffn_norm_gain, ffn_norm_shift, ffn_in, ffn_in_bias, ffn_mid_gain, ffn_mid_shift, ffn_out, ffn_out_bias):
    weights = (self_norm_gain, self_norm_shift, self_qkv, self_q_bias, self_v_bias, rel_bias_table, self_head_gain, self_mix_gain, self_mix_shift, self_out, self_out_bias, cross_norm_gain, cross_norm_shift, cross_q, cross_q_bias, cross_kv, cross_v_bias, cross_head_gain, cross_mix_gain, cross_mix_shift, cross_out, cross_out_bias, ffn_norm_gain, ffn_norm_shift, ffn_in, ffn_in_bias, ffn_mid_gain, ffn_mid_shift, ffn_out, ffn_out_bias)
    mem_of = serving_items(owner)

    def whole(decoder, memory_all, *params):
        return forward(decoder, memory_all, params, dec_len, task_prefix, mem_len, mem_of)
    result, pullback = jax.vjp(whole, dec_in.astype(jnp.float32), memory.astype(jnp.float32), *[w.astype(jnp.float32) for w in weights])
    valid = (jnp.arange(LMAX, dtype=jnp.int32)[None, :] < dec_len[:, None]).astype(jnp.float32)
    grads = pullback(cotangent.astype(jnp.float32) * valid[:, :, None])
    return (result.astype(jnp.bfloat16), grads[0].astype(jnp.bfloat16), grads[1].astype(jnp.bfloat16), grads[2], grads[3], grads[4], grads[5], grads[6], grads[7], grads[8], grads[9], grads[10], grads[11], grads[12], grads[13], grads[14], grads[15], grads[16], grads[17], grads[18], grads[19], grads[20], grads[21], grads[22], grads[23], grads[24], grads[25], grads[26], grads[27], grads[28], grads[29], grads[30], grads[31])
```

```python
import functools
import math

import jax
import jax.numpy as jnp
from jax import lax
from jax.experimental import pallas as pl
from jax.experimental.pallas import tpu as pltpu
from jax.sharding import PartitionSpec as P

H = 12
HD = 64
EPSILON = 1e-05
FACTOR = 1.0 / math.sqrt(HD)
MASKED = -1000000000.0
F32 = jnp.float32
BF16 = jnp.bfloat16
PAIR = 2 * HD
PAIRS = H // 2
VMEM_LIMIT = 60 * 1024 * 1024

(
    SELF_GAIN,
    SELF_SHIFT,
    SELF_QB,
    SELF_VB,
    SELF_HEAD,
    SELF_MIX_GAIN,
    SELF_MIX_SHIFT,
    SELF_OB,
    CROSS_GAIN,
    CROSS_SHIFT,
    CROSS_QB,
    CROSS_VB,
    CROSS_HEAD,
    CROSS_MIX_GAIN,
    CROSS_MIX_SHIFT,
    CROSS_OB,
    FFN_GAIN,
    FFN_SHIFT,
    FFN_OB,
) = range(19)


def dot(left, right):
    return jnp.dot(left, right, preferred_element_type=F32)


def dot_rows(left, right):
    return lax.dot_general(left, right, (((1,), (1,)), ((), ())), preferred_element_type=F32)


def dot_cols(left, right):
    return lax.dot_general(left, right, (((0,), (0,)), ((), ())), preferred_element_type=F32)


def normalize(values):
    average = jnp.mean(values, axis=-1, keepdims=True)
    centered = values - average
    spread = jnp.mean(centered * centered, axis=-1, keepdims=True)
    scale = lax.rsqrt(spread + EPSILON)
    return centered * scale, scale


def normalize_back(grad, normed, scale):
    mean_grad = jnp.mean(grad, axis=-1, keepdims=True)
    mean_both = jnp.mean(grad * normed, axis=-1, keepdims=True)
    return scale * (grad - mean_grad - normed * mean_both)


def total(values):
    return jnp.sum(values.astype(F32), axis=0, keepdims=True)


def lanes(start, size):
    return pl.ds(pl.multiple_of(start, 128), size)


def pick_head(values, half, axis):
    place = lax.broadcasted_iota(jnp.int32, values.shape, axis)
    inside = (place < HD) if half == 0 else (place >= HD)
    return jnp.where(inside, values, jnp.zeros_like(values))


def attend_pair(queries, keys, values, score_fn, e_ref, inv_ref, first):
    values_t = values.T
    parts = []
    for half in range(2):
        scores = score_fn(dot_rows(keys, pick_head(queries, half, 1)), first + half)
        peak = jnp.max(scores, axis=0, keepdims=True)
        weights = jnp.exp(scores - peak)
        inverse = 1.0 / jnp.sum(weights, axis=0, keepdims=True)
        low = weights.astype(BF16)
        e_ref[first + half] = low
        inv_ref[pl.ds(first + half, 1), :] = inverse
        parts.append(dot(values_t[half * HD : (half + 1) * HD], low) * inverse)
    return jnp.concatenate(parts, axis=0).T


def attend_pair_back(queries, keys, values, grad, prod, e_ref, inv_ref, first, keep_scores):
    keys_t = keys.T
    grad_t = grad.astype(F32).T
    prod_t = prod.T
    dq, dk, dv = [], None, None
    for half in range(2):
        rows = slice(half * HD, (half + 1) * HD)
        inverse = inv_ref[pl.ds(first + half, 1), :]
        delta = jnp.sum(prod_t[rows], axis=0, keepdims=True) * inverse
        grad_half = pick_head((grad_t * inverse).astype(BF16), half, 0)
        grad_probs = dot(values, grad_half)
        low = e_ref[first + half]
        grad_scores = (low.astype(F32) * (grad_probs - delta)).astype(BF16)
        if keep_scores is not None:
            keep_scores(grad_scores, first + half)
        dq.append(dot(keys_t[rows], grad_scores))
        part_k = dot(grad_scores, pick_head(queries, half, 1))
        part_v = dot_rows(low, grad_half)
        dk = part_k if dk is None else dk + part_k
        dv = part_v if dv is None else dv + part_v
    return jnp.concatenate(dq, axis=0).T * FACTOR, dk, dv


def self_forward_kernel(
    len_ref, prefix_ref, x_ref, bias_ref, qkv_w, out_w, q2_w, vec_ref,
    n1_ref, qkv_ref, e_ref, inv_ref, mixed_ref, z1_ref, x2_ref, n2_ref, q2_ref,
):
    item = pl.program_id(0)
    width = x_ref.shape[1]
    length = x_ref.shape[0]

    def vec(row):
        return vec_ref[row : row + 1, :]

    x = x_ref[...].astype(F32)
    normed, _ = normalize(x)
    n1_ref[...] = (normed * vec(SELF_GAIN) + vec(SELF_SHIFT)).astype(BF16)
    queries = dot(n1_ref[...], qkv_w[:, :width]) + vec(SELF_QB)
    qkv_ref[:, :width] = queries.astype(BF16) * jnp.asarray(FACTOR, BF16)
    qkv_ref[:, width : 2 * width] = dot(n1_ref[...], qkv_w[:, width : 2 * width]).astype(BF16)
    values = dot(n1_ref[...], qkv_w[:, 2 * width :]) + vec(SELF_VB)
    qkv_ref[:, 2 * width :] = values.astype(BF16)
    key_pos = lax.broadcasted_iota(jnp.int32, (length, length), 0)
    query_pos = lax.broadcasted_iota(jnp.int32, (length, length), 1)
    allowed = (key_pos < len_ref[item]) & ((key_pos <= query_pos) | (key_pos < prefix_ref[item]))
    inv_ref[...] = jnp.zeros_like(inv_ref)

    def scores_of(scores, head):
        return jnp.where(allowed, scores + bias_ref[head].astype(F32), MASKED)

    def one_pair(pair, _):
        base = pair * PAIR
        mixed_ref[:, lanes(base, PAIR)] = attend_pair(
            qkv_ref[:, lanes(base, PAIR)],
            qkv_ref[:, lanes(base + width, PAIR)],
            qkv_ref[:, lanes(base + 2 * width, PAIR)],
            scores_of, e_ref, inv_ref, 2 * pair,
        )
        return 0

    lax.fori_loop(0, PAIRS, one_pair, 0)
    normed, _ = normalize(mixed_ref[...] * vec(SELF_HEAD))
    z1_ref[...] = (normed * vec(SELF_MIX_GAIN) + vec(SELF_MIX_SHIFT)).astype(BF16)
    x2 = x + dot(z1_ref[...], out_w[...]) + vec(SELF_OB)
    x2_ref[...] = x2
    normed, _ = normalize(x2)
    n2_ref[...] = (normed * vec(CROSS_GAIN) + vec(CROSS_SHIFT)).astype(BF16)
    queries = dot(n2_ref[...], q2_w[...]) + vec(CROSS_QB)
    q2_ref[...] = queries.astype(BF16) * jnp.asarray(FACTOR, BF16)


def gelu_parts(hidden):
    gate = 0.5 * (1.0 + lax.erf(hidden * math.sqrt(0.5)))
    slope = hidden * (jnp.exp(-0.5 * hidden * hidden) * (1.0 / math.sqrt(2.0 * math.pi)))
    return hidden * gate, gate + slope


def cross_forward_kernel(
    item, count, mem_len_ref, dec_len_ref, x2_ref, q2_ref, mem_ref, cot_ref,
    kv_w, out_w, in_w, ffn_w, vec_ref, wide_ref, *rest,
):
    outs = rest[len(rest) - count - 2 :]
    (
        out_ref, kv_ref, e_ref, inv_ref, mixed_ref, z2_ref, n3_ref, hid_ref, mid_ref,
        cot_low_ref, gx3_ref, branch_ref, vg_ref, wg_ref,
    ) = outs[:count]
    act_ref, slope_ref = outs[count:]
    width = x2_ref.shape[1]
    length = x2_ref.shape[0]
    mem_tokens = mem_ref.shape[0]
    ff = in_w.shape[1]
    tiles = ff // width

    def vec(row):
        return vec_ref[row : row + 1, :]

    kv_ref[:, :width] = dot(mem_ref[...], kv_w[:, :width]).astype(BF16)
    kv_ref[:, width:] = (dot(mem_ref[...], kv_w[:, width:]) + vec(CROSS_VB)).astype(BF16)
    mem_len = mem_len_ref[item]
    inv_ref[...] = jnp.zeros_like(inv_ref)

    def scores_of(scores, head):
        del head
        key_pos = lax.broadcasted_iota(jnp.int32, (mem_tokens, length), 0)
        return jnp.where(key_pos < mem_len, scores, MASKED)

    def one_pair(pair, _):
        base = pair * PAIR
        mixed_ref[:, lanes(base, PAIR)] = attend_pair(
            q2_ref[:, lanes(base, PAIR)],
            kv_ref[:, lanes(base, PAIR)],
            kv_ref[:, lanes(base + width, PAIR)],
            scores_of, e_ref, inv_ref, 2 * pair,
        )
        return 0

    lax.fori_loop(0, PAIRS, one_pair, 0)
    normed, _ = normalize(mixed_ref[...] * vec(CROSS_HEAD))
    z2_ref[...] = (normed * vec(CROSS_MIX_GAIN) + vec(CROSS_MIX_SHIFT)).astype(BF16)
    x3 = x2_ref[...] + dot(z2_ref[...], out_w[...]) + vec(CROSS_OB)
    norm3, scale3 = normalize(x3)
    n3_ref[...] = (norm3 * vec(FFN_GAIN) + vec(FFN_SHIFT)).astype(BF16)

    def hidden_tile(tile, sums):
        cols = lanes(tile * width, width)
        hidden = dot(n3_ref[...], in_w[:, cols]) + wide_ref[0:1, cols]
        act, slope = gelu_parts(hidden)
        act_ref[:, cols] = act
        slope_ref[:, cols] = slope
        return sums + jnp.sum(act, axis=-1, keepdims=True)

    sums = lax.fori_loop(0, tiles, hidden_tile, jnp.zeros((length, 1), F32))
    average = sums / ff

    def spread_tile(tile, sums):
        centered = act_ref[:, lanes(tile * width, width)] - average
        return sums + jnp.sum(centered * centered, axis=-1, keepdims=True)

    sums = lax.fori_loop(0, tiles, spread_tile, jnp.zeros((length, 1), F32))
    scale = lax.rsqrt(sums / ff + EPSILON)

    def middle_tile(tile, _):
        cols = lanes(tile * width, width)
        normed = (act_ref[:, cols] - average) * scale
        act_ref[:, cols] = normed
        mid_ref[:, cols] = (normed * wide_ref[1:2, cols] + wide_ref[2:3, cols]).astype(BF16)
        return 0

    lax.fori_loop(0, tiles, middle_tile, 0)
    result = x3 + dot(mid_ref[...], ffn_w[...]) + vec(FFN_OB)
    out_ref[...] = result.astype(BF16)

    valid = lax.broadcasted_iota(jnp.int32, (length, 1), 0) < dec_len_ref[item]
    cot = jnp.where(valid, cot_ref[...].astype(F32), 0.0)
    cot_low_ref[...] = cot.astype(BF16)
    wg_ref[...] = jnp.zeros_like(wg_ref)
    vg_ref[...] = jnp.zeros_like(vg_ref)

    def grad_mid_tile(tile, sums):
        cols = lanes(tile * width, width)
        grad_mid = dot_rows(cot_low_ref[...], ffn_w[cols, :])
        normed = act_ref[:, cols]
        wg_ref[1:2, cols] = total(grad_mid * normed)
        wg_ref[2:3, cols] = total(grad_mid)
        grad = grad_mid * wide_ref[1:2, cols]
        hid_ref[:, cols] = grad.astype(BF16)
        return (
            sums[0] + jnp.sum(grad, axis=-1, keepdims=True),
            sums[1] + jnp.sum(grad * normed, axis=-1, keepdims=True),
        )

    zero = jnp.zeros((length, 1), F32)
    sum_grad, sum_both = lax.fori_loop(0, tiles, grad_mid_tile, (zero, zero))
    mean_grad, mean_both = sum_grad / ff, sum_both / ff

    def hidden_back_tile(tile, _):
        cols = lanes(tile * width, width)
        grad = dot_rows(cot_low_ref[...], ffn_w[cols, :]) * wide_ref[1:2, cols]
        grad = scale * (grad - mean_grad - act_ref[:, cols] * mean_both)
        low = (grad * slope_ref[:, cols]).astype(BF16)
        hid_ref[:, cols] = low
        wg_ref[0:1, cols] = total(low)
        return 0

    lax.fori_loop(0, tiles, hidden_back_tile, 0)
    grad_n3 = dot_rows(hid_ref[...], in_w[...])
    vg_ref[FFN_GAIN : FFN_GAIN + 1, :] = total(grad_n3 * norm3)
    vg_ref[FFN_SHIFT : FFN_SHIFT + 1, :] = total(grad_n3)
    vg_ref[FFN_OB : FFN_OB + 1, :] = total(cot_low_ref[...])
    gx3 = normalize_back(grad_n3 * vec(FFN_GAIN), norm3, scale3) + cot
    gx3_ref[...] = gx3
    branch_ref[...] = gx3.astype(BF16)
    vg_ref[CROSS_OB : CROSS_OB + 1, :] = total(branch_ref[...])


def cross_back_kernel(
    item, count, branch_ref, gx3_ref, mixed_ref, kv_ref, e_ref, inv_ref, q2_ref, x2_ref,
    kv_w, out_w, q2_w, vec_ref, *rest,
):
    del item
    outs = rest[len(rest) - count - 2 :]
    dq_ref, dkv_ref, gmem_ref, gx2_ref, branch2_ref, vg_ref = outs[:count]
    grad_ref, prod_ref = outs[count:]
    width = x2_ref.shape[1]

    def vec(row):
        return vec_ref[row : row + 1, :]

    def put(row, value):
        vg_ref[row : row + 1, :] = value

    vg_ref[...] = jnp.zeros_like(vg_ref)
    mixed = mixed_ref[...]
    normed, scale = normalize(mixed * vec(CROSS_HEAD))
    grad = dot_rows(branch_ref[...], out_w[...])
    put(CROSS_MIX_GAIN, total(grad * normed))
    put(CROSS_MIX_SHIFT, total(grad))
    grad = normalize_back(grad * vec(CROSS_MIX_GAIN), normed, scale)
    put(CROSS_HEAD, total(grad * mixed))
    grad = (grad * vec(CROSS_HEAD)).astype(BF16)
    grad_ref[...] = grad
    prod_ref[...] = grad.astype(F32) * mixed

    def one_pair(pair, _):
        base = pair * PAIR
        cols = lanes(base, PAIR)
        dq, dk, dv = attend_pair_back(
            q2_ref[:, cols], kv_ref[:, cols], kv_ref[:, lanes(base + width, PAIR)],
            grad_ref[:, cols], prod_ref[:, cols], e_ref, inv_ref, 2 * pair, None,
        )
        dq_ref[:, cols] = dq.astype(BF16)
        dkv_ref[:, cols] = dk.astype(BF16)
        dkv_ref[:, lanes(base + width, PAIR)] = dv.astype(BF16)
        return 0

    lax.fori_loop(0, PAIRS, one_pair, 0)
    put(CROSS_VB, total(dkv_ref[:, width:]))
    step = 256

    def memory_tile(tile, _):
        cols = lanes(tile * step, step)
        gmem_ref[:, cols] = dot_rows(dkv_ref[...], kv_w[cols, :]).astype(BF16)
        return 0

    lax.fori_loop(0, width // step, memory_tile, 0)
    put(CROSS_QB, total(dq_ref[...]))
    normed, scale = normalize(x2_ref[...])
    grad = dot_rows(dq_ref[...], q2_w[...])
    put(CROSS_GAIN, total(grad * normed))
    put(CROSS_SHIFT, total(grad))
    gx2 = normalize_back(grad * vec(CROSS_GAIN), normed, scale) + gx3_ref[...]
    gx2_ref[...] = gx2
    branch2_ref[...] = gx2.astype(BF16)
    put(SELF_OB, total(branch2_ref[...]))


def self_back_kernel(
    branch_ref, gx2_ref, mixed_ref, qkv_ref, e_ref, inv_ref, x_ref, qkv_w, out_w, vec_ref,
    dqkv_ref, gx_ref, vg_ref, diag_ref, grad_ref, prod_ref,
):
    width = x_ref.shape[1]
    length = x_ref.shape[0]

    def vec(row):
        return vec_ref[row : row + 1, :]

    def put(row, value):
        vg_ref[row : row + 1, :] = value

    vg_ref[...] = jnp.zeros_like(vg_ref)
    diag_ref[...] = jnp.zeros_like(diag_ref)
    mixed = mixed_ref[...]
    normed, scale = normalize(mixed * vec(SELF_HEAD))
    grad = dot_rows(branch_ref[...], out_w[...])
    put(SELF_MIX_GAIN, total(grad * normed))
    put(SELF_MIX_SHIFT, total(grad))
    grad = normalize_back(grad * vec(SELF_MIX_GAIN), normed, scale)
    put(SELF_HEAD, total(grad * mixed))
    grad = (grad * vec(SELF_HEAD)).astype(BF16)
    grad_ref[...] = grad
    prod_ref[...] = grad.astype(F32) * mixed

    backwards = (
        lax.broadcasted_iota(jnp.int32, (length, length), 0)
        + lax.broadcasted_iota(jnp.int32, (length, length), 1)
        == length - 1
    ).astype(F32).astype(BF16)

    def keep_scores(scores, head):
        flipped = dot(backwards, scores)
        padded = jnp.concatenate([flipped, jnp.zeros_like(flipped)], axis=1)
        rolled = pltpu.roll(padded, 0, 1, stride=1, stride_axis=0)
        diag_ref[pl.ds(head, 1), :] = jnp.sum(rolled, axis=0, keepdims=True)

    def one_pair(pair, _):
        base = pair * PAIR
        cols = lanes(base, PAIR)
        dq, dk, dv = attend_pair_back(
            qkv_ref[:, cols], qkv_ref[:, lanes(base + width, PAIR)],
            qkv_ref[:, lanes(base + 2 * width, PAIR)],
            grad_ref[:, cols], prod_ref[:, cols], e_ref, inv_ref, 2 * pair, keep_scores,
        )
        dqkv_ref[:, cols] = dq.astype(BF16)
        dqkv_ref[:, lanes(base + width, PAIR)] = dk.astype(BF16)
        dqkv_ref[:, lanes(base + 2 * width, PAIR)] = dv.astype(BF16)
        return 0

    lax.fori_loop(0, PAIRS, one_pair, 0)
    put(SELF_QB, total(dqkv_ref[:, :width]))
    put(SELF_VB, total(dqkv_ref[:, 2 * width :]))
    normed, scale = normalize(x_ref[...].astype(F32))
    grad = dot_rows(dqkv_ref[...], qkv_w[...])
    put(SELF_GAIN, total(grad * normed))
    put(SELF_SHIFT, total(grad))
    gx = normalize_back(grad * vec(SELF_GAIN), normed, scale) + gx2_ref[...]
    gx_ref[...] = gx.astype(BF16)


def per_item(shape):
    return pl.BlockSpec((None,) + shape, lambda i: (i,) + (0,) * len(shape))


def whole(array):
    return pl.BlockSpec(array.shape, lambda i: (0,) * array.ndim)


def at_item(array, item):
    return pl.BlockSpec((None,) + array.shape[1:], lambda i: (item,) + (0,) * (array.ndim - 1))


SMEM = pl.BlockSpec(memory_space=pltpu.SMEM)


def item_call(kernel, name, item, items, ins, in_specs, out_shapes, scratch, before, flops):
    shapes = [jax.ShapeDtypeStruct((items,) + s, d) for s, d in out_shapes]
    specs = [at_item(s, item) for s in shapes]
    aliases = {}
    if before is not None:
        aliases = {len(ins) + i: i for i in range(len(shapes))}
        ins = tuple(ins) + tuple(before)
        in_specs = list(in_specs) + [pl.BlockSpec(memory_space=pl.ANY)] * len(shapes)
    return pl.pallas_call(
        functools.partial(kernel, item, len(shapes)),
        out_shape=shapes,
        grid=(1,),
        in_specs=in_specs,
        out_specs=specs,
        scratch_shapes=scratch,
        input_output_aliases=aliases,
        compiler_params=pltpu.CompilerParams(vmem_limit_bytes=VMEM_LIMIT),
        cost_estimate=pl.CostEstimate(flops=flops, bytes_accessed=30_000_000, transcendentals=0),
        name=name,
    )(*ins)


def self_forward(dec_len, prefix, x, bias, qkv_w, out_w, q2_w, vecs):
    items, length, width = x.shape
    outs = [
        ((length, width), BF16),
        ((length, 3 * width), BF16),
        ((H, length, length), BF16),
        ((16, length), F32),
        ((length, width), F32),
        ((length, width), BF16),
        ((length, width), F32),
        ((length, width), BF16),
        ((length, width), BF16),
    ]
    return pl.pallas_call(
        self_forward_kernel,
        out_shape=[jax.ShapeDtypeStruct((items,) + s, d) for s, d in outs],
        grid=(items,),
        in_specs=[SMEM, SMEM, per_item((length, width))]
        + [whole(a) for a in (bias, qkv_w, out_w, q2_w, vecs)],
        out_specs=[per_item(s) for s, _ in outs],
        compiler_params=pltpu.CompilerParams(vmem_limit_bytes=VMEM_LIMIT),
        cost_estimate=pl.CostEstimate(
            flops=items * 2 * length * width * 8 * width, bytes_accessed=30_000_000, transcendentals=0
        ),
        name="self_forward",
    )(dec_len, prefix, x, bias, qkv_w, out_w, q2_w, vecs)


def cross_forward(item, before, mem_len, dec_len, x2, q2, mem, cot, kv_w, out_w, in_w, ffn_w, vecs, wides):
    items, length, width = x2.shape
    mem_tokens = mem.shape[0]
    ff = in_w.shape[1]
    outs = [
        ((length, width), BF16),
        ((mem_tokens, 2 * width), BF16),
        ((H, mem_tokens, length), BF16),
        ((16, length), F32),
        ((length, width), F32),
        ((length, width), BF16),
        ((length, width), BF16),
        ((length, ff), BF16),
        ((length, ff), BF16),
        ((length, width), BF16),
        ((length, width), F32),
        ((length, width), BF16),
        (vecs.shape, F32),
        (wides.shape, F32),
    ]
    ins = (mem_len, dec_len, x2, q2, mem, cot, kv_w, out_w, in_w, ffn_w, vecs, wides)
    specs = [SMEM, SMEM, at_item(x2, item), at_item(q2, item), whole(mem), at_item(cot, item)]
    specs += [whole(a) for a in (kv_w, out_w, in_w, ffn_w, vecs, wides)]
    scratch = [pltpu.VMEM((length, ff), F32), pltpu.VMEM((length, ff), F32)]
    flops = 2 * length * width * (5 * ff + width) + 4 * mem_tokens * width * (width + 4 * length)
    return item_call(
        cross_forward_kernel, "cross_forward", item, items, ins, specs, outs, scratch, before, flops
    )


def cross_back(item, before, branch, gx3, mixed, kv, e, inv, q2, x2, kv_w, out_w, q2_w, vecs):
    items, length, width = x2.shape
    mem_tokens = kv.shape[1]
    outs = [
        ((length, width), BF16),
        ((mem_tokens, 2 * width), BF16),
        ((mem_tokens, width), BF16),
        ((length, width), F32),
        ((length, width), BF16),
        (vecs.shape, F32),
    ]
    stacked = (branch, gx3, mixed, kv, e, inv, q2, x2)
    ins = stacked + (kv_w, out_w, q2_w, vecs)
    specs = [at_item(a, item) for a in stacked] + [whole(a) for a in (kv_w, out_w, q2_w, vecs)]
    scratch = [pltpu.VMEM((length, width), BF16), pltpu.VMEM((length, width), F32)]
    flops = 2 * length * width * 2 * width + 4 * mem_tokens * width * (width + 8 * length)
    return item_call(
        cross_back_kernel, "cross_back", item, items, ins, specs, outs, scratch, before, flops
    )


def self_back(branch, gx2, mixed, qkv, e, inv, x, qkv_w, out_w, vecs):
    items, length, width = x.shape
    outs = [
        ((length, 3 * width), BF16),
        ((length, width), BF16),
        (vecs.shape, F32),
        ((16, 2 * length), F32),
    ]
    stacked = (branch, gx2, mixed, qkv, e, inv, x)
    return pl.pallas_call(
        self_back_kernel,
        out_shape=[jax.ShapeDtypeStruct((items,) + s, d) for s, d in outs],
        grid=(items,),
        in_specs=[per_item(a.shape[1:]) for a in stacked] + [whole(a) for a in (qkv_w, out_w, vecs)],
        out_specs=[per_item(s) for s, _ in outs],
        scratch_shapes=[pltpu.VMEM((length, width), BF16), pltpu.VMEM((length, width), F32)],
        compiler_params=pltpu.CompilerParams(vmem_limit_bytes=VMEM_LIMIT),
        cost_estimate=pl.CostEstimate(
            flops=items * 2 * length * width * 8 * width, bytes_accessed=30_000_000, transcendentals=0
        ),
        name="self_back",
    )(*stacked, qkv_w, out_w, vecs)


def rel_bias_of(table, length):
    count = table.shape[0]
    positions = jnp.arange(length, dtype=jnp.int32)
    offset = jnp.clip(positions[:, None] - positions[None, :], -(count // 2), count // 2 - 1)
    one_hot = (offset + count // 2)[None] == jnp.arange(count, dtype=jnp.int32)[:, None, None]
    return lax.dot_general(
        table, one_hot.astype(BF16), (((0,), (0,)), ((), ())), preferred_element_type=F32
    ).astype(BF16)


def table_grad(diag, count):
    length = diag.shape[1] // 2
    offset = length - 1 - jnp.arange(2 * length, dtype=jnp.int32)
    bucket = jnp.clip(offset, -(count // 2), count // 2 - 1) + count // 2
    one_hot = (bucket[:, None] == jnp.arange(count, dtype=jnp.int32)[None, :]).astype(F32)
    return jnp.dot(diag, one_hot, precision=lax.Precision.HIGHEST).T


def reduce_plain(grads):
    shares = [
        lax.psum_scatter(g, "grp", scatter_dimension=0, tiled=True).astype(F32) for g in grads
    ]
    return lax.psum(tuple(shares), "seq")


CORE_PAIRS = [(0, 1), (1, 0), (2, 3), (3, 2)]
Y_PAIRS = [(0, 2), (2, 0), (1, 3), (3, 1)]
X_PAIRS = [(0, 1), (1, 0), (2, 3), (3, 2), (4, 5), (5, 4), (6, 7), (7, 6)]
Z_IN = [(0, 2), (1, 3), (6, 4), (7, 5)]
Z_MID = [(2, 4), (4, 2), (3, 5), (5, 3)]
Z_OUT = [(2, 0), (3, 1), (4, 6), (5, 7)]


def add_low(left, right):
    return (left.astype(F32) + right.astype(F32)).astype(BF16)


def take_at(array, index, axis):
    return lax.dynamic_index_in_dim(array, index, axis, keepdims=False)


def reduce_pairs(local):
    group = lax.axis_index("grp")
    seq = lax.axis_index("seq")
    core, y = group % 2, group // 2
    x, z = seq % 2, seq // 2
    rows = local.shape[0]
    parts = local.reshape((2, 2, rows // 4) + local.shape[1:])
    got = lax.ppermute(take_at(parts, 1 - core, 1), "grp", CORE_PAIRS)
    mine = add_low(take_at(parts, core, 1), got)
    got = lax.ppermute(take_at(mine, 1 - y, 0), "grp", Y_PAIRS)
    mine = add_low(take_at(mine, y, 0), got)
    mine = mine.reshape((2, rows // 8) + local.shape[1:])
    got = lax.ppermute(take_at(mine, 1 - x, 0), "seq", X_PAIRS)
    mine = add_low(take_at(mine, x, 0), got)
    got = lax.ppermute(mine, "seq", Z_IN)
    mine = add_low(mine, got)
    got = lax.ppermute(mine, "seq", Z_MID)
    mine = add_low(mine, got)
    got = lax.ppermute(mine, "seq", Z_OUT)
    inner = (z == 1) | (z == 2)
    mine = jnp.where(inner, mine, got)
    got = lax.ppermute(mine, "seq", X_PAIRS)
    first = jnp.where(x == 0, mine, got)
    second = jnp.where(x == 0, got, mine)
    return jnp.concatenate([first, second], axis=0).astype(F32)


def quarter_rows(vector):
    return vector.reshape(4, -1)


def local(
    dec_in,
    memory,
    cotangent,
    dec_len,
    task_prefix,
    owner,
    mem_len,
    self_norm_gain,
    self_norm_shift,
    self_qkv,
    self_q_bias,
    self_v_bias,
    rel_bias_table,
    self_head_gain,
    self_mix_gain,
    self_mix_shift,
    self_out,
    self_out_bias,
    cross_norm_gain,
    cross_norm_shift,
    cross_q,
    cross_q_bias,
    cross_kv,
    cross_v_bias,
    cross_head_gain,
    cross_mix_gain,
    cross_mix_shift,
    cross_out,
    cross_out_bias,
    ffn_norm_gain,
    ffn_norm_shift,
    ffn_in,
    ffn_in_bias,
    ffn_mid_gain,
    ffn_mid_shift,
    ffn_out,
    ffn_out_bias,
):
    items, length, width = dec_in.shape
    rows = items * length
    items_grp = owner.shape[1]
    shard_tokens = memory.shape[1]
    seq_size = lax.axis_size("seq")
    grp_size = lax.axis_size("grp")
    mem_tokens = shard_tokens * seq_size
    group = lax.axis_index("grp")
    seq_index = lax.axis_index("seq")
    paired = seq_size == 8 and grp_size == 4

    owner_row = lax.dynamic_index_in_dim(owner, group, 0, keepdims=False)
    inverse = (
        jnp.zeros((items_grp,), jnp.int32).at[owner_row].set(jnp.arange(items_grp, dtype=jnp.int32))
    )
    mine = lax.dynamic_slice_in_dim(inverse, seq_index * items, items)
    my_mem_len = jnp.take(mem_len, group * items_grp + mine)

    memories = []
    for item in range(items):
        sent = jnp.take(memory, inverse.reshape(seq_size, items)[:, item], axis=0)
        got = lax.all_to_all(sent, "seq", split_axis=0, concat_axis=0, tiled=True)
        memories.append(got.reshape(mem_tokens, width))

    def spread(gain):
        return jnp.repeat(gain, HD)

    vectors = [
        self_norm_gain, self_norm_shift, self_q_bias, self_v_bias, spread(self_head_gain),
        self_mix_gain, self_mix_shift, self_out_bias, cross_norm_gain, cross_norm_shift,
        cross_q_bias, cross_v_bias, spread(cross_head_gain), cross_mix_gain, cross_mix_shift,
        cross_out_bias, ffn_norm_gain, ffn_norm_shift, ffn_out_bias,
    ]
    vecs = jnp.stack(vectors + [jnp.zeros_like(self_norm_gain)] * 5).astype(F32)
    wides = jnp.stack([ffn_in_bias, ffn_mid_gain, ffn_mid_shift] + [jnp.zeros_like(ffn_in_bias)] * 5)
    wides = wides.astype(F32)
    bias = rel_bias_of(rel_bias_table, length)

    n1, qkv, e1, inv1, mixed1, z1, x2, n2, q2 = self_forward(
        dec_len, task_prefix, dec_in, bias, self_qkv, self_out, cross_q, vecs
    )

    ahead, back = None, None
    returned = []
    for item in range(items):
        ahead = cross_forward(
            item, ahead, my_mem_len, dec_len, x2, q2, memories[item], cotangent,
            cross_kv, cross_out, ffn_in, ffn_out, vecs, wides,
        )
        (out, kv, e2, inv2, mixed2, z2, n3, hid, mid, cot_low, gx3, branch3, vg2, wg2) = ahead
        back = cross_back(
            item, back, branch3, gx3, mixed2, kv, e2, inv2, q2, x2,
            cross_kv, cross_out, cross_q, vecs,
        )
        dq2, dkv, gmem, gx2, branch2, vg3 = back
        sent = gmem[item].reshape(seq_size, shard_tokens, width)
        returned.append(
            lax.all_to_all(sent, "seq", split_axis=0, concat_axis=0, tiled=True)
        )
    dqkv, gx, vg4, diag = self_back(
        branch2, gx2, mixed1, qkv, e1, inv1, dec_in, self_qkv, self_out, vecs
    )

    by_slot = jnp.stack(returned, axis=1).reshape(items_grp, shard_tokens, width)
    grad_memory = jnp.take(by_slot, owner_row, axis=0)

    def weight_grad(left, right):
        return dot_cols(left.reshape(-1, left.shape[-1]), right.reshape(-1, right.shape[-1])).astype(BF16)

    grad_ffn_out = weight_grad(mid, cot_low)
    grad_ffn_in = weight_grad(n3, hid)
    grad_cross_out = weight_grad(z2, branch3)
    grad_cross_kv = sum(dot_cols(memories[i], dkv[i]) for i in range(items)).astype(BF16)
    grad_cross_q = weight_grad(n2, dq2)
    grad_self_out = weight_grad(z1, branch2)
    grad_self_qkv = weight_grad(n1, dqkv)

    vg = jnp.sum(vg2 + vg3 + vg4, axis=0)
    wg = jnp.sum(wg2, axis=0)
    heads_self = jnp.sum(vg[SELF_HEAD].reshape(H, HD), axis=1)
    heads_cross = jnp.sum(vg[CROSS_HEAD].reshape(H, HD), axis=1)
    grad_table = table_grad(jnp.sum(diag, axis=0)[:H], rel_bias_table.shape[0])

    pieces = [vg[row] for row in range(19) if row not in (SELF_HEAD, CROSS_HEAD)]
    pieces += [wg[0], wg[1], wg[2], grad_table.reshape(-1), heads_self, heads_cross]
    sizes = [p.size // grp_size for p in pieces]
    small = jnp.concatenate([p.reshape(grp_size, -1) for p in pieces], axis=1)
    small = jnp.pad(small, ((0, 0), (0, -small.shape[1] % 128)))

    big = [
        grad_ffn_out, grad_ffn_in, grad_cross_out, grad_cross_kv, grad_cross_q, grad_self_out,
        grad_self_qkv,
    ]
    if paired:
        big = [reduce_pairs(g) for g in big]
    else:
        big = reduce_plain(big)
    small = lax.psum(lax.psum_scatter(small, "grp", scatter_dimension=0, tiled=True), "seq")[0]

    ends = [sum(sizes[: i + 1]) for i in range(len(sizes))]
    small = [small[end - size : end] for end, size in zip(ends, sizes)]
    (
        g_self_norm_gain, g_self_norm_shift, g_self_q_bias, g_self_v_bias, g_self_mix_gain,
        g_self_mix_shift, g_self_out_bias, g_cross_norm_gain, g_cross_norm_shift, g_cross_q_bias,
        g_cross_v_bias, g_cross_mix_gain, g_cross_mix_shift, g_cross_out_bias, g_ffn_norm_gain,
        g_ffn_norm_shift, g_ffn_out_bias, g_ffn_in_bias, g_ffn_mid_gain, g_ffn_mid_shift, g_table,
        g_self_head, g_cross_head,
    ) = small
    g_ffn_out, g_ffn_in, g_cross_out, g_cross_kv, g_cross_q, g_self_out, g_self_qkv = big
    return (
        out,
        gx,
        grad_memory,
        g_self_norm_gain,
        g_self_norm_shift,
        g_self_qkv,
        g_self_q_bias,
        g_self_v_bias,
        g_table.reshape(-1, H),
        g_self_head,
        g_self_mix_gain,
        g_self_mix_shift,
        g_self_out,
        g_self_out_bias,
        g_cross_norm_gain,
        g_cross_norm_shift,
        g_cross_q,
        g_cross_q_bias,
        g_cross_kv,
        g_cross_v_bias,
        g_cross_head,
        g_cross_mix_gain,
        g_cross_mix_shift,
        g_cross_out,
        g_cross_out_bias,
        g_ffn_norm_gain,
        g_ffn_norm_shift,
        g_ffn_in,
        g_ffn_in_bias,
        g_ffn_mid_gain,
        g_ffn_mid_shift,
        g_ffn_out,
        g_ffn_out_bias,
    )


def solution(mesh):
    rows = P(("seq", "grp"), None, None)
    matrix, vector = P("grp", None), P("grp")
    in_specs = (rows, P("grp", "seq", None), rows, P(("seq", "grp")), P(("seq", "grp"))) + (P(),) * 32
    out_specs = (
        rows, rows, P("grp", "seq", None),
        vector, vector, matrix, vector, vector, matrix, vector, vector, vector, matrix, vector,
        vector, vector, matrix, vector, matrix, vector, vector, vector, vector, matrix, vector,
        vector, vector, matrix, vector, vector, vector, matrix, vector,
    )
    return jax.shard_map(local, mesh=mesh, in_specs=in_specs, out_specs=out_specs, check_vma=False)
```

```python
import functools
import math

import jax
import jax.numpy as jnp
from jax import lax
from jax.experimental import pallas as pl
from jax.experimental.pallas import tpu as pltpu
from jax.sharding import PartitionSpec as P

H = 12
HD = 64
EPSILON = 1e-05
FACTOR = 1.0 / math.sqrt(HD)
MASKED = -1000000000.0
F32 = jnp.float32
BF16 = jnp.bfloat16
PAIR = 2 * HD
PAIRS = H // 2

(
    SELF_GAIN,
    SELF_SHIFT,
    SELF_QB,
    SELF_VB,
    SELF_HEAD,
    SELF_MIX_GAIN,
    SELF_MIX_SHIFT,
    SELF_OB,
    CROSS_GAIN,
    CROSS_SHIFT,
    CROSS_QB,
    CROSS_VB,
    CROSS_HEAD,
    CROSS_MIX_GAIN,
    CROSS_MIX_SHIFT,
    CROSS_OB,
    FFN_GAIN,
    FFN_SHIFT,
    FFN_OB,
) = range(19)
IN_BIAS, MID_GAIN, MID_SHIFT, TABLE = 20, 24, 28, 32
VEC_ROWS = 64


def dot(left, right):
    return jnp.dot(left, right, preferred_element_type=F32)


def dot_rows(left, right):
    return lax.dot_general(left, right, (((1,), (1,)), ((), ())), preferred_element_type=F32)


def dot_cols(left, right):
    return lax.dot_general(left, right, (((0,), (0,)), ((), ())), preferred_element_type=F32)


def normalize(values):
    average = jnp.mean(values, axis=-1, keepdims=True)
    centered = values - average
    spread = jnp.mean(centered * centered, axis=-1, keepdims=True)
    scale = lax.rsqrt(spread + EPSILON)
    return centered * scale, scale


def normalize_back(grad, normed, scale):
    mean_grad = jnp.mean(grad, axis=-1, keepdims=True)
    mean_both = jnp.mean(grad * normed, axis=-1, keepdims=True)
    return scale * (grad - mean_grad - normed * mean_both)


def total(values):
    return jnp.sum(values.astype(F32), axis=0, keepdims=True)


def lanes(start, size):
    return pl.ds(pl.multiple_of(start, 128), size)


def pick_head(values, half, axis):
    place = lax.broadcasted_iota(jnp.int32, values.shape, axis)
    inside = (place < HD) if half == 0 else (place >= HD)
    return jnp.where(inside, values, jnp.zeros_like(values))


def attend_pair(queries, keys, values, score_fn, e_ref, inv_ref, first):
    values_t = values.T
    parts = []
    for half in range(2):
        scores = score_fn(dot_rows(keys, pick_head(queries, half, 1)), first + half)
        peak = jnp.max(scores, axis=0, keepdims=True)
        weights = jnp.exp(scores - peak)
        inverse = 1.0 / jnp.sum(weights, axis=0, keepdims=True)
        low = weights.astype(BF16)
        e_ref[first + half] = low
        inv_ref[pl.ds(first + half, 1), :] = inverse
        parts.append(dot(values_t[half * HD : (half + 1) * HD], low) * inverse)
    return jnp.concatenate(parts, axis=0).T


def attend_pair_back(queries, keys, values, grad, prod, e_ref, inv_ref, first, keep_scores):
    keys_t = keys.T
    grad_t = grad.astype(F32).T
    prod_t = prod.T
    dq, dk, dv = [], None, None
    for half in range(2):
        rows = slice(half * HD, (half + 1) * HD)
        inverse = inv_ref[pl.ds(first + half, 1), :]
        delta = jnp.sum(prod_t[rows], axis=0, keepdims=True) * inverse
        grad_half = pick_head((grad_t * inverse).astype(BF16), half, 0)
        grad_probs = dot(values, grad_half)
        low = e_ref[first + half]
        grad_scores = (low.astype(F32) * (grad_probs - delta)).astype(BF16)
        if keep_scores is not None:
            keep_scores(grad_scores, first + half)
        dq.append(dot(keys_t[rows], grad_scores))
        part_k = dot(grad_scores, pick_head(queries, half, 1))
        part_v = dot_rows(low, grad_half)
        dk = part_k if dk is None else dk + part_k
        dv = part_v if dv is None else dv + part_v
    return jnp.concatenate(dq, axis=0).T * FACTOR, dk, dv


def self_forward_kernel(item, io, len_ref, prefix_ref):
    io.load("x", "vecs", "qkv_w", "bias", "out_w", "q2_w")
    _, length, width = io.x.shape
    vec_ref = io.vecs

    def vec(row):
        return vec_ref[row : row + 1, :]

    io.need("x", "vecs")
    x = io.x[item].astype(F32)
    normed, _ = normalize(x)
    low = (normed * vec(SELF_GAIN) + vec(SELF_SHIFT)).astype(BF16)
    io.n1t[...] = low.T
    io.store("n1t")
    io.need("qkv_w")
    queries = dot(low, io.qkv_w[:, :width]) + vec(SELF_QB)
    io.qkv[:, :width] = queries.astype(BF16) * jnp.asarray(FACTOR, BF16)
    io.qkv[:, width : 2 * width] = dot(low, io.qkv_w[:, width : 2 * width]).astype(BF16)
    values = dot(low, io.qkv_w[:, 2 * width :]) + vec(SELF_VB)
    io.qkv[:, 2 * width :] = values.astype(BF16)
    io.store("qkv")
    key_pos = lax.broadcasted_iota(jnp.int32, (length, length), 0)
    query_pos = lax.broadcasted_iota(jnp.int32, (length, length), 1)
    allowed = (key_pos < len_ref[item]) & ((key_pos <= query_pos) | (key_pos < prefix_ref[item]))
    io.inv[...] = jnp.zeros_like(io.inv)
    io.need("bias")

    def scores_of(scores, head):
        return jnp.where(allowed, scores + io.bias[head].astype(F32), MASKED)

    def one_pair(pair, _):
        base = pair * PAIR
        io.mixed[:, lanes(base, PAIR)] = attend_pair(
            io.qkv[:, lanes(base, PAIR)],
            io.qkv[:, lanes(base + width, PAIR)],
            io.qkv[:, lanes(base + 2 * width, PAIR)],
            scores_of, io.e, io.inv, 2 * pair,
        )
        return 0

    lax.fori_loop(0, PAIRS, one_pair, 0)
    io.store("e", "inv", "mixed")
    normed, _ = normalize(io.mixed[...] * vec(SELF_HEAD))
    low = (normed * vec(SELF_MIX_GAIN) + vec(SELF_MIX_SHIFT)).astype(BF16)
    io.z1t[...] = low.T
    io.store("z1t")
    io.need("out_w")
    x2 = x + dot(low, io.out_w[...]) + vec(SELF_OB)
    io.x2[...] = x2
    io.store("x2")
    normed, _ = normalize(x2)
    low = (normed * vec(CROSS_GAIN) + vec(CROSS_SHIFT)).astype(BF16)
    io.n2t[...] = low.T
    io.need("q2_w")
    queries = dot(low, io.q2_w[...]) + vec(CROSS_QB)
    io.q2[...] = queries.astype(BF16) * jnp.asarray(FACTOR, BF16)
    io.store("n2t", "q2")


def gelu_parts(hidden):
    gate = 0.5 * (1.0 + lax.erf(hidden * math.sqrt(0.5)))
    slope = hidden * (jnp.exp(-0.5 * hidden * hidden) * (1.0 / math.sqrt(2.0 * math.pi)))
    return hidden * gate, gate + slope


def cross_forward_kernel(item, io, mem_len_ref, dec_len_ref, act_ref, slope_ref, grad_ref, mid_ref):
    io.load("mem", "kv_w", "vecs")
    length, width = io.x2.shape
    mem_tokens = io.mem.shape[0]
    ff = io.in_w.shape[1]
    tiles = ff // width
    mem_ref, kv_ref, kv_w, vec_ref, wide_ref = io.mem, io.kv, io.kv_w, io.vecs, io.wides
    e_ref, inv_ref, mixed_ref, q2_ref = io.e, io.inv, io.mixed, io.q2
    hid_ref, midt_ref, cot_low_ref, vg_ref = io.hid, io.midt, io.cot_low, io.vg
    out_w, in_w, ffn_w = io.out_w, io.in_w, io.ffn_w

    def vec(row):
        return vec_ref[row : row + 1, :]

    io.need("mem", "kv_w", "vecs")
    io.load("q2", "x2", "out_w", "in_w", "wides", "cot", "ffn_w")
    io.memt[...] = mem_ref[...].T
    io.store("memt")
    kv_ref[:, :width] = dot(mem_ref[...], kv_w[:, :width]).astype(BF16)
    kv_ref[:, width:] = (dot(mem_ref[...], kv_w[:, width:]) + vec(CROSS_VB)).astype(BF16)
    io.store("kv")
    io.need("q2")
    mem_len = mem_len_ref[item]
    inv_ref[...] = jnp.zeros_like(inv_ref)

    def scores_of(scores, head):
        del head
        key_pos = lax.broadcasted_iota(jnp.int32, (mem_tokens, length), 0)
        return jnp.where(key_pos < mem_len, scores, MASKED)

    def one_pair(pair, _):
        base = pair * PAIR
        mixed_ref[:, lanes(base, PAIR)] = attend_pair(
            q2_ref[:, lanes(base, PAIR)],
            kv_ref[:, lanes(base, PAIR)],
            kv_ref[:, lanes(base + width, PAIR)],
            scores_of, e_ref, inv_ref, 2 * pair,
        )
        return 0

    lax.fori_loop(0, PAIRS, one_pair, 0)
    io.store("e", "inv", "mixed")
    normed, _ = normalize(mixed_ref[...] * vec(CROSS_HEAD))
    low = (normed * vec(CROSS_MIX_GAIN) + vec(CROSS_MIX_SHIFT)).astype(BF16)
    io.z2t[...] = low.T
    io.store("z2t")
    io.need("x2", "out_w")
    x3 = io.x2[...] + dot(low, out_w[...]) + vec(CROSS_OB)
    norm3, scale3 = normalize(x3)
    n3 = (norm3 * vec(FFN_GAIN) + vec(FFN_SHIFT)).astype(BF16)
    io.n3t[...] = n3.T
    io.store("n3t")
    io.need("in_w", "wides")

    def hidden_tile(tile, sums):
        cols = lanes(tile * width, width)
        hidden = dot(n3, in_w[:, cols]) + wide_ref[0:1, cols]
        act, slope = gelu_parts(hidden)
        act_ref[:, cols] = act
        slope_ref[:, cols] = slope
        return sums + jnp.sum(act, axis=-1, keepdims=True)

    sums = lax.fori_loop(0, tiles, hidden_tile, jnp.zeros((length, 1), F32))
    average = sums / ff

    def spread_tile(tile, sums):
        centered = act_ref[:, lanes(tile * width, width)] - average
        return sums + jnp.sum(centered * centered, axis=-1, keepdims=True)

    sums = lax.fori_loop(0, tiles, spread_tile, jnp.zeros((length, 1), F32))
    scale = lax.rsqrt(sums / ff + EPSILON)

    def middle_tile(tile, _):
        cols = lanes(tile * width, width)
        normed = (act_ref[:, cols] - average) * scale
        act_ref[:, cols] = normed
        low = (normed * wide_ref[1:2, cols] + wide_ref[2:3, cols]).astype(BF16)
        mid_ref[:, cols] = low
        midt_ref[pl.ds(pl.multiple_of(tile * width, 128), width), :] = low.T
        return 0

    lax.fori_loop(0, tiles, middle_tile, 0)
    io.store("midt")
    io.need("ffn_w", "cot")
    result = x3 + dot(mid_ref[...], ffn_w[...]) + vec(FFN_OB)
    io.out[...] = result.astype(BF16)
    io.store("out")

    valid = lax.broadcasted_iota(jnp.int32, (length, 1), 0) < dec_len_ref[item]
    cot = jnp.where(valid, io.cot[item].astype(F32), 0.0)
    cot_low_ref[...] = cot.astype(BF16)
    io.store("cot_low")
    vg_ref[...] = jnp.zeros_like(vg_ref)

    def grad_mid_tile(tile, sums):
        cols = lanes(tile * width, width)
        grad_mid = dot_rows(cot_low_ref[...], ffn_w[cols, :])
        normed = act_ref[:, cols]
        vg_ref[pl.ds(MID_GAIN + tile, 1), :] = total(grad_mid * normed)
        vg_ref[pl.ds(MID_SHIFT + tile, 1), :] = total(grad_mid)
        grad = grad_mid * wide_ref[1:2, cols]
        grad_ref[:, cols] = grad
        return (
            sums[0] + jnp.sum(grad, axis=-1, keepdims=True),
            sums[1] + jnp.sum(grad * normed, axis=-1, keepdims=True),
        )

    zero = jnp.zeros((length, 1), F32)
    sum_grad, sum_both = lax.fori_loop(0, tiles, grad_mid_tile, (zero, zero))
    mean_grad, mean_both = sum_grad / ff, sum_both / ff

    def hidden_back_tile(tile, _):
        cols = lanes(tile * width, width)
        grad = scale * (grad_ref[:, cols] - mean_grad - act_ref[:, cols] * mean_both)
        low = (grad * slope_ref[:, cols]).astype(BF16)
        hid_ref[:, cols] = low
        vg_ref[pl.ds(IN_BIAS + tile, 1), :] = total(low)
        return 0

    lax.fori_loop(0, tiles, hidden_back_tile, 0)
    io.store("hid")
    grad_n3 = dot_rows(hid_ref[...], in_w[...])
    vg_ref[FFN_GAIN : FFN_GAIN + 1, :] = total(grad_n3 * norm3)
    vg_ref[FFN_SHIFT : FFN_SHIFT + 1, :] = total(grad_n3)
    vg_ref[FFN_OB : FFN_OB + 1, :] = total(cot_low_ref[...])
    gx3 = normalize_back(grad_n3 * vec(FFN_GAIN), norm3, scale3) + cot
    io.gx3[...] = gx3
    io.branch[...] = gx3.astype(BF16)
    io.store("gx3", "branch")
    vg_ref[CROSS_OB : CROSS_OB + 1, :] = total(io.branch[...])
    io.store("vg")


def cross_back_kernel(io, grad_ref, prod_ref):
    io.load("vecs", "branch", "out_w", "mixed", "q2", "inv", "kv", "e", "x2", "kv_w", "q2_w", "gx3")
    width = io.x2.shape[1]
    vec_ref, vg_ref = io.vecs, io.vg

    def vec(row):
        return vec_ref[row : row + 1, :]

    def put(row, value):
        vg_ref[row : row + 1, :] = value

    vg_ref[...] = jnp.zeros_like(vg_ref)
    io.need("vecs", "mixed")
    mixed = io.mixed[...]
    normed, scale = normalize(mixed * vec(CROSS_HEAD))
    io.need("branch", "out_w")
    grad = dot_rows(io.branch[...], io.out_w[...])
    put(CROSS_MIX_GAIN, total(grad * normed))
    put(CROSS_MIX_SHIFT, total(grad))
    grad = normalize_back(grad * vec(CROSS_MIX_GAIN), normed, scale)
    put(CROSS_HEAD, total(grad * mixed))
    grad = (grad * vec(CROSS_HEAD)).astype(BF16)
    grad_ref[...] = grad
    prod_ref[...] = grad.astype(F32) * mixed
    io.need("q2", "inv", "kv", "e")

    def one_pair(pair, _):
        base = pair * PAIR
        cols = lanes(base, PAIR)
        dq, dk, dv = attend_pair_back(
            io.q2[:, cols], io.kv[:, cols], io.kv[:, lanes(base + width, PAIR)],
            grad_ref[:, cols], prod_ref[:, cols], io.e, io.inv, 2 * pair, None,
        )
        io.dq[:, cols] = dq.astype(BF16)
        io.dkv[:, cols] = dk.astype(BF16)
        io.dkv[:, lanes(base + width, PAIR)] = dv.astype(BF16)
        return 0

    lax.fori_loop(0, PAIRS, one_pair, 0)
    io.store("dkv", "dq")
    put(CROSS_VB, total(io.dkv[:, width:]))
    step = 256
    io.need("kv_w")

    def memory_tile(tile, _):
        cols = lanes(tile * step, step)
        io.gmem[:, cols] = dot_rows(io.dkv[...], io.kv_w[cols, :]).astype(BF16)
        return 0

    lax.fori_loop(0, width // step, memory_tile, 0)
    io.store("gmem")
    put(CROSS_QB, total(io.dq[...]))
    io.need("x2", "q2_w", "gx3")
    normed, scale = normalize(io.x2[...])
    grad = dot_rows(io.dq[...], io.q2_w[...])
    put(CROSS_GAIN, total(grad * normed))
    put(CROSS_SHIFT, total(grad))
    gx2 = normalize_back(grad * vec(CROSS_GAIN), normed, scale) + io.gx3[...]
    io.gx2[...] = gx2
    io.branch2[...] = gx2.astype(BF16)
    io.store("gx2", "branch2")
    put(SELF_OB, total(io.branch2[...]))
    io.store("vg")


def self_back_kernel(item, io, grad_ref, prod_ref, diag_ref):
    io.load("vecs", "mixed", "branch", "out_w", "qkv", "inv", "e", "x", "qkv_w", "gx2", "buckets")
    _, length, width = io.x.shape
    vec_ref, vg_ref = io.vecs, io.vg

    def vec(row):
        return vec_ref[row : row + 1, :]

    def put(row, value):
        vg_ref[row : row + 1, :] = value

    vg_ref[...] = jnp.zeros_like(vg_ref)
    diag_ref[...] = jnp.zeros_like(diag_ref)
    io.need("vecs", "mixed")
    mixed = io.mixed[...]
    normed, scale = normalize(mixed * vec(SELF_HEAD))
    io.need("branch", "out_w")
    grad = dot_rows(io.branch[...], io.out_w[...])
    put(SELF_MIX_GAIN, total(grad * normed))
    put(SELF_MIX_SHIFT, total(grad))
    grad = normalize_back(grad * vec(SELF_MIX_GAIN), normed, scale)
    put(SELF_HEAD, total(grad * mixed))
    grad = (grad * vec(SELF_HEAD)).astype(BF16)
    grad_ref[...] = grad
    prod_ref[...] = grad.astype(F32) * mixed
    io.need("qkv", "inv", "e")

    backwards = (
        lax.broadcasted_iota(jnp.int32, (length, length), 0)
        + lax.broadcasted_iota(jnp.int32, (length, length), 1)
        == length - 1
    ).astype(F32).astype(BF16)

    def keep_scores(scores, head):
        flipped = dot(backwards, scores)
        padded = jnp.concatenate([flipped, jnp.zeros_like(flipped)], axis=1)
        rolled = pltpu.roll(padded, 0, 1, stride=1, stride_axis=0)
        diag_ref[pl.ds(head, 1), :] = jnp.sum(rolled, axis=0, keepdims=True)

    def one_pair(pair, _):
        base = pair * PAIR
        cols = lanes(base, PAIR)
        dq, dk, dv = attend_pair_back(
            io.qkv[:, cols], io.qkv[:, lanes(base + width, PAIR)],
            io.qkv[:, lanes(base + 2 * width, PAIR)],
            grad_ref[:, cols], prod_ref[:, cols], io.e, io.inv, 2 * pair, keep_scores,
        )
        io.dqkv[:, cols] = dq.astype(BF16)
        io.dqkv[:, lanes(base + width, PAIR)] = dk.astype(BF16)
        io.dqkv[:, lanes(base + 2 * width, PAIR)] = dv.astype(BF16)
        return 0

    lax.fori_loop(0, PAIRS, one_pair, 0)
    io.store("dqkv")
    io.need("buckets")
    table = jnp.dot(
        diag_ref[...], io.buckets[...], precision=lax.Precision.HIGHEST, preferred_element_type=F32
    )
    vg_ref[TABLE : TABLE + 16, : table.shape[1]] = table
    put(SELF_QB, total(io.dqkv[:, :width]))
    put(SELF_VB, total(io.dqkv[:, 2 * width :]))
    io.need("x", "qkv_w", "gx2")
    normed, scale = normalize(io.x[item].astype(F32))
    grad = dot_rows(io.dqkv[...], io.qkv_w[...])
    put(SELF_GAIN, total(grad * normed))
    put(SELF_SHIFT, total(grad))
    gx = normalize_back(grad * vec(SELF_GAIN), normed, scale) + io.gx2[...]
    io.gx[...] = gx.astype(BF16)
    io.store("gx", "vg")


SMEM = pl.BlockSpec(memory_space=pltpu.SMEM)
VMEM = pl.BlockSpec(memory_space=pltpu.VMEM)
ANY = pl.BlockSpec(memory_space=pl.ANY)
HBM = pl.BlockSpec(memory_space=pltpu.HBM)
MIB = 1024 * 1024


COST = dict(
    self_forward=11, cross_forward=28, cross_back=18, self_back=10, weight_grads=5, finish=2, split_add=1,
    gather_items=3, scatter_items=4, add=1, pick=1, vectors=1,
)
COST_SCALE = 3_000_000


class Kept:
    def __init__(self, shape, dtype):
        self.shape, self.dtype = tuple(shape), dtype


class Stored(Kept):
    pass


def call(kernel, name, ins, outs, scratch=(), after=(), limit=16, scalars=(), far=()):
    after = tuple(after)
    first = len(scalars) + len(far) + len(ins)
    last = first + len(after)

    def body(*refs):
        kernel(*refs[:first], *refs[last:])

    ins = [pltpu.with_memory_space_constraint(a, pltpu.VMEM) for a in ins]
    shapes = [
        jax.ShapeDtypeStruct(o.shape, o.dtype) if isinstance(o, Stored) else pltpu.VMEM(o.shape, o.dtype)
        for o in outs
    ]
    return pl.pallas_call(
        body,
        out_shape=shapes,
        in_specs=[SMEM] * len(scalars) + [HBM] * len(far) + [VMEM] * len(ins) + [ANY] * len(after),
        out_specs=[VMEM] * len(shapes),
        scratch_shapes=list(scratch),
        compiler_params=pltpu.CompilerParams(vmem_limit_bytes=limit * MIB),
        cost_estimate=pl.CostEstimate(flops=int(COST.get(name, 1) * 1_000_000_000), bytes_accessed=1000, transcendentals=0),
        name=name,
    )(*scalars, *far, *ins, *after)


class Stream:
    def __init__(self, ins, outs, far, near, sems):
        self.names = list(ins) + list(outs)
        self.far, self.near = dict(zip(self.names, far)), dict(zip(self.names, near))
        self.sems = dict(zip(self.names, range(len(self.names))))
        self.sem_refs = sems
        self.loading, self.storing = {}, []

    def __getattr__(self, name):
        return self.near[name]

    def load(self, *names):
        for name in names:
            copy = pltpu.make_async_copy(
                self.far[name], self.near[name], self.sem_refs.at[self.sems[name]]
            )
            copy.start()
            self.loading[name] = copy

    def need(self, *names):
        for name in names:
            self.loading.pop(name).wait()

    def store(self, *names):
        for name in names:
            copy = pltpu.make_async_copy(
                self.near[name], self.far[name], self.sem_refs.at[self.sems[name]]
            )
            copy.start()
            self.storing.append(copy)

    def drain(self):
        assert not self.loading
        for copy in self.storing:
            copy.wait()


def stream_call(kernel, name, ins, outs, scratch=(), after=(), scalars=(), limit=16, kept=()):
    after = tuple(after)
    n_in, n_out = len(ins), len(outs)
    far_outs = [n for n in outs if n not in kept]

    def body(*refs):
        refs = list(refs)

        def take(count):
            taken, refs[:] = refs[:count], refs[count:]
            return taken

        scalar_refs, far_in = take(len(scalars)), take(n_in)
        take(len(after))
        out_refs = dict(zip(outs, take(n_out)))
        near_in = take(n_in)
        near_out = dict(zip(far_outs, take(len(far_outs))))
        sems = refs.pop()
        near_out.update({n: out_refs[n] for n in kept})
        io = Stream(
            ins, outs, far_in + [out_refs[n] for n in outs], near_in + [near_out[n] for n in outs], sems
        )
        kernel(io, *scalar_refs, *refs)
        io.drain()

    shapes = [
        pltpu.VMEM(s, d) if n in kept else pltpu.HBM(s, d) for n, (s, d) in outs.items()
    ]
    buffers = [pltpu.VMEM(a.shape, a.dtype) for a in ins.values()]
    buffers += [pltpu.VMEM(*outs[n]) for n in far_outs]
    results = pl.pallas_call(
        body,
        out_shape=shapes,
        in_specs=[SMEM] * len(scalars) + [HBM] * n_in + [ANY] * len(after),
        out_specs=[VMEM if n in kept else HBM for n in outs],
        scratch_shapes=buffers + list(scratch) + [pltpu.SemaphoreType.DMA((n_in + n_out,))],
        compiler_params=pltpu.CompilerParams(vmem_limit_bytes=limit * MIB),
        cost_estimate=pl.CostEstimate(flops=int(COST.get(name, 1) * 1_000_000_000), bytes_accessed=1000, transcendentals=0),
        name=name,
    )(*scalars, *[pltpu.with_memory_space_constraint(a, pltpu.HBM) for a in ins.values()], *after)
    return Result(zip(outs, results))


class Result(dict):
    def __getattr__(self, name):
        return self[name]


def self_forward(item, dec_len, prefix, x, bias, qkv_w, out_w, q2_w, vecs, after):
    _, length, width = x.shape
    outs = {
        "n1t": ((width, length), BF16),
        "qkv": ((length, 3 * width), BF16),
        "e": ((H, length, length), BF16),
        "inv": ((16, length), F32),
        "mixed": ((length, width), F32),
        "z1t": ((width, length), BF16),
        "x2": ((length, width), F32),
        "n2t": ((width, length), BF16),
        "q2": ((length, width), BF16),
    }
    ins = dict(x=x, bias=bias, qkv_w=qkv_w, out_w=out_w, q2_w=q2_w, vecs=vecs)
    return stream_call(
        functools.partial(self_forward_kernel, item), "self_forward", ins, outs, after=after,
        scalars=(dec_len, prefix), limit=40,
    )


def cross_forward(item, mem_len, dec_len, x2, q2, mem, cot, kv_w, out_w, in_w, ffn_w, vecs, wides, after):
    length, width = x2.shape
    mem_tokens = mem.shape[0]
    ff = in_w.shape[1]
    outs = {
        "out": ((length, width), BF16),
        "kv": ((mem_tokens, 2 * width), BF16),
        "e": ((H, mem_tokens, length), BF16),
        "inv": ((16, length), F32),
        "mixed": ((length, width), F32),
        "memt": ((width, mem_tokens), BF16),
        "z2t": ((width, length), BF16),
        "n3t": ((width, length), BF16),
        "hid": ((length, ff), BF16),
        "midt": ((ff, length), BF16),
        "cot_low": ((length, width), BF16),
        "gx3": ((length, width), F32),
        "branch": ((length, width), BF16),
        "vg": ((VEC_ROWS, width), F32),
    }
    ins = dict(
        x2=x2, q2=q2, mem=mem, cot=cot, kv_w=kv_w, out_w=out_w, in_w=in_w, ffn_w=ffn_w, vecs=vecs, wides=wides
    )
    scratch = [pltpu.VMEM((length, ff), F32)] * 3 + [pltpu.VMEM((length, ff), BF16)]
    return stream_call(
        functools.partial(cross_forward_kernel, item), "cross_forward", ins, outs,
        scratch=scratch, after=after, scalars=(mem_len, dec_len), limit=58,
    )


def cross_back(branch, gx3, mixed, kv, e, inv, q2, x2, kv_w, out_w, q2_w, vecs, after):
    length, width = x2.shape
    mem_tokens = kv.shape[0]
    outs = {
        "dq": ((length, width), BF16),
        "dkv": ((mem_tokens, 2 * width), BF16),
        "gmem": ((mem_tokens, width), BF16),
        "gx2": ((length, width), F32),
        "branch2": ((length, width), BF16),
        "vg": ((VEC_ROWS, width), F32),
    }
    ins = dict(
        branch=branch, gx3=gx3, mixed=mixed, kv=kv, e=e, inv=inv, q2=q2, x2=x2,
        kv_w=kv_w, out_w=out_w, q2_w=q2_w, vecs=vecs,
    )
    scratch = [pltpu.VMEM((length, width), BF16), pltpu.VMEM((length, width), F32)]
    return stream_call(cross_back_kernel, "cross_back", ins, outs, scratch=scratch, after=after, limit=40)


def self_back(item, branch, gx2, mixed, qkv, e, inv, x, qkv_w, out_w, vecs, buckets, after):
    _, length, width = x.shape
    outs = {
        "dqkv": ((length, 3 * width), BF16),
        "gx": ((length, width), BF16),
        "vg": ((VEC_ROWS, width), F32),
    }
    ins = dict(
        branch=branch, gx2=gx2, mixed=mixed, qkv=qkv, e=e, inv=inv, x=x, qkv_w=qkv_w, out_w=out_w,
        vecs=vecs, buckets=buckets,
    )
    scratch = [
        pltpu.VMEM((length, width), BF16),
        pltpu.VMEM((length, width), F32),
        pltpu.VMEM((16, 2 * length), F32),
    ]
    return stream_call(
        functools.partial(self_back_kernel, item), "self_back", ins, outs, scratch=scratch, after=after,
        limit=36,
    )


def prepare_kernel(narrow, wide, *refs):
    ins, (vec_ref, wide_ref) = refs[: narrow + wide], refs[narrow + wide :]
    vec_ref[...] = jnp.zeros_like(vec_ref)
    wide_ref[...] = jnp.zeros_like(wide_ref)
    for row in range(narrow):
        vec_ref[row, :] = ins[row][...].astype(F32)
    for row in range(wide):
        wide_ref[row, :] = ins[narrow + row][...].astype(F32)


def prepare(vectors, wides, after):
    count = len(vectors) + len(wides)
    shapes = [
        jax.ShapeDtypeStruct((24, vectors[0].shape[0]), F32), jax.ShapeDtypeStruct((8, wides[0].shape[0]), F32)
    ]

    def body(*refs):
        prepare_kernel(len(vectors), len(wides), *refs[:count], *refs[count + len(after) :])

    return pl.pallas_call(
        body, out_shape=shapes, in_specs=[VMEM] * count + [ANY] * len(after), out_specs=[VMEM] * 2,
        name="prepare",
    )(*vectors, *wides, *after)


def rel_bias_of(table, length):
    count = table.shape[0]
    positions = jnp.arange(length, dtype=jnp.int32)
    offset = jnp.clip(positions[:, None] - positions[None, :], -(count // 2), count // 2 - 1)
    one_hot = (offset + count // 2)[None] == jnp.arange(count, dtype=jnp.int32)[:, None, None]
    return lax.dot_general(
        table, one_hot.astype(BF16), (((0,), (0,)), ((), ())), preferred_element_type=F32
    ).astype(BF16)


def bucket_lanes(length, count):
    offset = length - 1 - jnp.arange(2 * length, dtype=jnp.int32)
    bucket = jnp.clip(offset, -(count // 2), count // 2 - 1) + count // 2
    return (bucket[:, None] == jnp.arange(128, dtype=jnp.int32)[None, :]).astype(F32)


def gather_kernel(slots_ref, memory_ref, out_ref, sems):
    copies = [
        pltpu.make_async_copy(memory_ref.at[slots_ref[i]], out_ref.at[i], sems.at[i])
        for i in range(out_ref.shape[0])
    ]
    for copy in copies:
        copy.start()
    for copy in copies:
        copy.wait()


def gather_items(memory, slots, after):
    count = slots.shape[0]
    return call(
        gather_kernel, "gather_items", (), [Stored((count,) + memory.shape[1:], memory.dtype)],
        scratch=[pltpu.SemaphoreType.DMA((count,))], after=after, scalars=(slots,), far=(memory,), limit=8,
    )


def scatter_kernel(items, slots_ref, *refs):
    parts, out_ref, sems = refs[:items], refs[items], refs[items + 1]
    copies = []
    for p in range(parts[0].shape[0]):
        for j in range(items):
            i = p * items + j
            copies.append(pltpu.make_async_copy(parts[j].at[p], out_ref.at[slots_ref[i]], sems.at[i]))
    for copy in copies:
        copy.start()
    for copy in copies:
        copy.wait()


def scatter_items(parts, slots, after):
    count = slots.shape[0]
    return call(
        functools.partial(scatter_kernel, len(parts)), "scatter_items", (),
        [Stored((count,) + parts[0].shape[1:], parts[0].dtype)],
        scratch=[pltpu.SemaphoreType.DMA((count,))], after=after, scalars=(slots,), far=tuple(parts), limit=8,
    )


class Bundle:
    def __init__(self, jobs, width, parts, vectors=()):
        self.jobs, self.width, self.parts, self.vectors = jobs, width, parts, tuple(vectors)
        self.blocks = []
        row = 0
        for index, (lefts, rights) in enumerate(jobs):
            size = lefts[0].shape[0] // parts
            for column in range(rights[0].shape[1] // width):
                self.blocks.append((index, column, row, size))
                row += size
        self.vector_row = row
        self.rows = row + (VEC_ROWS if self.vectors else 0)

    def kernel(self, items, has_got, io, quarters_ref):
        io.load(*[n for n in io.names if not n.startswith("out")])
        pairs = [[io.near[f"{side}{i}_{j}"] for side in "lr" for i in range(items)] for j in range(len(self.jobs))]
        outs = [io.near[n] for n in io.names if n.startswith("out")]
        if has_got:
            got_ref = io.got
            io.need("got")
        count = len(outs) if has_got else outs[0].shape[0]

        def put(step, place, value):
            if has_got:
                value = value + got_ref[step, place, :].astype(F32)
                outs[step][place, :] = value.astype(BF16)
            else:
                outs[0][step, place, :] = value.astype(BF16)

        for index, column, row, size in self.blocks:
            if column == 0:
                io.need(*[f"{side}{i}_{index}" for side in "lr" for i in range(items)])
            lefts, rights = pairs[index][:items], pairs[index][items:]
            cols = slice(column * self.width, (column + 1) * self.width)
            chunk = 256 if size % 256 == 0 else size
            for step in range(count):
                for start in range(0, size, chunk):
                    rows = pl.ds(pl.multiple_of(quarters_ref[step] * size + start, 16), chunk)
                    value = dot(lefts[0][rows, :], rights[0][:, cols])
                    for left, right in zip(lefts[1:], rights[1:]):
                        value = value + dot(left[rows, :], right[:, cols])
                    put(step, slice(row + start, row + start + chunk), value)
        if self.vectors:
            value = jnp.zeros((VEC_ROWS, self.width), F32)
            for i in range(len(self.vectors)):
                io.need(f"v{i}")
                value = value + io.near[f"v{i}"][...]
            for step in range(count):
                put(step, slice(self.vector_row, self.rows), value)

    def compute(self, quarters, got, after):
        count = quarters.shape[0]
        ins = {}
        for index, (lefts, rights) in enumerate(self.jobs):
            ins.update({f"l{i}_{index}": left for i, left in enumerate(lefts)})
            ins.update({f"r{i}_{index}": right for i, right in enumerate(rights)})
        ins.update({f"v{i}": vector for i, vector in enumerate(self.vectors)})
        if got is None:
            outs = {"out0": ((count, self.rows, self.width), BF16)}
        else:
            ins["got"] = got
            outs = {f"out{i}": ((self.rows, self.width), BF16) for i in range(2)}
        return stream_call(
            functools.partial(self.kernel, len(self.jobs[0][0]), got is not None), "weight_grads", ins, outs,
            after=after, scalars=(quarters,), limit=30, kept=tuple(outs),
        )

    def finish_kernel(self, whole_rows, place_ref, mine_ref, got_ref, *out_refs):
        half = mine_ref.shape[0]

        def rows_of(start, size):
            pieces = []
            while size:
                side = start // half
                take = min(size, (side + 1) * half - start)
                rows = slice(start - side * half, start - side * half + take)
                if whole_rows:
                    pieces.append(mine_ref[rows, :].astype(F32))
                else:
                    own = place_ref[0] == side
                    pieces.append(jnp.where(own, mine_ref[rows, :].astype(F32), got_ref[rows, :].astype(F32)))
                start, size = start + take, size - take
            return pieces

        def store(out_ref, cols, start, size):
            done = 0
            for piece in rows_of(start, size):
                out_ref[done : done + piece.shape[0], cols] = piece
                done += piece.shape[0]

        for index, column, row, size in self.blocks:
            store(out_refs[index], slice(column * self.width, (column + 1) * self.width), row, size)
        if self.vectors:
            store(out_refs[-1], slice(None), self.vector_row, VEC_ROWS)

    def finish(self, mine, got, place, after):
        outs = [Stored((l[0].shape[0] // self.parts, r[0].shape[1]), F32) for l, r in self.jobs]
        if self.vectors:
            outs.append(Kept((VEC_ROWS, self.width), F32))
        ins = (mine, mine if got is None else got)
        return call(
            functools.partial(self.finish_kernel, got is None), "finish", ins, outs,
            after=after, scalars=(place,), limit=12,
        )


def add_low(left, right):
    return (left.astype(F32) + right.astype(F32)).astype(BF16)


def split_add_kernel(side_ref, left_ref, right_ref, sent_ref, kept_ref):
    half = sent_ref.shape[0]
    for side in range(2):
        rows = slice(side * half, (side + 1) * half)
        value = add_low(left_ref[rows, :], right_ref[rows, :])

        @pl.when(side_ref[0] == side)
        def _():
            kept_ref[...] = value

        @pl.when(side_ref[0] != side)
        def _():
            sent_ref[...] = value


def split_add(left, right, side, after):
    rows, width = left.shape
    return call(
        split_add_kernel, "split_add", (left, right), [Kept((rows // 2, width), BF16)] * 2,
        after=after, scalars=(side,), limit=8,
    )


def add_kernel(left_ref, right_ref, out_ref):
    out_ref[...] = add_low(left_ref[...], right_ref[...])


def add(left, right, after):
    return call(add_kernel, "add", (left, right), [Kept(left.shape, BF16)], after=after, limit=4)


def pick_kernel(own_ref, mine_ref, got_ref, out_ref):
    @pl.when(own_ref[0] == 1)
    def _():
        out_ref[...] = mine_ref[...]

    @pl.when(own_ref[0] != 1)
    def _():
        out_ref[...] = got_ref[...]


def pick(mine, got, own, after):
    return call(
        pick_kernel, "pick", (mine, got), [Kept(mine.shape, BF16)], after=after, scalars=(own,), limit=4
    )


def vectors_kernel(parts, group_ref, vec_ref, *refs):
    outs, scratch = refs[:-1], refs[-1]
    group = group_ref[0]
    width = vec_ref.shape[1]
    size = width // parts
    values = vec_ref[...]
    rolled = pltpu.roll(values, lax.rem(width - size * group, width), 1)
    narrow = [row for row in range(FFN_OB + 1) if row not in (SELF_HEAD, CROSS_HEAD)]
    for out, row in zip(outs, narrow):
        out[...] = rolled[row, :size]
    outs = outs[len(narrow) :]
    tiles = outs[0].shape[0] * parts // width
    for out, row in zip(outs, (IN_BIAS, MID_GAIN, MID_SHIFT)):
        if tiles == parts:
            out[...] = vec_ref[pl.ds(row + group, 1), :][0]
    heads = H // parts
    lane = lax.broadcasted_iota(jnp.int32, (width, 128), 0) // HD
    one_hot = (lane == lax.broadcasted_iota(jnp.int32, (width, 128), 1)).astype(F32)
    sums = jnp.dot(values, one_hot, precision=lax.Precision.HIGHEST, preferred_element_type=F32)
    sums = pltpu.roll(sums, lax.rem(128 - heads * group, 128), 1)
    outs[3][...] = sums[SELF_HEAD, :heads]
    outs[4][...] = sums[CROSS_HEAD, :heads]
    scratch[...] = values[TABLE : TABLE + 16, :128].T
    buckets = outs[5].shape[0]
    outs[5][...] = scratch[pl.ds(pl.multiple_of(buckets * group, buckets), buckets), :][:, :H]


def vector_outputs(vec, group, parts, ff, buckets, after):
    width = vec.shape[1]
    outs = [Stored((width // parts,), F32)] * 17 + [Stored((ff // parts,), F32)] * 3
    outs += [Stored((H // parts,), F32)] * 2 + [Stored((buckets // parts, H), F32)]
    return call(
        functools.partial(vectors_kernel, parts), "vectors", (vec,), outs,
        scratch=[pltpu.VMEM((128, 16), F32)], after=after, scalars=(group,), limit=8,
    )


CORE_PAIRS = [(0, 1), (1, 0), (2, 3), (3, 2)]
Y_PAIRS = [(0, 2), (2, 0), (1, 3), (3, 1)]
X_PAIRS = [(0, 1), (1, 0), (2, 3), (3, 2), (4, 5), (5, 4), (6, 7), (7, 6)]
Z_IN = [(0, 2), (1, 3), (6, 4), (7, 5)]
Z_MID = [(2, 4), (4, 2), (3, 5), (5, 3)]
Z_OUT = [(2, 0), (3, 1), (4, 6), (5, 7)]


class Chain:
    def __init__(self):
        self.last = ()

    def run(self, function, *args, also=()):
        result = function(*args, after=self.last + tuple(also))
        arrays = list(result.values()) if isinstance(result, Result) else list(result)
        self.last = (arrays[0],)
        return result if isinstance(result, Result) else arrays


def local(
    dec_in,
    memory,
    cotangent,
    dec_len,
    task_prefix,
    owner,
    mem_len,
    self_norm_gain,
    self_norm_shift,
    self_qkv,
    self_q_bias,
    self_v_bias,
    rel_bias_table,
    self_head_gain,
    self_mix_gain,
    self_mix_shift,
    self_out,
    self_out_bias,
    cross_norm_gain,
    cross_norm_shift,
    cross_q,
    cross_q_bias,
    cross_kv,
    cross_v_bias,
    cross_head_gain,
    cross_mix_gain,
    cross_mix_shift,
    cross_out,
    cross_out_bias,
    ffn_norm_gain,
    ffn_norm_shift,
    ffn_in,
    ffn_in_bias,
    ffn_mid_gain,
    ffn_mid_shift,
    ffn_out,
    ffn_out_bias,
):
    items, length, width = dec_in.shape
    items_grp = owner.shape[1]
    shard_tokens = memory.shape[1]
    seq_size = lax.axis_size("seq")
    parts = lax.axis_size("grp")
    mem_tokens = shard_tokens * seq_size
    ff = ffn_in.shape[1]
    group = lax.axis_index("grp")
    seq_index = lax.axis_index("seq")
    paired = seq_size == 8 and parts == 4 and items == 2

    owner_row = lax.dynamic_index_in_dim(owner, group, 0, keepdims=False)
    slots = jnp.arange(items_grp, dtype=jnp.int32)
    inverse = jnp.sum(jnp.where(owner_row[None, :] == slots[:, None], slots[None, :], 0), axis=1)
    mine = lax.dynamic_slice_in_dim(inverse, seq_index * items, items)
    my_mem_len = jnp.take(mem_len, group * items_grp + mine)

    def exchange(sent):
        return lax.all_to_all(sent, "seq", split_axis=0, concat_axis=0, tiled=True)

    chain = Chain()
    by_item = inverse.reshape(seq_size, items)
    memories = [exchange(chain.run(gather_items, memory, by_item[:, 0])[0])]

    def spread(gain):
        return jnp.repeat(gain, HD)

    vectors = [
        self_norm_gain, self_norm_shift, self_q_bias, self_v_bias, spread(self_head_gain),
        self_mix_gain, self_mix_shift, self_out_bias, cross_norm_gain, cross_norm_shift,
        cross_q_bias, cross_v_bias, spread(cross_head_gain), cross_mix_gain, cross_mix_shift,
        cross_out_bias, ffn_norm_gain, ffn_norm_shift, ffn_out_bias,
    ]
    vecs, wides = chain.run(prepare, vectors, [ffn_in_bias, ffn_mid_gain, ffn_mid_shift])
    bias = rel_bias_of(rel_bias_table, length)
    buckets = bucket_lanes(length, rel_bias_table.shape[0])

    starts = [
        chain.run(
            self_forward, item, dec_len, task_prefix, dec_in, bias, self_qkv, self_out, cross_q, vecs
        )
        for item in range(items)
    ]
    for item in range(1, items):
        sent = chain.run(gather_items, memory, by_item[:, item], also=memories[-1:])[0]
        memories.append(exchange(sent))
    memories = [m.reshape(mem_tokens, width) for m in memories]

    ahead, behind, returned = [], [], []

    def forward(item):
        ahead.append(
            chain.run(
                cross_forward, item, my_mem_len, dec_len, starts[item].x2, starts[item].q2, memories[item], cotangent,
                cross_kv, cross_out, ffn_in, ffn_out, vecs, wides,
            )
        )

    def backward(item):
        a = ahead[item]
        behind.append(
            chain.run(
                cross_back, a.branch, a.gx3, a.mixed, a.kv, a.e, a.inv, starts[item].q2, starts[item].x2,
                cross_kv, cross_out, cross_q, vecs,
            )
        )
        returned.append(exchange(behind[item].gmem.reshape(seq_size, shard_tokens, width)))

    ends = []

    def self_backward(item):
        a, b = starts[item], behind[item]
        ends.append(
            chain.run(
                self_back, item, b.branch2, b.gx2, a.mixed, a.qkv, a.e, a.inv, dec_in,
                self_qkv, self_out, vecs, buckets,
            )
        )

    def of(results, name):
        return [result[name] for result in results]

    def bundle_ffn_out():
        return Bundle([(of(ahead, "midt"), of(ahead, "cot_low"))], width, parts)

    def bundle_ffn_in():
        return Bundle([(of(ahead, "n3t"), of(ahead, "hid"))], width, parts)

    def bundle_cross():
        jobs = [
            (of(ahead, "z2t"), of(ahead, "branch")),
            (of(ahead, "memt"), of(behind, "dkv")),
            (of(starts, "n2t"), of(behind, "dq")),
            (of(starts, "z1t"), of(behind, "branch2")),
        ]
        return Bundle(jobs, width, parts)

    def bundle_self():
        grads = of(ahead, "vg") + of(behind, "vg") + of(ends, "vg")
        return Bundle([(of(starts, "n1t"), of(ends, "dqkv"))], width, parts, grads)

    def scatter_memory():
        return chain.run(scatter_items, returned, inverse)[0]

    if paired:
        core, y = group % 2, group // 2
        x, z = seq_index % 2, seq_index // 2
        send_core = jnp.stack([(1 - y) * 2 + 1 - core, y * 2 + 1 - core])
        keep_core = jnp.stack([(1 - y) * 2 + core, y * 2 + core])
        side = x.reshape(1)
        inner = ((z == 1) | (z == 2)).astype(jnp.int32).reshape(1)

        def core_step(bundle):
            sent = chain.run(bundle.compute, send_core, None)["out0"]
            return lax.ppermute(sent, "grp", CORE_PAIRS)

        def y_step(bundle, got):
            sent, kept = chain.run(bundle.compute, keep_core, got).values()
            return kept, lax.ppermute(sent, "grp", Y_PAIRS)

        def x_step(state):
            sent, kept = chain.run(split_add, *state, side)
            return kept, lax.ppermute(sent, "seq", X_PAIRS)

        def z_step(state, pairs):
            kept = chain.run(add, *state)[0]
            return kept, lax.ppermute(kept, "seq", pairs)

        def back_step(state):
            kept = chain.run(pick, *state, inner)[0]
            return kept, lax.ppermute(kept, "seq", X_PAIRS)

        def finish(bundle, state):
            return chain.run(bundle.finish, *state, side)

        forward(0)
        backward(0)
        forward(1)
        b1, b2 = bundle_ffn_out(), bundle_ffn_in()
        s1 = core_step(b1)
        s2 = core_step(b2)
        s1 = y_step(b1, s1)
        backward(1)
        b3 = bundle_cross()
        s3 = core_step(b3)
        s1 = x_step(s1)
        s2 = y_step(b2, s2)
        self_backward(0)
        self_backward(1)
        b4 = bundle_self()
        s1 = z_step(s1, Z_IN)
        s4 = core_step(b4)
        s2 = x_step(s2)
        s3 = y_step(b3, s3)
        s1 = z_step(s1, Z_MID)
        s2 = z_step(s2, Z_IN)
        s1 = z_step(s1, Z_OUT)
        s3 = x_step(s3)
        s4 = y_step(b4, s4)
        s2 = z_step(s2, Z_MID)
        s1 = back_step(s1)
        s2 = z_step(s2, Z_OUT)
        s3 = z_step(s3, Z_IN)
        s4 = x_step(s4)
        s1 = finish(b1, s1)
        s2 = back_step(s2)
        s3 = z_step(s3, Z_MID)
        s4 = z_step(s4, Z_IN)
        grad_memory = scatter_memory()
        s2 = finish(b2, s2)
        s3 = z_step(s3, Z_OUT)
        s4 = z_step(s4, Z_MID)
        s3 = back_step(s3)
        s4 = z_step(s4, Z_OUT)
        s4 = back_step(s4)
        s3 = finish(b3, s3)
        s4 = finish(b4, s4)
    else:
        for item in range(items):
            forward(item)
            backward(item)
            self_backward(item)
        every = jnp.arange(parts, dtype=jnp.int32)
        none = jnp.zeros((1,), jnp.int32)
        done = []
        for bundle in (bundle_ffn_out(), bundle_ffn_in(), bundle_cross(), bundle_self()):
            sums = chain.run(bundle.compute, every, None)["out0"]
            share = lax.psum_scatter(sums, "grp", scatter_dimension=0, tiled=True)[0]
            share = lax.psum(share, "seq")
            done.append(chain.run(bundle.finish, share, None, none))
        s1, s2, s3, s4 = done
        grad_memory = scatter_memory()

    out = jnp.stack(of(ahead, "out"))
    gx = jnp.stack(of(ends, "gx"))
    g_ffn_out, g_ffn_in = s1[0], s2[0]
    g_cross_out, g_cross_kv, g_cross_q, g_self_out = s3
    g_self_qkv = s4[0]
    (
        g_self_norm_gain, g_self_norm_shift, g_self_q_bias, g_self_v_bias, g_self_mix_gain,
        g_self_mix_shift, g_self_out_bias, g_cross_norm_gain, g_cross_norm_shift, g_cross_q_bias,
        g_cross_v_bias, g_cross_mix_gain, g_cross_mix_shift, g_cross_out_bias, g_ffn_norm_gain,
        g_ffn_norm_shift, g_ffn_out_bias, g_ffn_in_bias, g_ffn_mid_gain, g_ffn_mid_shift,
        g_self_head, g_cross_head, g_table,
    ) = chain.run(
        vector_outputs, s4[1], group.reshape(1), parts, ff, rel_bias_table.shape[0]
    )
    return (
        out,
        gx,
        grad_memory,
        g_self_norm_gain,
        g_self_norm_shift,
        g_self_qkv,
        g_self_q_bias,
        g_self_v_bias,
        g_table,
        g_self_head,
        g_self_mix_gain,
        g_self_mix_shift,
        g_self_out,
        g_self_out_bias,
        g_cross_norm_gain,
        g_cross_norm_shift,
        g_cross_q,
        g_cross_q_bias,
        g_cross_kv,
        g_cross_v_bias,
        g_cross_head,
        g_cross_mix_gain,
        g_cross_mix_shift,
        g_cross_out,
        g_cross_out_bias,
        g_ffn_norm_gain,
        g_ffn_norm_shift,
        g_ffn_in,
        g_ffn_in_bias,
        g_ffn_mid_gain,
        g_ffn_mid_shift,
        g_ffn_out,
        g_ffn_out_bias,
    )


def solution(mesh):
    rows = P(("seq", "grp"), None, None)
    matrix, vector = P("grp", None), P("grp")
    in_specs = (rows, P("grp", "seq", None), rows, P(("seq", "grp")), P(("seq", "grp"))) + (P(),) * 32
    out_specs = (
        rows, rows, P("grp", "seq", None),
        vector, vector, matrix, vector, vector, matrix, vector, vector, vector, matrix, vector,
        vector, vector, matrix, vector, matrix, vector, vector, vector, vector, matrix, vector,
        vector, vector, matrix, vector, vector, vector, matrix, vector,
    )
    return jax.shard_map(local, mesh=mesh, in_specs=in_specs, out_specs=out_specs, check_vma=False)
```

```python
import functools
import math

import jax
import jax.numpy as jnp
from jax import lax
from jax.experimental import pallas as pl
from jax.experimental.pallas import tpu as pltpu
from jax.sharding import PartitionSpec as P

H = 12
HD = 64
EPSILON = 1e-05
FACTOR = 1.0 / math.sqrt(HD)
MASKED = -1000000000.0
F32 = jnp.float32
BF16 = jnp.bfloat16
PAIR = 2 * HD
PAIRS = H // 2

(
    SELF_GAIN,
    SELF_SHIFT,
    SELF_QB,
    SELF_VB,
    SELF_HEAD,
    SELF_MIX_GAIN,
    SELF_MIX_SHIFT,
    SELF_OB,
    CROSS_GAIN,
    CROSS_SHIFT,
    CROSS_QB,
    CROSS_VB,
    CROSS_HEAD,
    CROSS_MIX_GAIN,
    CROSS_MIX_SHIFT,
    CROSS_OB,
    FFN_GAIN,
    FFN_SHIFT,
    FFN_OB,
) = range(19)
IN_BIAS, MID_GAIN, MID_SHIFT, TABLE = 20, 24, 28, 32
VEC_ROWS = 64


def dot(left, right):
    return jnp.dot(left, right, preferred_element_type=F32)


def dot_rows(left, right):
    return lax.dot_general(left, right, (((1,), (1,)), ((), ())), preferred_element_type=F32)


def dot_cols(left, right):
    return lax.dot_general(left, right, (((0,), (0,)), ((), ())), preferred_element_type=F32)


def normalize(values):
    average = jnp.mean(values, axis=-1, keepdims=True)
    centered = values - average
    spread = jnp.mean(centered * centered, axis=-1, keepdims=True)
    scale = lax.rsqrt(spread + EPSILON)
    return centered * scale, scale


def normalize_back(grad, normed, scale):
    mean_grad = jnp.mean(grad, axis=-1, keepdims=True)
    mean_both = jnp.mean(grad * normed, axis=-1, keepdims=True)
    return scale * (grad - mean_grad - normed * mean_both)


def total(values):
    return jnp.sum(values.astype(F32), axis=0, keepdims=True)


def lanes(start, size):
    return pl.ds(pl.multiple_of(start, 128), size)


def pick_head(values, half, axis):
    place = lax.broadcasted_iota(jnp.int32, values.shape, axis)
    inside = (place < HD) if half == 0 else (place >= HD)
    return jnp.where(inside, values, jnp.zeros_like(values))


def attend_pair(queries, keys, values, score_fn, e_ref, inv_ref, first):
    values_t = values.T
    ones = jnp.ones((16, values.shape[0]), BF16)
    scores = [score_fn(dot_rows(keys, pick_head(queries, half, 1)), first + half) for half in range(2)]
    parts = []
    for half in range(2):
        peak = jnp.max(scores[half], axis=0, keepdims=True)
        low = jnp.exp(scores[half] - peak).astype(BF16)
        e_ref[first + half] = low
        mixed = dot(jnp.concatenate([values_t[half * HD : (half + 1) * HD], ones], axis=0), low)
        inverse = 1.0 / mixed[HD : HD + 1]
        inv_ref[pl.ds(first + half, 1), :] = inverse
        parts.append(mixed[:HD] * inverse)
    return jnp.concatenate(parts, axis=0).T


def attend_pair_back(queries, keys, values, grad, prod, e_ref, inv_ref, first, keep_scores):
    keys_t = keys.T
    grad_t = grad.astype(F32).T
    prod_t = prod.T
    grads, deltas, grad_probs = [], [], []
    for half in range(2):
        rows = slice(half * HD, (half + 1) * HD)
        inverse = inv_ref[pl.ds(first + half, 1), :]
        deltas.append(jnp.sum(prod_t[rows], axis=0, keepdims=True) * inverse)
        grads.append(pick_head((grad_t * inverse).astype(BF16), half, 0))
        grad_probs.append(dot(values, grads[half]))
    lows = [e_ref[first + half] for half in range(2)]
    dv = dot_rows(jnp.concatenate(lows, axis=1), jnp.concatenate(grads, axis=1))
    scores = []
    for half in range(2):
        scores.append((lows[half].astype(F32) * (grad_probs[half] - deltas[half])).astype(BF16))
        if keep_scores is not None:
            keep_scores(scores[half], first + half)
    heads = jnp.concatenate([pick_head(queries, half, 1) for half in range(2)], axis=0)
    dk = dot(jnp.concatenate(scores, axis=1), heads)
    dq = [dot(keys_t[half * HD : (half + 1) * HD], scores[half]) for half in range(2)]
    return jnp.concatenate(dq, axis=0).T * FACTOR, dk, dv


class Gradients:
    def __init__(self, order_ref, sems, width):
        self.order_ref, self.sems, self.width = order_ref, sems, width
        self.parts = order_ref.shape[0] // 2
        self.used, self.copies = 0, []

    def load(self, far, near):
        copy = pltpu.make_async_copy(far, near, self.sems.at[self.used])
        copy.start()
        self.copies.append(copy)
        self.used += 1

    def load_left(self, far, near, item):
        size, depth = far.shape[0] // self.parts, far.shape[1]
        for j in range(self.parts):
            rows = pl.ds(pl.multiple_of(self.order_ref[j] * size, 16), size)
            self.load(far.at[rows, :], near.at[pl.ds(j * size, size), pl.ds(item * depth, depth)])

    def load_right(self, far, near, item):
        depth = far.shape[0]
        self.load(far, near.at[pl.ds(item * depth, depth), :])

    def wait(self):
        for copy in self.copies:
            copy.wait()
        self.copies = []

    def place(self, quarter, size):
        return pl.ds(pl.multiple_of(self.order_ref[self.parts + quarter] * size, 16), size)

    def put_left(self, value, near, item):
        size, depth = value.shape[0] // self.parts, value.shape[1]
        for quarter in range(self.parts):
            near[self.place(quarter, size), item * depth : (item + 1) * depth] = value[
                quarter * size : (quarter + 1) * size
            ]

    def put(self, outs, quarter, place, value):
        half = self.parts // 2
        outs[quarter // half][quarter % half, place, :] = value.astype(BF16)

    def sum(self, left, right, outs, row):
        size = left.shape[0] // self.parts
        span = min(left.shape[0], self.width)
        for column in range(right.shape[1] // self.width):
            cols = slice(column * self.width, (column + 1) * self.width)
            for top in range(0, left.shape[0], span):
                value = dot(left[top : top + span, :], right[:, cols])
                for quarter in range(top // size, (top + span - 1) // size + 1):
                    low, high = max(top, quarter * size), min(top + span, (quarter + 1) * size)
                    place = slice(row + low - quarter * size, row + high - quarter * size)
                    self.put(outs, quarter, place, value[low - top : high - top])
            row += size
        return row


def item_rows(ref, item, depth):
    return ref.at[pl.ds(item * depth, depth), :]


def self_forward_kernel(item, io, len_ref, prefix_ref):
    io.load("x", "vecs", "qkv_w", "bias", "out_w", "q2_w")
    _, length, width = io.x.shape
    vec_ref = io.vecs

    def vec(row):
        return vec_ref[row : row + 1, :]

    io.need("x", "vecs")
    x = io.x[item].astype(F32)
    normed, _ = normalize(x)
    low = (normed * vec(SELF_GAIN) + vec(SELF_SHIFT)).astype(BF16)
    io.n1t[...] = low.T
    io.store("n1t")
    io.need("qkv_w")
    queries = dot(low, io.qkv_w[:, :width]) + vec(SELF_QB)
    io.qkv[:, :width] = queries.astype(BF16) * jnp.asarray(FACTOR, BF16)
    io.qkv[:, width : 2 * width] = dot(low, io.qkv_w[:, width : 2 * width]).astype(BF16)
    values = dot(low, io.qkv_w[:, 2 * width :]) + vec(SELF_VB)
    io.qkv[:, 2 * width :] = values.astype(BF16)
    io.store("qkv")
    key_pos = lax.broadcasted_iota(jnp.int32, (length, length), 0)
    query_pos = lax.broadcasted_iota(jnp.int32, (length, length), 1)
    allowed = (key_pos < len_ref[item]) & ((key_pos <= query_pos) | (key_pos < prefix_ref[item]))
    io.inv[...] = jnp.zeros_like(io.inv)
    io.need("bias")

    def scores_of(scores, head):
        return jnp.where(allowed, scores + io.bias[head].astype(F32), MASKED)

    def one_pair(pair, _):
        base = pair * PAIR
        io.mixed[:, lanes(base, PAIR)] = attend_pair(
            io.qkv[:, lanes(base, PAIR)],
            io.qkv[:, lanes(base + width, PAIR)],
            io.qkv[:, lanes(base + 2 * width, PAIR)],
            scores_of, io.e, io.inv, 2 * pair,
        )
        return 0

    lax.fori_loop(0, PAIRS, one_pair, 0, unroll=2)
    io.store("e", "inv", "mixed")
    normed, _ = normalize(io.mixed[...] * vec(SELF_HEAD))
    low = (normed * vec(SELF_MIX_GAIN) + vec(SELF_MIX_SHIFT)).astype(BF16)
    io.z1t[...] = low.T
    io.store("z1t")
    io.need("out_w")
    x2 = x + dot(low, io.out_w[...]) + vec(SELF_OB)
    io.x2[...] = x2
    io.store("x2")
    normed, _ = normalize(x2)
    low = (normed * vec(CROSS_GAIN) + vec(CROSS_SHIFT)).astype(BF16)
    io.n2t[...] = low.T
    io.need("q2_w")
    queries = dot(low, io.q2_w[...]) + vec(CROSS_QB)
    io.q2[...] = queries.astype(BF16) * jnp.asarray(FACTOR, BF16)
    io.store("n2t", "q2")


def gelu_parts(hidden):
    gate = 0.5 * (1.0 + lax.erf(hidden * math.sqrt(0.5)))
    slope = hidden * (jnp.exp(-0.5 * hidden * hidden) * (1.0 / math.sqrt(2.0 * math.pi)))
    return hidden * gate, gate + slope


def cross_forward_kernel(item, last, io, mem_len_ref, dec_len_ref, *refs):
    act_ref, grad_ref, slope_ref, mid_ref = refs[-4:]
    io.load("mem", "kv_w", "vecs")
    length, width = io.x2.shape
    mem_tokens = io.mem.shape[0]
    ff = io.in_w.shape[1]
    tiles = ff // width
    mem_ref, kv_ref, kv_w, vec_ref, wide_ref = io.mem, io.kv, io.kv_w, io.vecs, io.wides
    e_ref, inv_ref, mixed_ref, q2_ref, vg_ref = io.e, io.inv, io.mixed, io.q2, io.vg
    out_w, in_w, ffn_w = io.out_w, io.in_w, io.ffn_w
    if last:
        order_ref, left_out, right_out, left_in, right_in, sems = refs[:-4]
        grads = Gradients(order_ref, sems, width)
        hid_ref, cot_low_ref = item_rows(right_in, item, length), item_rows(right_out, item, length)
    else:
        hid_ref, cot_low_ref = io.hid, io.cot_low

    def vec(row):
        return vec_ref[row : row + 1, :]

    io.need("mem", "kv_w", "vecs")
    io.load("q2", "x2", "out_w", "in_w", "wides")
    io.load("cot", at=item)
    io.load("ffn_w")
    if last:
        for i in range(item):
            grads.load_left(io.far[f"midt{i}"], left_out, i)
            grads.load_right(io.far[f"cot_low{i}"], right_out, i)
            grads.load_left(io.far[f"n3t{i}"], left_in, i)
            grads.load_right(io.far[f"hid{i}"], right_in, i)
    io.memt[...] = mem_ref[...].T
    io.store("memt")
    kv_ref[:, :width] = dot(mem_ref[...], kv_w[:, :width]).astype(BF16)
    kv_ref[:, width:] = (dot(mem_ref[...], kv_w[:, width:]) + vec(CROSS_VB)).astype(BF16)
    io.store("kv")
    io.need("q2")
    mem_len = mem_len_ref[item]
    inv_ref[...] = jnp.zeros_like(inv_ref)

    def scores_of(scores, head):
        del head
        key_pos = lax.broadcasted_iota(jnp.int32, (mem_tokens, length), 0)
        return jnp.where(key_pos < mem_len, scores, MASKED)

    def one_pair(pair, _):
        base = pair * PAIR
        mixed_ref[:, lanes(base, PAIR)] = attend_pair(
            q2_ref[:, lanes(base, PAIR)],
            kv_ref[:, lanes(base, PAIR)],
            kv_ref[:, lanes(base + width, PAIR)],
            scores_of, e_ref, inv_ref, 2 * pair,
        )
        return 0

    lax.fori_loop(0, PAIRS, one_pair, 0, unroll=2)
    io.store("e", "inv", "mixed")
    normed, _ = normalize(mixed_ref[...] * vec(CROSS_HEAD))
    low = (normed * vec(CROSS_MIX_GAIN) + vec(CROSS_MIX_SHIFT)).astype(BF16)
    io.z2t[...] = low.T
    io.store("z2t")
    io.need("x2", "out_w")
    x3 = io.x2[...] + dot(low, out_w[...]) + vec(CROSS_OB)
    norm3, scale3 = normalize(x3)
    n3 = (norm3 * vec(FFN_GAIN) + vec(FFN_SHIFT)).astype(BF16)
    if last:
        grads.put_left(n3.T, left_in, item)
    else:
        io.n3t[...] = n3.T
        io.store("n3t")
    io.need("in_w", "wides")

    def hidden_tile(tile, sums):
        cols = lanes(tile * width, width)
        hidden = dot(n3, in_w[:, cols]) + wide_ref[0:1, cols]
        act, slope = gelu_parts(hidden)
        act_ref[:, cols] = act
        slope_ref[:, cols] = slope.astype(BF16)
        return sums + jnp.sum(act, axis=-1, keepdims=True)

    sums = lax.fori_loop(0, tiles, hidden_tile, jnp.zeros((length, 1), F32))
    average = sums / ff

    def spread_tile(tile, sums):
        centered = act_ref[:, lanes(tile * width, width)] - average
        return sums + jnp.sum(centered * centered, axis=-1, keepdims=True)

    sums = lax.fori_loop(0, tiles, spread_tile, jnp.zeros((length, 1), F32))
    scale = lax.rsqrt(sums / ff + EPSILON)

    def middle_tile(tile, _):
        cols = lanes(tile * width, width)
        normed = (act_ref[:, cols] - average) * scale
        act_ref[:, cols] = normed
        low = (normed * wide_ref[1:2, cols] + wide_ref[2:3, cols]).astype(BF16)
        mid_ref[:, cols] = low
        if last:
            left_out[grads.place(tile, width), item * length : (item + 1) * length] = low.T
        else:
            io.midt[pl.ds(pl.multiple_of(tile * width, 128), width), :] = low.T
        return 0

    lax.fori_loop(0, tiles, middle_tile, 0)
    if not last:
        io.store("midt")
    io.need("ffn_w", "cot")
    result = x3 + dot(mid_ref[...], ffn_w[...]) + vec(FFN_OB)
    io.out[...] = result.astype(BF16)
    io.store("out", at=item)

    valid = lax.broadcasted_iota(jnp.int32, (length, 1), 0) < dec_len_ref[item]
    cot = jnp.where(valid, io.cot[...].astype(F32), 0.0)
    cot_low_ref[...] = cot.astype(BF16)
    if not last:
        io.store("cot_low")
    vg_ref[...] = jnp.zeros_like(vg_ref)

    def grad_mid_tile(tile, sums):
        cols = lanes(tile * width, width)
        grad_mid = dot_rows(cot_low_ref[...], ffn_w[cols, :])
        normed = act_ref[:, cols]
        vg_ref[pl.ds(MID_GAIN + tile, 1), :] = total(grad_mid * normed)
        vg_ref[pl.ds(MID_SHIFT + tile, 1), :] = total(grad_mid)
        grad = grad_mid * wide_ref[1:2, cols]
        grad_ref[:, cols] = grad.astype(BF16)
        return (
            sums[0] + jnp.sum(grad, axis=-1, keepdims=True),
            sums[1] + jnp.sum(grad * normed, axis=-1, keepdims=True),
        )

    zero = jnp.zeros((length, 1), F32)
    sum_grad, sum_both = lax.fori_loop(0, tiles, grad_mid_tile, (zero, zero))
    mean_grad, mean_both = sum_grad / ff, sum_both / ff

    def hidden_back_tile(tile, _):
        cols = lanes(tile * width, width)
        grad = scale * (grad_ref[:, cols].astype(F32) - mean_grad - act_ref[:, cols] * mean_both)
        low = (grad * slope_ref[:, cols].astype(F32)).astype(BF16)
        hid_ref[:, cols] = low
        vg_ref[pl.ds(IN_BIAS + tile, 1), :] = total(low)
        return 0

    lax.fori_loop(0, tiles, hidden_back_tile, 0)
    if not last:
        io.store("hid")
    grad_n3 = dot_rows(hid_ref[...], in_w[...])
    vg_ref[FFN_GAIN : FFN_GAIN + 1, :] = total(grad_n3 * norm3)
    vg_ref[FFN_SHIFT : FFN_SHIFT + 1, :] = total(grad_n3)
    vg_ref[FFN_OB : FFN_OB + 1, :] = total(cot_low_ref[...])
    gx3 = normalize_back(grad_n3 * vec(FFN_GAIN), norm3, scale3) + cot
    io.gx3[...] = gx3
    io.branch[...] = gx3.astype(BF16)
    io.store("gx3", "branch")
    vg_ref[CROSS_OB : CROSS_OB + 1, :] = total(io.branch[...])
    io.store("vg")
    if last:
        grads.wait()
        grads.sum(left_out, right_out, (io.sentA, io.keptA), 0)
        grads.sum(left_in, right_in, (io.sentC, io.keptC), 0)


def cross_back_kernel(item, last, io, *refs):
    grad_ref, prod_ref = refs[-2:]
    length, width = io.x2.shape
    mem_tokens = io.kv.shape[0]
    vec_ref, vg_ref = io.vecs, io.vg
    if last:
        order_ref, left_mem, right_mem, left_z, right_z, left_n, right_n, left_s, right_s, sems = refs[:-2]
        grads = Gradients(order_ref, sems, width)
        dkv_ref, dq_ref = item_rows(right_mem, item, mem_tokens), item_rows(right_n, item, length)
    else:
        dkv_ref, dq_ref = io.dkv, io.dq
    io.load("vecs", "mixed", "branch", "out_w", "q2", "inv", "kv", "e", "x2", "kv_w", "q2_w", "gx3")
    if last:
        for i in range(item + 1):
            grads.load_left(io.far[f"memt{i}"], left_mem, i)
            grads.load_left(io.far[f"z2t{i}"], left_z, i)
            grads.load_left(io.far[f"n2t{i}"], left_n, i)
            grads.load_left(io.far[f"z1t{i}"], left_s, i)
            grads.load_right(io.far[f"branch{i}"], right_z, i)
            if i < item:
                grads.load_right(io.far[f"dkv{i}"], right_mem, i)
                grads.load_right(io.far[f"dq{i}"], right_n, i)
                grads.load_right(io.far[f"branch2{i}"], right_s, i)

    def vec(row):
        return vec_ref[row : row + 1, :]

    def put(row, value):
        vg_ref[row : row + 1, :] = value

    vg_ref[...] = jnp.zeros_like(vg_ref)
    io.need("vecs", "mixed")
    mixed = io.mixed[...]
    normed, scale = normalize(mixed * vec(CROSS_HEAD))
    io.need("branch", "out_w")
    grad = dot_rows(io.branch[...], io.out_w[...])
    put(CROSS_MIX_GAIN, total(grad * normed))
    put(CROSS_MIX_SHIFT, total(grad))
    grad = normalize_back(grad * vec(CROSS_MIX_GAIN), normed, scale)
    put(CROSS_HEAD, total(grad * mixed))
    grad = (grad * vec(CROSS_HEAD)).astype(BF16)
    grad_ref[...] = grad
    prod_ref[...] = grad.astype(F32) * mixed
    io.need("q2", "inv", "kv", "e")

    def one_pair(pair, _):
        base = pair * PAIR
        cols = lanes(base, PAIR)
        dq, dk, dv = attend_pair_back(
            io.q2[:, cols], io.kv[:, cols], io.kv[:, lanes(base + width, PAIR)],
            grad_ref[:, cols], prod_ref[:, cols], io.e, io.inv, 2 * pair, None,
        )
        dq_ref[:, cols] = dq.astype(BF16)
        dkv_ref[:, cols] = dk.astype(BF16)
        dkv_ref[:, lanes(base + width, PAIR)] = dv.astype(BF16)
        return 0

    lax.fori_loop(0, PAIRS, one_pair, 0, unroll=2)
    if not last:
        io.store("dkv", "dq")
    put(CROSS_VB, total(dkv_ref[:, width:]))
    step = 256
    io.need("kv_w")

    def memory_tile(tile, _):
        cols = lanes(tile * step, step)
        io.gmem[:, cols] = dot_rows(dkv_ref[...], io.kv_w[cols, :]).astype(BF16)
        return 0

    lax.fori_loop(0, width // step, memory_tile, 0)
    io.store("gmem")
    put(CROSS_QB, total(dq_ref[...]))
    io.need("x2", "q2_w", "gx3")
    normed, scale = normalize(io.x2[...])
    grad = dot_rows(dq_ref[...], io.q2_w[...])
    put(CROSS_GAIN, total(grad * normed))
    put(CROSS_SHIFT, total(grad))
    gx2 = normalize_back(grad * vec(CROSS_GAIN), normed, scale) + io.gx3[...]
    io.gx2[...] = gx2
    io.branch2[...] = gx2.astype(BF16)
    io.store("gx2", "branch2")
    put(SELF_OB, total(io.branch2[...]))
    io.store("vg")
    if last:
        right_s[item * length : (item + 1) * length, :] = io.branch2[...]
        grads.wait()
        grads.sum(left_mem, right_mem, (io.sentD, io.keptD), 0)
        row = 0
        for left, right in ((left_z, right_z), (left_n, right_n), (left_s, right_s)):
            row = grads.sum(left, right, (io.sentG, io.keptG), row)


def self_back_kernel(items, io, order_ref, left, right, vg_refs, sems, grad_ref, prod_ref, diag_ref):
    _, length, width = io.x.shape
    shared = ("mixed", "branch", "qkv", "inv", "e")
    io.load("vecs", "mixed0", "branch0", "out_w", "qkv0", "inv0", "e0", "x", "qkv_w", "gx20", "buckets")
    for item in range(1, items):
        io.load(*[f"{name}{item}" for name in shared + ("gx2",)])
    grads = Gradients(order_ref, sems, width)
    for item in range(items):
        grads.load_left(io.far[f"n1t{item}"], left, item)
        for i, name in enumerate(("vgf", "vgb")):
            grads.load(io.far[f"{name}{item}"], vg_refs.at[2 * item + i])
    own = 2 * items
    for item in range(items):
        self_back_item(item, io, item_rows(right, item, length), vg_refs.at[own + item], grad_ref, prod_ref, diag_ref)
    grads.wait()
    outs = (io.sentE, io.keptE)
    row = grads.sum(left, right, outs, 0)
    value = vg_refs[0]
    for i in range(1, 3 * items):
        value = value + vg_refs[i]
    for quarter in range(grads.parts):
        grads.put(outs, quarter, slice(row, row + VEC_ROWS), value)


def self_back_item(item, io, dqkv_ref, vg_ref, grad_ref, prod_ref, diag_ref):
    _, length, width = io.x.shape
    vec_ref = io.vecs
    near = {name: io.near[f"{name}{item}"] for name in ("mixed", "branch", "qkv", "inv", "e", "gx2")}
    qkv_ref = near["qkv"]

    def vec(row):
        return vec_ref[row : row + 1, :]

    def put(row, value):
        vg_ref[row : row + 1, :] = value

    vg_ref[...] = jnp.zeros_like(vg_ref)
    diag_ref[...] = jnp.zeros_like(diag_ref)
    if item == 0:
        io.need("vecs")
    io.need(f"mixed{item}")
    mixed = near["mixed"][...]
    normed, scale = normalize(mixed * vec(SELF_HEAD))
    io.need(f"branch{item}")
    if item == 0:
        io.need("out_w")
    grad = dot_rows(near["branch"][...], io.out_w[...])
    put(SELF_MIX_GAIN, total(grad * normed))
    put(SELF_MIX_SHIFT, total(grad))
    grad = normalize_back(grad * vec(SELF_MIX_GAIN), normed, scale)
    put(SELF_HEAD, total(grad * mixed))
    grad = (grad * vec(SELF_HEAD)).astype(BF16)
    grad_ref[...] = grad
    prod_ref[...] = grad.astype(F32) * mixed
    io.need(f"qkv{item}", f"inv{item}", f"e{item}")
    backwards = (
        lax.broadcasted_iota(jnp.int32, (length, length), 0)
        + lax.broadcasted_iota(jnp.int32, (length, length), 1)
        == length - 1
    ).astype(F32).astype(BF16)

    def keep_scores(scores, head):
        flipped = dot(backwards, scores)
        padded = jnp.concatenate([flipped, jnp.zeros_like(flipped)], axis=1)
        rolled = pltpu.roll(padded, 0, 1, stride=1, stride_axis=0)
        diag_ref[pl.ds(head, 1), :] = jnp.sum(rolled, axis=0, keepdims=True)

    def one_pair(pair, _):
        base = pair * PAIR
        cols = lanes(base, PAIR)
        dq, dk, dv = attend_pair_back(
            qkv_ref[:, cols], qkv_ref[:, lanes(base + width, PAIR)],
            qkv_ref[:, lanes(base + 2 * width, PAIR)],
            grad_ref[:, cols], prod_ref[:, cols], near["e"], near["inv"], 2 * pair, keep_scores,
        )
        dqkv_ref[:, cols] = dq.astype(BF16)
        dqkv_ref[:, lanes(base + width, PAIR)] = dk.astype(BF16)
        dqkv_ref[:, lanes(base + 2 * width, PAIR)] = dv.astype(BF16)
        return 0

    lax.fori_loop(0, PAIRS, one_pair, 0, unroll=2)
    if item == 0:
        io.need("buckets", "x", "qkv_w")
    table = jnp.dot(
        diag_ref[...], io.buckets[...], precision=lax.Precision.HIGHEST, preferred_element_type=F32
    )
    vg_ref[TABLE : TABLE + 16, : table.shape[1]] = table
    put(SELF_QB, total(dqkv_ref[:, :width]))
    put(SELF_VB, total(dqkv_ref[:, 2 * width :]))
    normed, scale = normalize(io.x[item].astype(F32))
    grad = dot_rows(dqkv_ref[...], io.qkv_w[...])
    put(SELF_GAIN, total(grad * normed))
    put(SELF_SHIFT, total(grad))
    io.need(f"gx2{item}")
    gx = normalize_back(grad * vec(SELF_GAIN), normed, scale) + near["gx2"][...]
    io.gx[item] = gx.astype(BF16)
    if item == io.gx.shape[0] - 1:
        io.store("gx")


SMEM = pl.BlockSpec(memory_space=pltpu.SMEM)
VMEM = pl.BlockSpec(memory_space=pltpu.VMEM)
ANY = pl.BlockSpec(memory_space=pl.ANY)
HBM = pl.BlockSpec(memory_space=pltpu.HBM)
MIB = 1024 * 1024


COST = dict(
    self_forward=11, cross_forward=28, cross_back=18, self_back=10, weight_grads=5, finish=2, split_add=1, core_add=1,
    gather_items=3, scatter_items=4, add=1, pick=1, vectors=1,
)
COST_SCALE = 3_000_000


class Kept:
    def __init__(self, shape, dtype):
        self.shape, self.dtype = tuple(shape), dtype


class Stored(Kept):
    pass


class Token:
    def __init__(self, array, near):
        self.space = pltpu.VMEM if near else pltpu.HBM
        self.spec = VMEM if near else HBM
        self.array = array

    def operand(self):
        return pltpu.with_memory_space_constraint(self.array, self.space)


def token_args(after):
    return [t.spec for t in after], [t.operand() for t in after]


def call(kernel, name, ins, outs, scratch=(), after=(), limit=16, scalars=(), far=()):
    after_specs, after_args = token_args(after)
    first = len(scalars) + len(far) + len(ins)
    last = first + len(after)

    def body(*refs):
        kernel(*refs[:first], *refs[last:])

    ins = [pltpu.with_memory_space_constraint(a, pltpu.VMEM) for a in ins]
    far = [pltpu.with_memory_space_constraint(a, pltpu.HBM) for a in far]
    shapes = [(pltpu.HBM if isinstance(o, Stored) else pltpu.VMEM)(o.shape, o.dtype) for o in outs]
    Chain.token = 0, not isinstance(outs[0], Stored)
    return pl.pallas_call(
        body,
        out_shape=shapes,
        in_specs=[SMEM] * len(scalars) + [HBM] * len(far) + [VMEM] * len(ins) + after_specs,
        out_specs=[VMEM] * len(shapes),
        scratch_shapes=list(scratch),
        compiler_params=pltpu.CompilerParams(vmem_limit_bytes=limit * MIB),
        cost_estimate=cost_of(name),
        name=name,
    )(*scalars, *far, *ins, *after_args)


class Stream:
    def __init__(self, ins, outs, far, near, sems):
        self.names = list(ins) + list(outs)
        self.far, self.near = dict(zip(self.names, far)), dict(zip(self.names, near))
        self.sems = dict(zip(self.names, range(len(self.names))))
        self.sem_refs = sems
        self.loading, self.storing = {}, []

    def __getattr__(self, name):
        return self.near[name]

    def load(self, *names, at=None):
        for name in names:
            far = self.far[name] if at is None else self.far[name].at[at]
            copy = pltpu.make_async_copy(far, self.near[name], self.sem_refs.at[self.sems[name]])
            copy.start()
            self.loading[name] = copy

    def need(self, *names):
        for name in names:
            self.loading.pop(name).wait()

    def store(self, *names, at=None):
        for name in names:
            far = self.far[name] if at is None else self.far[name].at[at]
            copy = pltpu.make_async_copy(self.near[name], far, self.sem_refs.at[self.sems[name]])
            copy.start()
            self.storing.append(copy)

    def drain(self):
        assert not self.loading
        for copy in self.storing:
            copy.wait()


def stream_call(kernel, name, ins, outs, scratch=(), after=(), scalars=(), limit=16, kept=(), free=(), token="vg", gathered={}, far=None, parted=()):
    far = far or {}
    after_specs, after_args = token_args(after)
    n_in, n_out = len(ins), len(outs)
    far_outs = [n for n in outs if n not in kept]

    def body(*refs):
        refs = list(refs)

        def take(count):
            taken, refs[:] = refs[:count], refs[count:]
            return taken

        scalar_refs, far_in = take(len(scalars)), take(n_in)
        far_only = dict(zip(far, take(len(far))))
        take(len(after) + len(filled))
        out_refs = dict(zip(outs, take(n_out)))
        near_in = take(n_in)
        near_out = dict(zip(far_outs, take(len(far_outs))))
        sems = refs.pop()
        near_out.update({n: out_refs[n] for n in kept})
        io = Stream(
            ins, outs, far_in + [out_refs[n] for n in outs], near_in + [near_out[n] for n in outs], sems
        )
        io.far.update(far_only)
        kernel(io, *scalar_refs, *refs)
        io.drain()

    filled = {n: array for n, (_, array) in gathered.items() if array is not None}
    before = len(scalars) + n_in + len(far) + len(after)
    aliases = {before + i: list(outs).index(n) for i, n in enumerate(filled)}
    shapes = [
        pltpu.VMEM(s, d) if n in kept else pltpu.HBM((gathered[n][0],) + s if n in gathered else s, d)
        for n, (s, d) in outs.items()
    ]
    buffers = [pltpu.VMEM(a.shape[1:] if n in parted else a.shape, a.dtype) for n, a in ins.items()]
    buffers += [pltpu.VMEM(*outs[n]) for n in far_outs]
    results = pl.pallas_call(
        body,
        out_shape=shapes,
        in_specs=[SMEM] * len(scalars)
        + [ANY if n in free else HBM for n in ins]
        + [HBM] * len(far)
        + after_specs
        + [HBM] * len(filled),
        input_output_aliases=aliases,
        out_specs=[VMEM if n in kept else HBM for n in outs],
        scratch_shapes=buffers + list(scratch) + [pltpu.SemaphoreType.DMA((n_in + n_out,))],
        compiler_params=pltpu.CompilerParams(vmem_limit_bytes=limit * MIB),
        cost_estimate=cost_of(name),
        name=name,
    )(
        *scalars,
        *[a if n in free else pltpu.with_memory_space_constraint(a, pltpu.HBM) for n, a in ins.items()],
        *[pltpu.with_memory_space_constraint(a, pltpu.HBM) for a in far.values()],
        *after_args,
        *filled.values(),
    )
    Chain.token = list(outs).index(token), token in kept
    return Result(zip(outs, results))


class Result(dict):
    def __getattr__(self, name):
        return self[name]


def self_forward(item, dec_len, prefix, x, bias, qkv_w, out_w, q2_w, vecs, after):
    _, length, width = x.shape
    outs = {
        "n1t": ((width, length), BF16),
        "qkv": ((length, 3 * width), BF16),
        "e": ((H, length, length), BF16),
        "inv": ((16, length), F32),
        "mixed": ((length, width), F32),
        "z1t": ((width, length), BF16),
        "x2": ((length, width), F32),
        "n2t": ((width, length), BF16),
        "q2": ((length, width), BF16),
    }
    ins = dict(x=x, bias=bias, qkv_w=qkv_w, out_w=out_w, q2_w=q2_w, vecs=vecs)
    return stream_call(
        functools.partial(self_forward_kernel, item), "self_forward", ins, outs, after=after,
        scalars=(dec_len, prefix), limit=40, token="inv",
    )


def sums_of(names, rows, parts, width):
    outs = {}
    for name, count in zip(names, rows):
        outs.update({f"{side}{name}": ((parts // 2, count, width), BF16) for side in ("sent", "kept")})
    return outs


def operand_pair(rows, depth, columns):
    return [pltpu.VMEM((rows, depth), BF16), pltpu.VMEM((depth, columns), BF16)]


def cross_forward(item, earlier, order, mem_len, dec_len, x2, q2, mem, cot, kv_w, out_w, in_w, ffn_w, vecs, wides, after):
    length, width = x2.shape
    items = cot.shape[0]
    last = item == items - 1
    mem_tokens = mem.shape[0]
    ff = in_w.shape[1]
    parts = order.shape[0] // 2
    outs = {
        "out": ((length, width), BF16),
        "kv": ((mem_tokens, 2 * width), BF16),
        "e": ((H, mem_tokens, length), BF16),
        "inv": ((16, length), F32),
        "mixed": ((length, width), F32),
        "memt": ((width, mem_tokens), BF16),
        "z2t": ((width, length), BF16),
        "gx3": ((length, width), F32),
        "branch": ((length, width), BF16),
        "vg": ((VEC_ROWS, width), F32),
    }
    operands = {
        "n3t": ((width, length), BF16),
        "hid": ((length, ff), BF16),
        "midt": ((ff, length), BF16),
        "cot_low": ((length, width), BF16),
    }
    ins = dict(
        x2=x2, q2=q2, mem=mem, cot=cot, kv_w=kv_w, out_w=out_w, in_w=in_w, ffn_w=ffn_w, vecs=vecs, wides=wides
    )
    scratch = [pltpu.VMEM((length, ff), F32)] + [pltpu.VMEM((length, ff), BF16)] * 3
    scalars, far, sums = (mem_len, dec_len), {}, {}
    if last:
        sums = sums_of("AC", (ff // parts, ff // parts), parts, width)
        outs.update(sums)
        scalars += (order,)
        far = {f"{n}{i}": earlier[i][n] for i in range(item) for n in operands}
        scratch = (
            operand_pair(ff, items * length, width)
            + operand_pair(width, items * length, ff)
            + [pltpu.SemaphoreType.DMA((item * (2 * parts + 2),))]
            + scratch
        )
    else:
        outs.update(operands)
    return stream_call(
        functools.partial(cross_forward_kernel, item, last), "cross_forward", ins, outs,
        scratch=scratch, after=after, scalars=scalars, limit=53 if last else 50, free=("mem",),
        gathered=dict(out=(items, earlier[item - 1].out if item else None)), far=far, kept=tuple(sums), parted=("cot",),
    )


def cross_back(item, items, earlier, starts, ahead, order, kv_w, out_w, q2_w, vecs, after):
    a, x2, q2 = ahead[item], starts[item].x2, starts[item].q2
    last = item == items - 1
    length, width = x2.shape
    mem_tokens = a.kv.shape[0]
    parts = order.shape[0] // 2
    outs = {
        "gmem": ((mem_tokens, width), BF16),
        "gx2": ((length, width), F32),
        "branch2": ((length, width), BF16),
        "vg": ((VEC_ROWS, width), F32),
    }
    operands = {"dq": ((length, width), BF16), "dkv": ((mem_tokens, 2 * width), BF16)}
    ins = dict(
        branch=a.branch, gx3=a.gx3, mixed=a.mixed, kv=a.kv, e=a.e, inv=a.inv, q2=q2, x2=x2,
        kv_w=kv_w, out_w=out_w, q2_w=q2_w, vecs=vecs,
    )
    scratch = [pltpu.VMEM((length, width), BF16), pltpu.VMEM((length, width), F32)]
    scalars, far, sums = (), {}, {}
    if last:
        quarter = width // parts
        sums = sums_of("DG", (2 * quarter, 3 * quarter), parts, width)
        outs.update(sums)
        scalars = (order,)
        for i in range(items):
            far.update({f"memt{i}": ahead[i].memt, f"z2t{i}": ahead[i].z2t, f"branch{i}": ahead[i].branch})
            far.update({f"n2t{i}": starts[i].n2t, f"z1t{i}": starts[i].z1t})
            if i < item:
                b = earlier[i]
                far.update({f"dkv{i}": b.dkv, f"dq{i}": b.dq, f"branch2{i}": b.branch2})
        scratch = (
            operand_pair(width, items * mem_tokens, 2 * width)
            + operand_pair(width, items * length, width) * 3
            + [pltpu.SemaphoreType.DMA((items * (4 * parts + 1) + item * 3,))]
            + scratch
        )
    else:
        outs.update(operands)
    return stream_call(
        functools.partial(cross_back_kernel, item, last), "cross_back", ins, outs, scratch=scratch, after=after,
        scalars=scalars, limit=46 if last else 34, far=far, kept=tuple(sums),
    )


def self_back(starts, ahead, behind, order, x, qkv_w, out_w, vecs, buckets, after):
    items, length, width = x.shape
    parts = order.shape[0] // 2
    ins = dict(x=x, qkv_w=qkv_w, out_w=out_w, vecs=vecs, buckets=buckets)
    far = {}
    for item in range(items):
        a, b = starts[item], behind[item]
        ins.update({f"{name}{item}": a[name] for name in ("mixed", "qkv", "e", "inv")})
        ins.update({f"branch{item}": b.branch2, f"gx2{item}": b.gx2})
        far.update({f"n1t{item}": a.n1t, f"vgf{item}": ahead[item].vg, f"vgb{item}": b.vg})
    sums = sums_of("E", (3 * width // parts + VEC_ROWS,), parts, width)
    outs = {"gx": (x.shape, BF16), **sums}
    scratch = operand_pair(width, items * length, 3 * width) + [
        pltpu.VMEM((3 * items, VEC_ROWS, width), F32),
        pltpu.SemaphoreType.DMA((items * (parts + 2),)),
        pltpu.VMEM((length, width), BF16),
        pltpu.VMEM((length, width), F32),
        pltpu.VMEM((16, 2 * length), F32),
    ]
    return stream_call(
        functools.partial(self_back_kernel, items), "self_back", ins, outs, scratch=scratch, after=after,
        scalars=(order,), limit=40, far=far, kept=tuple(sums), token="keptE",
    )


def prepare_kernel(narrow, wide, *refs):
    ins, (vec_ref, wide_ref) = refs[: narrow + wide], refs[narrow + wide :]
    vec_ref[...] = jnp.zeros_like(vec_ref)
    wide_ref[...] = jnp.zeros_like(wide_ref)
    for row in range(narrow):
        vec_ref[row, :] = ins[row][...].astype(F32)
    for row in range(wide):
        wide_ref[row, :] = ins[narrow + row][...].astype(F32)


def prepare(vectors, wides, after):
    count = len(vectors) + len(wides)
    shapes = [
        pltpu.HBM((24, vectors[0].shape[0]), F32), pltpu.HBM((8, wides[0].shape[0]), F32)
    ]

    after_specs, after_args = token_args(after)

    def body(*refs):
        prepare_kernel(len(vectors), len(wides), *refs[:count], *refs[count + len(after) :])

    Chain.token = 0, False
    return pl.pallas_call(
        body, out_shape=shapes, in_specs=[VMEM] * count + after_specs, out_specs=[VMEM] * 2,
        name="prepare",
    )(*vectors, *wides, *after_args)


def rel_bias_of(table, length):
    count = table.shape[0]
    positions = jnp.arange(length, dtype=jnp.int32)
    offset = jnp.clip(positions[:, None] - positions[None, :], -(count // 2), count // 2 - 1)
    one_hot = (offset + count // 2)[None] == jnp.arange(count, dtype=jnp.int32)[:, None, None]
    return lax.dot_general(
        table, one_hot.astype(BF16), (((0,), (0,)), ((), ())), preferred_element_type=F32
    ).astype(BF16)


def bucket_lanes(length, count):
    offset = length - 1 - jnp.arange(2 * length, dtype=jnp.int32)
    bucket = jnp.clip(offset, -(count // 2), count // 2 - 1) + count // 2
    return (bucket[:, None] == jnp.arange(128, dtype=jnp.int32)[None, :]).astype(F32)


def gather_kernel(slots_ref, memory_ref, out_ref, sems):
    copies = [
        pltpu.make_async_copy(memory_ref.at[slots_ref[i]], out_ref.at[i], sems.at[i])
        for i in range(out_ref.shape[0])
    ]
    for copy in copies:
        copy.start()
    for copy in copies:
        copy.wait()


def gather_items(memory, slots, after):
    count = slots.shape[0]
    return call(
        gather_kernel, "gather_items", (), [Stored((count,) + memory.shape[1:], memory.dtype)],
        scratch=[pltpu.SemaphoreType.DMA((count,))], after=after, scalars=(slots,), far=(memory,), limit=8,
    )


def scatter_kernel(items, slots_ref, *refs):
    parts, out_ref, sems = refs[:items], refs[items], refs[items + 1]
    copies = []
    for p in range(parts[0].shape[0]):
        for j in range(items):
            i = p * items + j
            copies.append(pltpu.make_async_copy(parts[j].at[p], out_ref.at[slots_ref[i]], sems.at[i]))
    for copy in copies:
        copy.start()
    for copy in copies:
        copy.wait()


def scatter_items(parts, slots, after):
    count = slots.shape[0]
    return call(
        functools.partial(scatter_kernel, len(parts)), "scatter_items", (),
        [Stored((count,) + parts[0].shape[1:], parts[0].dtype)],
        scratch=[pltpu.SemaphoreType.DMA((count,))], after=after, scalars=(slots,), far=tuple(parts), limit=8,
    )


class Bundle:
    def __init__(self, shapes, width, parts, vectors=False):
        self.shapes, self.width, self.parts, self.vectors = shapes, width, parts, vectors
        self.blocks = []
        row = 0
        for index, (rows, columns) in enumerate(shapes):
            size = rows // parts
            for column in range(columns // width):
                self.blocks.append((index, column, row, size))
                row += size
        self.vector_row = row
        self.rows = row + (VEC_ROWS if vectors else 0)

    def finish_kernel(self, whole_rows, place_ref, mine_ref, got_ref, *out_refs):
        half = mine_ref.shape[0]

        def rows_of(start, size):
            pieces = []
            while size:
                side = start // half
                take = min(size, (side + 1) * half - start)
                rows = slice(start - side * half, start - side * half + take)
                if whole_rows:
                    pieces.append(mine_ref[rows, :].astype(F32))
                else:
                    own = place_ref[0] == side
                    pieces.append(jnp.where(own, mine_ref[rows, :].astype(F32), got_ref[rows, :].astype(F32)))
                start, size = start + take, size - take
            return pieces

        def store(out_ref, cols, start, size):
            done = 0
            for piece in rows_of(start, size):
                out_ref[done : done + piece.shape[0], cols] = piece
                done += piece.shape[0]

        for index, column, row, size in self.blocks:
            store(out_refs[index], slice(column * self.width, (column + 1) * self.width), row, size)
        if self.vectors:
            store(out_refs[-1], slice(None), self.vector_row, VEC_ROWS)

    def finish(self, mine, got, place, after):
        outs = [Stored((rows // self.parts, columns), F32) for rows, columns in self.shapes]
        if self.vectors:
            outs.append(Kept((VEC_ROWS, self.width), F32))
        ins = (mine, mine if got is None else got)
        return call(
            functools.partial(self.finish_kernel, got is None), "finish", ins, outs,
            after=after, scalars=(place,), limit=12,
        )


def add_low(left, right):
    return left + right


def core_add_kernel(left_ref, right_ref, sent_ref, kept_ref):
    sent_ref[...] = add_low(left_ref[0], right_ref[0])
    kept_ref[...] = add_low(left_ref[1], right_ref[1])


def core_add(left, right, after):
    shape = left.shape[1:]
    return call(core_add_kernel, "core_add", (left, right), [Kept(shape, BF16)] * 2, after=after, limit=8)


def split_add_kernel(side_ref, left_ref, right_ref, sent_ref, kept_ref):
    half = sent_ref.shape[-2]
    mine = pl.ds(pl.multiple_of(side_ref[0] * half, 16), half)
    other = pl.ds(pl.multiple_of((1 - side_ref[0]) * half, 16), half)
    if len(left_ref.shape) == 2:
        sent_ref[...] = add_low(left_ref[other, :], right_ref[other, :])
        kept_ref[...] = add_low(left_ref[mine, :], right_ref[mine, :])
    else:
        sent_ref[...] = add_low(left_ref[:, other, :], right_ref[:, other, :])
        kept_ref[...] = add_low(left_ref[:, mine, :], right_ref[:, mine, :])


def split_add(left, right, side, after):
    shape = left.shape[:-2] + (left.shape[-2] // 2, left.shape[-1])
    return call(
        split_add_kernel, "split_add", (left, right), [Kept(shape, BF16)] * 2,
        after=after, scalars=(side,), limit=8,
    )


def add_kernel(left_ref, right_ref, out_ref):
    out_ref[...] = add_low(left_ref[...], right_ref[...])


def add(left, right, after):
    return call(add_kernel, "add", (left, right), [Kept(left.shape, BF16)], after=after, limit=4)


def pick_kernel(own_ref, mine_ref, got_ref, out_ref):
    @pl.when(own_ref[0] == 1)
    def _():
        out_ref[...] = mine_ref[...]

    @pl.when(own_ref[0] != 1)
    def _():
        out_ref[...] = got_ref[...]


def pick(mine, got, own, after):
    return call(
        pick_kernel, "pick", (mine, got), [Kept(mine.shape, BF16)], after=after, scalars=(own,), limit=4
    )


def vectors_kernel(parts, group_ref, vec_ref, *refs):
    outs, scratch = refs[:-1], refs[-1]
    group = group_ref[0]
    width = vec_ref.shape[1]
    size = width // parts
    values = vec_ref[...]
    rolled = pltpu.roll(values, lax.rem(width - size * group, width), 1)
    narrow = [row for row in range(FFN_OB + 1) if row not in (SELF_HEAD, CROSS_HEAD)]
    for out, row in zip(outs, narrow):
        out[...] = rolled[row, :size]
    outs = outs[len(narrow) :]
    tiles = outs[0].shape[0] * parts // width
    for out, row in zip(outs, (IN_BIAS, MID_GAIN, MID_SHIFT)):
        if tiles == parts:
            out[...] = vec_ref[pl.ds(row + group, 1), :][0]
    heads = H // parts
    lane = lax.broadcasted_iota(jnp.int32, (width, 128), 0) // HD
    one_hot = (lane == lax.broadcasted_iota(jnp.int32, (width, 128), 1)).astype(F32)
    sums = jnp.dot(values, one_hot, precision=lax.Precision.HIGHEST, preferred_element_type=F32)
    sums = pltpu.roll(sums, lax.rem(128 - heads * group, 128), 1)
    outs[3][...] = sums[SELF_HEAD, :heads]
    outs[4][...] = sums[CROSS_HEAD, :heads]
    scratch[...] = values[TABLE : TABLE + 16, :128].T
    buckets = outs[5].shape[0]
    outs[5][...] = scratch[pl.ds(pl.multiple_of(buckets * group, buckets), buckets), :][:, :H]


def vector_outputs(vec, group, parts, ff, buckets, after):
    width = vec.shape[1]
    outs = [Stored((width // parts,), F32)] * 17 + [Stored((ff // parts,), F32)] * 3
    outs += [Stored((H // parts,), F32)] * 2 + [Stored((buckets // parts, H), F32)]
    return call(
        functools.partial(vectors_kernel, parts), "vectors", (vec,), outs,
        scratch=[pltpu.VMEM((128, 16), F32)], after=after, scalars=(group,), limit=8,
    )


CORE_PAIRS = [(0, 1), (1, 0), (2, 3), (3, 2)]
Y_PAIRS = [(0, 2), (2, 0), (1, 3), (3, 1)]
X_PAIRS = [(0, 1), (1, 0), (2, 3), (3, 2), (4, 5), (5, 4), (6, 7), (7, 6)]
Z_IN = [(0, 2), (1, 3), (6, 4), (7, 5)]
Z_MID = [(2, 4), (4, 2), (3, 5), (5, 3)]
Z_OUT = [(2, 0), (3, 1), (4, 6), (5, 7)]


ROUTE = dict(A="Y", C="Y", D="X", G="Y", E="Y")
STEPS = [
    ("F0", 3), ("B0", 8), ("F1", 0.2), ("A1", 1), ("B1", 0), ("C1", 0), ("A2", 13), ("S", 1), ("D1", 2),
    ("G1", 0), ("C2", 2), ("A3", 0), ("SC", 20), ("E1", 1), ("A4", 0.5), ("C3", 0), ("G2", 0), ("D2", 8),
    ("A5", 0.5), ("C4", 0.2), ("G3", 2), ("E2", 1), ("D3", 2), ("A6", 0.2), ("C5", 0.5), ("G4", 1),
    ("E3", 0.5), ("D4", 3), ("G5", 0.2), ("C6", 0.2), ("E4", 0), ("A7", 0.5), ("D5", 0.5), ("G6", 2),
    ("C7", 0), ("D6", 0.5), ("E5", 0.2), ("G7", 2), ("E6", 0), ("D7", 13), ("E7", 3),
]


class Chain:
    def __init__(self):
        self.last = ()

    def run(self, function, *args, also=(), cost=None):
        Chain.cost = cost
        result = function(*args, after=self.last + tuple(also))
        Chain.cost = None
        index, near = Chain.token
        arrays = Chain.flat(result)
        self.last = (Token(arrays[index], near),)
        return result

    @staticmethod
    def flat(result):
        return jax.tree.leaves(list(result.values()) if isinstance(result, dict) else result)

    cost = None
    token = None


def cost_of(name):
    us = COST.get(name, 1) if Chain.cost is None else Chain.cost
    return pl.CostEstimate(flops=int(us * 1_000_000_000), bytes_accessed=1000, transcendentals=0)


def local(
    dec_in,
    memory,
    cotangent,
    dec_len,
    task_prefix,
    owner,
    mem_len,
    self_norm_gain,
    self_norm_shift,
    self_qkv,
    self_q_bias,
    self_v_bias,
    rel_bias_table,
    self_head_gain,
    self_mix_gain,
    self_mix_shift,
    self_out,
    self_out_bias,
    cross_norm_gain,
    cross_norm_shift,
    cross_q,
    cross_q_bias,
    cross_kv,
    cross_v_bias,
    cross_head_gain,
    cross_mix_gain,
    cross_mix_shift,
    cross_out,
    cross_out_bias,
    ffn_norm_gain,
    ffn_norm_shift,
    ffn_in,
    ffn_in_bias,
    ffn_mid_gain,
    ffn_mid_shift,
    ffn_out,
    ffn_out_bias,
):
    items, length, width = dec_in.shape
    items_grp = owner.shape[1]
    shard_tokens = memory.shape[1]
    seq_size = lax.axis_size("seq")
    parts = lax.axis_size("grp")
    mem_tokens = shard_tokens * seq_size
    ff = ffn_in.shape[1]
    group = lax.axis_index("grp")
    seq_index = lax.axis_index("seq")
    paired = seq_size == 8 and parts == 4 and items == 2

    owner_row = lax.dynamic_index_in_dim(owner, group, 0, keepdims=False)
    slots = jnp.arange(items_grp, dtype=jnp.int32)
    inverse = jnp.sum(jnp.where(owner_row[None, :] == slots[:, None], slots[None, :], 0), axis=1)
    mine = lax.dynamic_slice_in_dim(inverse, seq_index * items, items)
    my_mem_len = jnp.take(mem_len, group * items_grp + mine)

    def exchange(sent):
        return lax.all_to_all(sent, "seq", split_axis=0, concat_axis=0, tiled=True)

    chain = Chain()
    by_item = inverse.reshape(seq_size, items)
    memories = []

    def gather(item):
        sent = chain.run(gather_items, memory, by_item[:, item])[0]
        memories.append(exchange(sent).reshape(mem_tokens, width))

    gather(0)

    def spread(gain):
        return jnp.repeat(gain, HD)

    vectors = [
        self_norm_gain, self_norm_shift, self_q_bias, self_v_bias, spread(self_head_gain),
        self_mix_gain, self_mix_shift, self_out_bias, cross_norm_gain, cross_norm_shift,
        cross_q_bias, cross_v_bias, spread(cross_head_gain), cross_mix_gain, cross_mix_shift,
        cross_out_bias, ffn_norm_gain, ffn_norm_shift, ffn_out_bias,
    ]
    vecs, wides = chain.run(prepare, vectors, [ffn_in_bias, ffn_mid_gain, ffn_mid_shift])
    bias = rel_bias_of(rel_bias_table, length)
    buckets = bucket_lanes(length, rel_bias_table.shape[0])

    starts = [
        chain.run(
            self_forward, item, dec_len, task_prefix, dec_in, bias, self_qkv, self_out, cross_q, vecs
        )
        for item in range(items)
    ]
    for item in range(1, items):
        gather(item)

    core, y = group % 2, group // 2
    x, z = seq_index % 2, seq_index // 2
    if paired:
        order = jnp.stack([(1 - y) * 2 + 1 - core, y * 2 + 1 - core, (1 - y) * 2 + core, y * 2 + core])
        places = jnp.sum(jnp.where(order[None, :] == jnp.arange(parts)[:, None], jnp.arange(parts)[None, :], 0), axis=1)
    else:
        order = places = jnp.arange(parts)
    order = jnp.concatenate([order, places]).astype(jnp.int32)

    bundles = dict(
        A=Bundle([ffn_out.shape], width, parts),
        C=Bundle([ffn_in.shape], width, parts),
        D=Bundle([cross_kv.shape], width, parts),
        G=Bundle([cross_out.shape, cross_q.shape, self_out.shape], width, parts),
        E=Bundle([self_qkv.shape], width, parts, vectors=True),
    )
    ahead, behind, returned, ends, state, done = {}, {}, {}, {}, {}, {}

    def start_sums(result, names):
        for name in names:
            sent, kept = result[f"sent{name}"], result[f"kept{name}"]
            state[name] = (kept, lax.ppermute(sent, "grp", CORE_PAIRS)) if paired else (sent, kept)

    def forward(item, **how):
        ahead[item] = chain.run(
            cross_forward, item, ahead, order, my_mem_len, dec_len, starts[item].x2, starts[item].q2,
            memories[item], cotangent, cross_kv, cross_out, ffn_in, ffn_out, vecs, wides, **how,
        )
        if item == items - 1:
            start_sums(ahead[item], "AC")

    def backward(item, **how):
        behind[item] = chain.run(
            cross_back, item, items, behind, starts, ahead, order, cross_kv, cross_out, cross_q, vecs, **how
        )
        returned[item] = exchange(behind[item].gmem.reshape(seq_size, shard_tokens, width))
        if item == items - 1:
            start_sums(behind[item], "DG")

    def self_backward(**how):
        ends.update(
            chain.run(
                self_back, starts, ahead, behind, order, dec_in, self_qkv, self_out, vecs, buckets, **how
            )
        )
        start_sums(ends, "E")

    def scatter_memory(**how):
        return chain.run(scatter_items, [returned[i] for i in range(items)], inverse, **how)[0]

    if paired:
        side = x.reshape(1)
        inner = ((z == 1) | (z == 2)).astype(jnp.int32).reshape(1)

        def reduce_step(name, step, **how):
            if step == (1 if ROUTE[name] == "Y" else 2):
                sent, kept = chain.run(core_add, *state[name], **how)
                axis, pairs = "grp", Y_PAIRS
            elif step in (1, 2):
                sent, kept = chain.run(split_add, *state[name], side, **how)
                axis, pairs = "seq", X_PAIRS
            elif step in (3, 4, 5):
                sent = kept = chain.run(add, *state[name], **how)[0]
                axis, pairs = "seq", (Z_IN, Z_MID, Z_OUT)[step - 3]
            elif step == 6:
                sent = kept = chain.run(pick, *state[name], inner, **how)[0]
                axis, pairs = "seq", X_PAIRS
            else:
                done[name] = chain.run(bundles[name].finish, *state[name], side, **how)
                return
            state[name] = kept, lax.ppermute(sent, axis, pairs)

        for step, cost in STEPS:
            if step[0] == "F":
                forward(int(step[1]), cost=cost)
            elif step[0] == "B":
                backward(int(step[1]), cost=cost)
            elif step == "S":
                self_backward(cost=cost)
            elif step == "SC":
                grad_memory = scatter_memory(cost=cost)
            else:
                reduce_step(step[0], int(step[1]), cost=cost)
    else:
        for item in range(items):
            forward(item)
            backward(item)
        self_backward()
        none = jnp.zeros((1,), jnp.int32)
        for name in ROUTE:
            share = lax.psum_scatter(jnp.concatenate(state[name]), "grp", scatter_dimension=0, tiled=True)[0]
            done[name] = chain.run(bundles[name].finish, lax.psum(share, "seq"), None, none)
        grad_memory = scatter_memory()

    out, gx = ahead[items - 1].out, ends["gx"]
    g_ffn_out, g_ffn_in, g_cross_kv = (done[name][0] for name in ("A", "C", "D"))
    g_cross_out, g_cross_q, g_self_out = done["G"]
    g_self_qkv, vec = done["E"]
    (
        g_self_norm_gain, g_self_norm_shift, g_self_q_bias, g_self_v_bias, g_self_mix_gain,
        g_self_mix_shift, g_self_out_bias, g_cross_norm_gain, g_cross_norm_shift, g_cross_q_bias,
        g_cross_v_bias, g_cross_mix_gain, g_cross_mix_shift, g_cross_out_bias, g_ffn_norm_gain,
        g_ffn_norm_shift, g_ffn_out_bias, g_ffn_in_bias, g_ffn_mid_gain, g_ffn_mid_shift,
        g_self_head, g_cross_head, g_table,
    ) = chain.run(
        vector_outputs, vec, group.reshape(1), parts, ff, rel_bias_table.shape[0]
    )
    return (
        out,
        gx,
        grad_memory,
        g_self_norm_gain,
        g_self_norm_shift,
        g_self_qkv,
        g_self_q_bias,
        g_self_v_bias,
        g_table,
        g_self_head,
        g_self_mix_gain,
        g_self_mix_shift,
        g_self_out,
        g_self_out_bias,
        g_cross_norm_gain,
        g_cross_norm_shift,
        g_cross_q,
        g_cross_q_bias,
        g_cross_kv,
        g_cross_v_bias,
        g_cross_head,
        g_cross_mix_gain,
        g_cross_mix_shift,
        g_cross_out,
        g_cross_out_bias,
        g_ffn_norm_gain,
        g_ffn_norm_shift,
        g_ffn_in,
        g_ffn_in_bias,
        g_ffn_mid_gain,
        g_ffn_mid_shift,
        g_ffn_out,
        g_ffn_out_bias,
    )


def solution(mesh):
    rows = P(("seq", "grp"), None, None)
    matrix, vector = P("grp", None), P("grp")
    in_specs = (rows, P("grp", "seq", None), rows, P(("seq", "grp")), P(("seq", "grp"))) + (P(),) * 32
    out_specs = (
        rows, rows, P("grp", "seq", None),
        vector, vector, matrix, vector, vector, matrix, vector, vector, vector, matrix, vector,
        vector, vector, matrix, vector, matrix, vector, vector, vector, vector, matrix, vector,
        vector, vector, matrix, vector, vector, vector, matrix, vector,
    )
    return jax.shard_map(local, mesh=mesh, in_specs=in_specs, out_specs=out_specs, check_vma=False)
```

```python
import functools
import math

import jax
import jax.numpy as jnp
from jax import lax
from jax.experimental import pallas as pl
from jax.experimental.pallas import tpu as pltpu
from jax.sharding import PartitionSpec as P

H = 12
HD = 64
EPSILON = 1e-05
FACTOR = 1.0 / math.sqrt(HD)
MASKED = -1000000000.0
F32 = jnp.float32
BF16 = jnp.bfloat16
PAIR = 2 * HD
PAIRS = H // 2

(
    SELF_GAIN,
    SELF_SHIFT,
    SELF_QB,
    SELF_VB,
    SELF_HEAD,
    SELF_MIX_GAIN,
    SELF_MIX_SHIFT,
    SELF_OB,
    CROSS_GAIN,
    CROSS_SHIFT,
    CROSS_QB,
    CROSS_VB,
    CROSS_HEAD,
    CROSS_MIX_GAIN,
    CROSS_MIX_SHIFT,
    CROSS_OB,
    FFN_GAIN,
    FFN_SHIFT,
    FFN_OB,
) = range(19)
IN_BIAS, MID_GAIN, MID_SHIFT, TABLE = 20, 24, 28, 32
VEC_ROWS = 64


def dot(left, right):
    return jnp.dot(left, right, preferred_element_type=F32)


def dot_rows(left, right):
    return lax.dot_general(left, right, (((1,), (1,)), ((), ())), preferred_element_type=F32)


def dot_cols(left, right):
    return lax.dot_general(left, right, (((0,), (0,)), ((), ())), preferred_element_type=F32)


def normalize(values):
    average = jnp.mean(values, axis=-1, keepdims=True)
    centered = values - average
    spread = jnp.mean(centered * centered, axis=-1, keepdims=True)
    scale = lax.rsqrt(spread + EPSILON)
    return centered * scale, scale


def normalize_back(grad, normed, scale):
    mean_grad = jnp.mean(grad, axis=-1, keepdims=True)
    mean_both = jnp.mean(grad * normed, axis=-1, keepdims=True)
    return scale * (grad - mean_grad - normed * mean_both)


def total(values):
    return jnp.sum(values.astype(F32), axis=0, keepdims=True)


def lanes(start, size):
    return pl.ds(pl.multiple_of(start, 128), size)


def pick_head(values, half, axis):
    place = lax.broadcasted_iota(jnp.int32, values.shape, axis)
    inside = (place < HD) if half == 0 else (place >= HD)
    return jnp.where(inside, values, jnp.zeros_like(values))


def attend_pair(queries, keys, values, score_fn, e_ref, inv_ref, first):
    values_t = values.T
    ones = jnp.ones((16, values.shape[0]), BF16)
    scores = [score_fn(dot_rows(keys, pick_head(queries, half, 1)), first + half) for half in range(2)]
    parts = []
    for half in range(2):
        peak = jnp.max(scores[half], axis=0, keepdims=True)
        low = jnp.exp(scores[half] - peak).astype(BF16)
        e_ref[first + half] = low
        mixed = dot(jnp.concatenate([values_t[half * HD : (half + 1) * HD], ones], axis=0), low)
        inverse = 1.0 / mixed[HD : HD + 1]
        inv_ref[pl.ds(first + half, 1), :] = inverse
        parts.append(mixed[:HD] * inverse)
    return jnp.concatenate(parts, axis=0).T


def attend_pair_back(queries, keys, values, grad, prod, e_ref, inv_ref, first, keep_scores):
    keys_t = keys.T
    grad_t = grad.astype(F32).T
    prod_t = prod.T
    grads, deltas, grad_probs = [], [], []
    for half in range(2):
        rows = slice(half * HD, (half + 1) * HD)
        inverse = inv_ref[pl.ds(first + half, 1), :]
        deltas.append(jnp.sum(prod_t[rows], axis=0, keepdims=True) * inverse)
        grads.append(pick_head((grad_t * inverse).astype(BF16), half, 0))
        grad_probs.append(dot(values, grads[half]))
    lows = [e_ref[first + half] for half in range(2)]
    dv = dot_rows(jnp.concatenate(lows, axis=1), jnp.concatenate(grads, axis=1))
    scores = []
    for half in range(2):
        scores.append((lows[half].astype(F32) * (grad_probs[half] - deltas[half])).astype(BF16))
        if keep_scores is not None:
            keep_scores(scores[half], first + half)
    heads = jnp.concatenate([pick_head(queries, half, 1) for half in range(2)], axis=0)
    dk = dot(jnp.concatenate(scores, axis=1), heads)
    dq = [dot(keys_t[half * HD : (half + 1) * HD], scores[half]) for half in range(2)]
    return jnp.concatenate(dq, axis=0).T * FACTOR, dk, dv


class Gradients:
    def __init__(self, order_ref, sems, width):
        self.order_ref, self.sems, self.width = order_ref, sems, width
        self.parts = order_ref.shape[0] // 2
        self.used, self.copies = 0, []

    def load(self, far, near):
        copy = pltpu.make_async_copy(far, near, self.sems.at[self.used])
        copy.start()
        self.copies.append(copy)
        self.used += 1

    def load_left(self, far, near, item):
        size, depth = far.shape[0] // self.parts, far.shape[1]
        for j in range(self.parts):
            rows = pl.ds(pl.multiple_of(self.order_ref[j] * size, 16), size)
            self.load(far.at[rows, :], near.at[pl.ds(j * size, size), pl.ds(item * depth, depth)])

    def load_right(self, far, near, item):
        depth = far.shape[0]
        self.load(far, near.at[pl.ds(item * depth, depth), :])

    def wait(self):
        for copy in self.copies:
            copy.wait()
        self.copies = []

    def place(self, quarter, size):
        return pl.ds(pl.multiple_of(self.order_ref[self.parts + quarter] * size, 16), size)

    def put_left(self, value, near, item):
        size, depth = value.shape[0] // self.parts, value.shape[1]
        for quarter in range(self.parts):
            near[self.place(quarter, size), item * depth : (item + 1) * depth] = value[
                quarter * size : (quarter + 1) * size
            ]

    def put(self, outs, quarter, place, value):
        half = self.parts // 2
        outs[quarter // half][quarter % half, place, :] = value.astype(BF16)

    def sum(self, left, right, outs, row):
        size = left.shape[0] // self.parts
        span = min(left.shape[0], self.width)
        for column in range(right.shape[1] // self.width):
            cols = slice(column * self.width, (column + 1) * self.width)
            for top in range(0, left.shape[0], span):
                value = dot(left[top : top + span, :], right[:, cols])
                for quarter in range(top // size, (top + span - 1) // size + 1):
                    low, high = max(top, quarter * size), min(top + span, (quarter + 1) * size)
                    place = slice(row + low - quarter * size, row + high - quarter * size)
                    self.put(outs, quarter, place, value[low - top : high - top])
            row += size
        return row


def item_rows(ref, item, depth):
    return ref.at[pl.ds(item * depth, depth), :]


def self_forward_kernel(item, io, len_ref, prefix_ref):
    io.load("x", "vecs", "qkv_w", "bias", "out_w", "q2_w")
    _, length, width = io.x.shape
    vec_ref = io.vecs

    def vec(row):
        return vec_ref[row : row + 1, :]

    io.need("x", "vecs")
    x = io.x[item].astype(F32)
    normed, _ = normalize(x)
    low = (normed * vec(SELF_GAIN) + vec(SELF_SHIFT)).astype(BF16)
    io.n1t[...] = low.T
    io.store("n1t")
    io.need("qkv_w")
    queries = dot(low, io.qkv_w[:, :width]) + vec(SELF_QB)
    io.qkv[:, :width] = queries.astype(BF16) * jnp.asarray(FACTOR, BF16)
    io.qkv[:, width : 2 * width] = dot(low, io.qkv_w[:, width : 2 * width]).astype(BF16)
    values = dot(low, io.qkv_w[:, 2 * width :]) + vec(SELF_VB)
    io.qkv[:, 2 * width :] = values.astype(BF16)
    io.store("qkv")
    key_pos = lax.broadcasted_iota(jnp.int32, (length, length), 0)
    query_pos = lax.broadcasted_iota(jnp.int32, (length, length), 1)
    allowed = (key_pos < len_ref[item]) & ((key_pos <= query_pos) | (key_pos < prefix_ref[item]))
    io.inv[...] = jnp.zeros_like(io.inv)
    io.need("bias")

    def scores_of(scores, head):
        return jnp.where(allowed, scores + io.bias[head].astype(F32), MASKED)

    def one_pair(pair, _):
        base = pair * PAIR
        io.mixed[:, lanes(base, PAIR)] = attend_pair(
            io.qkv[:, lanes(base, PAIR)],
            io.qkv[:, lanes(base + width, PAIR)],
            io.qkv[:, lanes(base + 2 * width, PAIR)],
            scores_of, io.e, io.inv, 2 * pair,
        )
        return 0

    lax.fori_loop(0, PAIRS, one_pair, 0, unroll=2)
    io.store("e", "inv", "mixed")
    normed, _ = normalize(io.mixed[...] * vec(SELF_HEAD))
    low = (normed * vec(SELF_MIX_GAIN) + vec(SELF_MIX_SHIFT)).astype(BF16)
    io.z1t[...] = low.T
    io.store("z1t")
    io.need("out_w")
    x2 = x + dot(low, io.out_w[...]) + vec(SELF_OB)
    io.x2[...] = x2
    io.store("x2")
    normed, _ = normalize(x2)
    low = (normed * vec(CROSS_GAIN) + vec(CROSS_SHIFT)).astype(BF16)
    io.n2t[...] = low.T
    io.need("q2_w")
    queries = dot(low, io.q2_w[...]) + vec(CROSS_QB)
    io.q2[...] = queries.astype(BF16) * jnp.asarray(FACTOR, BF16)
    io.store("n2t", "q2")


def gelu_parts(hidden):
    gate = 0.5 * (1.0 + lax.erf(hidden * math.sqrt(0.5)))
    slope = hidden * (jnp.exp(-0.5 * hidden * hidden) * (1.0 / math.sqrt(2.0 * math.pi)))
    return hidden * gate, gate + slope


def cross_forward_kernel(item, last, io, mem_len_ref, dec_len_ref, *refs):
    act_ref, grad_ref, slope_ref, mid_ref = refs[-4:]
    io.load("mem", "kv_w", "vecs")
    length, width = io.x2.shape
    mem_tokens = io.mem.shape[0]
    ff = io.in_w.shape[1]
    tiles = ff // width
    mem_ref, kv_ref, kv_w, vec_ref, wide_ref = io.mem, io.kv, io.kv_w, io.vecs, io.wides
    e_ref, inv_ref, mixed_ref, q2_ref, vg_ref = io.e, io.inv, io.mixed, io.q2, io.vg
    out_w, in_w, ffn_w = io.out_w, io.in_w, io.ffn_w
    if last:
        order_ref, left_out, right_out, left_in, right_in, sems = refs[:-4]
        grads = Gradients(order_ref, sems, width)
        hid_ref, cot_low_ref = item_rows(right_in, item, length), item_rows(right_out, item, length)
    else:
        hid_ref, cot_low_ref = io.hid, io.cot_low

    def vec(row):
        return vec_ref[row : row + 1, :]

    io.need("mem", "kv_w", "vecs")
    io.load("q2", "x2", "out_w", "in_w", "wides")
    io.load("cot", at=item)
    io.load("ffn_w")
    if last:
        for i in range(item):
            grads.load_left(io.far[f"midt{i}"], left_out, i)
            grads.load_right(io.far[f"cot_low{i}"], right_out, i)
            grads.load_left(io.far[f"n3t{i}"], left_in, i)
            grads.load_right(io.far[f"hid{i}"], right_in, i)
    io.memt[...] = mem_ref[...].T
    io.store("memt")
    kv_ref[:, :width] = dot(mem_ref[...], kv_w[:, :width]).astype(BF16)
    kv_ref[:, width:] = (dot(mem_ref[...], kv_w[:, width:]) + vec(CROSS_VB)).astype(BF16)
    io.store("kv")
    io.need("q2")
    mem_len = mem_len_ref[item]
    inv_ref[...] = jnp.zeros_like(inv_ref)

    def scores_of(scores, head):
        del head
        key_pos = lax.broadcasted_iota(jnp.int32, (mem_tokens, length), 0)
        return jnp.where(key_pos < mem_len, scores, MASKED)

    def one_pair(pair, _):
        base = pair * PAIR
        mixed_ref[:, lanes(base, PAIR)] = attend_pair(
            q2_ref[:, lanes(base, PAIR)],
            kv_ref[:, lanes(base, PAIR)],
            kv_ref[:, lanes(base + width, PAIR)],
            scores_of, e_ref, inv_ref, 2 * pair,
        )
        return 0

    lax.fori_loop(0, PAIRS, one_pair, 0, unroll=2)
    io.store("e", "inv", "mixed")
    normed, _ = normalize(mixed_ref[...] * vec(CROSS_HEAD))
    low = (normed * vec(CROSS_MIX_GAIN) + vec(CROSS_MIX_SHIFT)).astype(BF16)
    io.z2t[...] = low.T
    io.store("z2t")
    io.need("x2", "out_w")
    x3 = io.x2[...] + dot(low, out_w[...]) + vec(CROSS_OB)
    norm3, scale3 = normalize(x3)
    n3 = (norm3 * vec(FFN_GAIN) + vec(FFN_SHIFT)).astype(BF16)
    if last:
        grads.put_left(n3.T, left_in, item)
    else:
        io.n3t[...] = n3.T
        io.store("n3t")
    io.need("in_w", "wides")

    def hidden_tile(tile, sums):
        cols = lanes(tile * width, width)
        hidden = dot(n3, in_w[:, cols]) + wide_ref[0:1, cols]
        act, slope = gelu_parts(hidden)
        act_ref[:, cols] = act
        slope_ref[:, cols] = slope.astype(BF16)
        return sums + jnp.sum(act, axis=-1, keepdims=True)

    sums = lax.fori_loop(0, tiles, hidden_tile, jnp.zeros((length, 1), F32), unroll=True)
    average = sums / ff

    def spread_tile(tile, sums):
        centered = act_ref[:, lanes(tile * width, width)] - average
        return sums + jnp.sum(centered * centered, axis=-1, keepdims=True)

    sums = lax.fori_loop(0, tiles, spread_tile, jnp.zeros((length, 1), F32), unroll=True)
    scale = lax.rsqrt(sums / ff + EPSILON)

    def middle_tile(tile, _):
        cols = lanes(tile * width, width)
        normed = (act_ref[:, cols] - average) * scale
        act_ref[:, cols] = normed
        low = (normed * wide_ref[1:2, cols] + wide_ref[2:3, cols]).astype(BF16)
        mid_ref[:, cols] = low
        if last:
            left_out[grads.place(tile, width), item * length : (item + 1) * length] = low.T
        else:
            io.midt[pl.ds(pl.multiple_of(tile * width, 128), width), :] = low.T
        return 0

    lax.fori_loop(0, tiles, middle_tile, 0, unroll=True)
    if not last:
        io.store("midt")
    io.need("ffn_w", "cot")
    result = x3 + dot(mid_ref[...], ffn_w[...]) + vec(FFN_OB)
    io.out[...] = result.astype(BF16)
    io.store("out", at=item)

    valid = lax.broadcasted_iota(jnp.int32, (length, 1), 0) < dec_len_ref[item]
    cot = jnp.where(valid, io.cot[...].astype(F32), 0.0)
    cot_low_ref[...] = cot.astype(BF16)
    if not last:
        io.store("cot_low")
    vg_ref[...] = jnp.zeros_like(vg_ref)

    def grad_mid_tile(tile, sums):
        cols = lanes(tile * width, width)
        grad_mid = dot_rows(cot_low_ref[...], ffn_w[cols, :])
        normed = act_ref[:, cols]
        vg_ref[pl.ds(MID_GAIN + tile, 1), :] = total(grad_mid * normed)
        vg_ref[pl.ds(MID_SHIFT + tile, 1), :] = total(grad_mid)
        grad = grad_mid * wide_ref[1:2, cols]
        grad_ref[:, cols] = grad.astype(BF16)
        return (
            sums[0] + jnp.sum(grad, axis=-1, keepdims=True),
            sums[1] + jnp.sum(grad * normed, axis=-1, keepdims=True),
        )

    zero = jnp.zeros((length, 1), F32)
    sum_grad, sum_both = lax.fori_loop(0, tiles, grad_mid_tile, (zero, zero), unroll=True)
    mean_grad, mean_both = sum_grad / ff, sum_both / ff

    def hidden_back_tile(tile, _):
        cols = lanes(tile * width, width)
        grad = scale * (grad_ref[:, cols].astype(F32) - mean_grad - act_ref[:, cols] * mean_both)
        low = (grad * slope_ref[:, cols].astype(F32)).astype(BF16)
        hid_ref[:, cols] = low
        vg_ref[pl.ds(IN_BIAS + tile, 1), :] = total(low)
        return 0

    lax.fori_loop(0, tiles, hidden_back_tile, 0, unroll=True)
    if not last:
        io.store("hid")
    grad_n3 = dot_rows(hid_ref[...], in_w[...])
    vg_ref[FFN_GAIN : FFN_GAIN + 1, :] = total(grad_n3 * norm3)
    vg_ref[FFN_SHIFT : FFN_SHIFT + 1, :] = total(grad_n3)
    vg_ref[FFN_OB : FFN_OB + 1, :] = total(cot_low_ref[...])
    gx3 = normalize_back(grad_n3 * vec(FFN_GAIN), norm3, scale3) + cot
    io.gx3[...] = gx3
    io.branch[...] = gx3.astype(BF16)
    io.store("gx3", "branch")
    vg_ref[CROSS_OB : CROSS_OB + 1, :] = total(io.branch[...])
    io.store("vg")
    if last:
        grads.wait()
        grads.sum(left_out, right_out, (io.sentA, io.keptA), 0)
        io.store("sentA", "keptA")
        grads.sum(left_in, right_in, (io.sentC, io.keptC), 0)
        io.store("sentC", "keptC")


def cross_back_kernel(item, last, io, *refs):
    e_ref, _, grad_ref, prod_ref = refs[-4:]
    length, width = io.x2.shape
    mem_tokens = io.kv.shape[0]
    vec_ref, vg_ref = io.vecs, io.vg
    if last:
        order_ref, left_mem, right_mem, left_z, right_z, left_n, right_n, left_s, right_s, sems = refs[:-4]
        grads = Gradients(order_ref, sems, width)
        dkv_ref, dq_ref = item_rows(right_mem, item, mem_tokens), item_rows(right_n, item, length)
    else:
        dkv_ref, dq_ref = io.dkv, io.dq
    io.load("vecs", "mixed", "branch", "out_w", "q2", "inv", "kv")
    pair_sems = refs[-3]
    pair_copies = [
        pltpu.make_async_copy(io.far["e"].at[pl.ds(2 * p, 2)], e_ref.at[pl.ds(2 * p, 2)], pair_sems.at[p])
        for p in range(PAIRS)
    ]
    for copy in pair_copies:
        copy.start()
    io.load("x2", "kv_w", "q2_w", "gx3")
    if last:
        for i in range(item + 1):
            grads.load_left(io.far[f"memt{i}"], left_mem, i)
            grads.load_left(io.far[f"z2t{i}"], left_z, i)
            grads.load_left(io.far[f"n2t{i}"], left_n, i)
            grads.load_left(io.far[f"z1t{i}"], left_s, i)
            grads.load_right(io.far[f"branch{i}"], right_z, i)
            if i < item:
                grads.load_right(io.far[f"dkv{i}"], right_mem, i)
                grads.load_right(io.far[f"dq{i}"], right_n, i)
                grads.load_right(io.far[f"branch2{i}"], right_s, i)

    def vec(row):
        return vec_ref[row : row + 1, :]

    def put(row, value):
        vg_ref[row : row + 1, :] = value

    vg_ref[...] = jnp.zeros_like(vg_ref)
    io.need("vecs", "mixed")
    mixed = io.mixed[...]
    normed, scale = normalize(mixed * vec(CROSS_HEAD))
    io.need("branch", "out_w")
    grad = dot_rows(io.branch[...], io.out_w[...])
    put(CROSS_MIX_GAIN, total(grad * normed))
    put(CROSS_MIX_SHIFT, total(grad))
    grad = normalize_back(grad * vec(CROSS_MIX_GAIN), normed, scale)
    put(CROSS_HEAD, total(grad * mixed))
    grad = (grad * vec(CROSS_HEAD)).astype(BF16)
    grad_ref[...] = grad
    prod_ref[...] = grad.astype(F32) * mixed
    io.need("q2", "inv", "kv")
    for pair in range(PAIRS):
        pair_copies[pair].wait()
        base = pair * PAIR
        cols = slice(base, base + PAIR)
        dq, dk, dv = attend_pair_back(
            io.q2[:, cols], io.kv[:, cols], io.kv[:, base + width : base + width + PAIR],
            grad_ref[:, cols], prod_ref[:, cols], e_ref, io.inv, 2 * pair, None,
        )
        dq_ref[:, cols] = dq.astype(BF16)
        dkv_ref[:, cols] = dk.astype(BF16)
        dkv_ref[:, base + width : base + width + PAIR] = dv.astype(BF16)

    if not last:
        io.store("dkv", "dq")
    put(CROSS_VB, total(dkv_ref[:, width:]))
    step = 256
    io.need("kv_w")

    def memory_tile(tile, _):
        cols = lanes(tile * step, step)
        io.gmem[:, cols] = dot_rows(dkv_ref[...], io.kv_w[cols, :]).astype(BF16)
        return 0

    lax.fori_loop(0, width // step, memory_tile, 0, unroll=True)
    io.store("gmem")
    put(CROSS_QB, total(dq_ref[...]))
    io.need("x2", "q2_w", "gx3")
    normed, scale = normalize(io.x2[...])
    grad = dot_rows(dq_ref[...], io.q2_w[...])
    put(CROSS_GAIN, total(grad * normed))
    put(CROSS_SHIFT, total(grad))
    gx2 = normalize_back(grad * vec(CROSS_GAIN), normed, scale) + io.gx3[...]
    io.gx2[...] = gx2
    io.branch2[...] = gx2.astype(BF16)
    io.store("gx2", "branch2")
    put(SELF_OB, total(io.branch2[...]))
    io.store("vg")
    if last:
        right_s[item * length : (item + 1) * length, :] = io.branch2[...]
        grads.wait()
        grads.sum(left_mem, right_mem, (io.sentD, io.keptD), 0)
        io.store("sentD", "keptD")
        row = 0
        for left, right in ((left_z, right_z), (left_n, right_n), (left_s, right_s)):
            row = grads.sum(left, right, (io.sentG, io.keptG), row)
        io.store("sentG", "keptG")


def self_back_kernel(items, io, order_ref, left, right, vg_refs, sems, grad_ref, prod_ref, diag_ref):
    _, length, width = io.x.shape
    shared = ("mixed", "branch", "qkv", "inv", "e")
    io.load("vecs", "mixed0", "branch0", "out_w", "qkv0", "inv0", "e0", "x", "qkv_w", "gx20", "buckets")
    for item in range(1, items):
        io.load(*[f"{name}{item}" for name in shared + ("gx2",)])
    grads = Gradients(order_ref, sems, width)
    for item in range(items):
        grads.load_left(io.far[f"n1t{item}"], left, item)
        for i, name in enumerate(("vgf", "vgb")):
            grads.load(io.far[f"{name}{item}"], vg_refs.at[2 * item + i])
    own = 2 * items
    for item in range(items):
        self_back_item(item, io, item_rows(right, item, length), vg_refs.at[own + item], grad_ref, prod_ref, diag_ref)
    grads.wait()
    outs = (io.sentE, io.keptE)
    grads.sum(left, right.at[:, pl.ds(width, 2 * width)], (io.sentH, io.keptH), 0)
    io.store("sentH", "keptH")
    row = grads.sum(left, right.at[:, pl.ds(0, width)], outs, 0)
    value = vg_refs[0]
    for i in range(1, 3 * items):
        value = value + vg_refs[i]
    for quarter in range(grads.parts):
        grads.put(outs, quarter, slice(row, row + VEC_ROWS), value)
    io.store("sentE", "keptE")


def self_back_item(item, io, dqkv_ref, vg_ref, grad_ref, prod_ref, diag_ref):
    _, length, width = io.x.shape
    vec_ref = io.vecs
    near = {name: io.near[f"{name}{item}"] for name in ("mixed", "branch", "qkv", "inv", "e", "gx2")}
    qkv_ref = near["qkv"]

    def vec(row):
        return vec_ref[row : row + 1, :]

    def put(row, value):
        vg_ref[row : row + 1, :] = value

    vg_ref[...] = jnp.zeros_like(vg_ref)
    diag_ref[...] = jnp.zeros_like(diag_ref)
    if item == 0:
        io.need("vecs")
    io.need(f"mixed{item}")
    mixed = near["mixed"][...]
    normed, scale = normalize(mixed * vec(SELF_HEAD))
    io.need(f"branch{item}")
    if item == 0:
        io.need("out_w")
    grad = dot_rows(near["branch"][...], io.out_w[...])
    put(SELF_MIX_GAIN, total(grad * normed))
    put(SELF_MIX_SHIFT, total(grad))
    grad = normalize_back(grad * vec(SELF_MIX_GAIN), normed, scale)
    put(SELF_HEAD, total(grad * mixed))
    grad = (grad * vec(SELF_HEAD)).astype(BF16)
    grad_ref[...] = grad
    prod_ref[...] = grad.astype(F32) * mixed
    io.need(f"qkv{item}", f"inv{item}", f"e{item}")
    backwards = (
        lax.broadcasted_iota(jnp.int32, (length, length), 0)
        + lax.broadcasted_iota(jnp.int32, (length, length), 1)
        == length - 1
    ).astype(F32).astype(BF16)

    def keep_scores(scores, head):
        flipped = dot(backwards, scores)
        padded = jnp.concatenate([flipped, jnp.zeros_like(flipped)], axis=1)
        rolled = pltpu.roll(padded, 0, 1, stride=1, stride_axis=0)
        diag_ref[pl.ds(head, 1), :] = jnp.sum(rolled, axis=0, keepdims=True)

    def one_pair(pair, _):
        base = pair * PAIR
        cols = lanes(base, PAIR)
        dq, dk, dv = attend_pair_back(
            qkv_ref[:, cols], qkv_ref[:, lanes(base + width, PAIR)],
            qkv_ref[:, lanes(base + 2 * width, PAIR)],
            grad_ref[:, cols], prod_ref[:, cols], near["e"], near["inv"], 2 * pair, keep_scores,
        )
        dqkv_ref[:, cols] = dq.astype(BF16)
        dqkv_ref[:, lanes(base + width, PAIR)] = dk.astype(BF16)
        dqkv_ref[:, lanes(base + 2 * width, PAIR)] = dv.astype(BF16)
        return 0

    lax.fori_loop(0, PAIRS, one_pair, 0, unroll=2)
    if item == 0:
        io.need("buckets", "x", "qkv_w")
    table = jnp.dot(
        diag_ref[...], io.buckets[...], precision=lax.Precision.HIGHEST, preferred_element_type=F32
    )
    vg_ref[TABLE : TABLE + 16, : table.shape[1]] = table
    put(SELF_QB, total(dqkv_ref[:, :width]))
    put(SELF_VB, total(dqkv_ref[:, 2 * width :]))
    normed, scale = normalize(io.x[item].astype(F32))
    grad = dot_rows(dqkv_ref[...], io.qkv_w[...])
    put(SELF_GAIN, total(grad * normed))
    put(SELF_SHIFT, total(grad))
    io.need(f"gx2{item}")
    gx = normalize_back(grad * vec(SELF_GAIN), normed, scale) + near["gx2"][...]
    io.gx[item] = gx.astype(BF16)
    if item == io.gx.shape[0] - 1:
        io.store("gx")


SMEM = pl.BlockSpec(memory_space=pltpu.SMEM)
VMEM = pl.BlockSpec(memory_space=pltpu.VMEM)
ANY = pl.BlockSpec(memory_space=pl.ANY)
HBM = pl.BlockSpec(memory_space=pltpu.HBM)
MIB = 1024 * 1024


COST = dict(
    self_forward=11, cross_forward=28, cross_back=18, self_back=10, weight_grads=5, finish=2, split_add=1, core_add=1, first_add=2, join=1,
    gather_items=3, scatter_items=4, add=1, pick=1, vectors=1,
)
COST_SCALE = 3_000_000


class Kept:
    def __init__(self, shape, dtype):
        self.shape, self.dtype = tuple(shape), dtype


class Stored(Kept):
    pass


class Token:
    def __init__(self, array, near):
        self.space = pltpu.VMEM if near else pltpu.HBM
        self.spec = VMEM if near else HBM
        self.array = array

    def operand(self):
        return pltpu.with_memory_space_constraint(self.array, self.space)


def token_args(after):
    return [t.spec for t in after], [t.operand() for t in after]


def call(kernel, name, ins, outs, scratch=(), after=(), limit=16, scalars=(), far=()):
    after_specs, after_args = token_args(after)
    first = len(scalars) + len(far) + len(ins)
    last = first + len(after)

    def body(*refs):
        kernel(*refs[:first], *refs[last:])

    ins = [pltpu.with_memory_space_constraint(a, pltpu.VMEM) for a in ins]
    far = [pltpu.with_memory_space_constraint(a, pltpu.HBM) for a in far]
    shapes = [(pltpu.HBM if isinstance(o, Stored) else pltpu.VMEM)(o.shape, o.dtype) for o in outs]
    Chain.token = 0, not isinstance(outs[0], Stored)
    return pl.pallas_call(
        body,
        out_shape=shapes,
        in_specs=[SMEM] * len(scalars) + [HBM] * len(far) + [VMEM] * len(ins) + after_specs,
        out_specs=[VMEM] * len(shapes),
        scratch_shapes=list(scratch),
        compiler_params=pltpu.CompilerParams(vmem_limit_bytes=limit * MIB),
        cost_estimate=cost_of(name),
        name=name,
    )(*scalars, *far, *ins, *after_args)


class Stream:
    def __init__(self, ins, outs, far, near, sems):
        self.names = list(ins) + list(outs)
        self.far, self.near = dict(zip(self.names, far)), dict(zip(self.names, near))
        self.sems = dict(zip(self.names, range(len(self.names))))
        self.sem_refs = sems
        self.loading, self.storing = {}, []

    def __getattr__(self, name):
        return self.near[name]

    def load(self, *names, at=None):
        for name in names:
            far = self.far[name] if at is None else self.far[name].at[at]
            copy = pltpu.make_async_copy(far, self.near[name], self.sem_refs.at[self.sems[name]])
            copy.start()
            self.loading[name] = copy

    def need(self, *names):
        for name in names:
            self.loading.pop(name).wait()

    def store(self, *names, at=None):
        for name in names:
            far = self.far[name] if at is None else self.far[name].at[at]
            copy = pltpu.make_async_copy(self.near[name], far, self.sem_refs.at[self.sems[name]])
            copy.start()
            self.storing.append(copy)

    def drain(self):
        assert not self.loading
        for copy in self.storing:
            copy.wait()


def stream_call(kernel, name, ins, outs, scratch=(), after=(), scalars=(), limit=16, kept=(), free=(), token="vg", gathered={}, far=None, parted=()):
    far = far or {}
    after_specs, after_args = token_args(after)
    n_in, n_out = len(ins), len(outs)
    far_outs = [n for n in outs if n not in kept]

    def body(*refs):
        refs = list(refs)

        def take(count):
            taken, refs[:] = refs[:count], refs[count:]
            return taken

        scalar_refs, far_in = take(len(scalars)), take(n_in)
        far_only = dict(zip(far, take(len(far))))
        take(len(after) + len(filled))
        out_refs = dict(zip(outs, take(n_out)))
        near_in = take(n_in)
        near_out = dict(zip(far_outs, take(len(far_outs))))
        sems = refs.pop()
        near_out.update({n: out_refs[n] for n in kept})
        io = Stream(
            ins, outs, far_in + [out_refs[n] for n in outs], near_in + [near_out[n] for n in outs], sems
        )
        io.far.update(far_only)
        kernel(io, *scalar_refs, *refs)
        io.drain()

    filled = {n: array for n, (_, array) in gathered.items() if array is not None}
    before = len(scalars) + n_in + len(far) + len(after)
    aliases = {before + i: list(outs).index(n) for i, n in enumerate(filled)}
    shapes = [
        pltpu.VMEM(s, d) if n in kept else pltpu.HBM((gathered[n][0],) + s if n in gathered else s, d)
        for n, (s, d) in outs.items()
    ]
    buffers = [pltpu.VMEM(a.shape[1:] if n in parted else a.shape, a.dtype) for n, a in ins.items()]
    buffers += [pltpu.VMEM(*outs[n]) for n in far_outs]
    results = pl.pallas_call(
        body,
        out_shape=shapes,
        in_specs=[SMEM] * len(scalars)
        + [ANY if n in free else HBM for n in ins]
        + [HBM] * len(far)
        + after_specs
        + [HBM] * len(filled),
        input_output_aliases=aliases,
        out_specs=[VMEM if n in kept else HBM for n in outs],
        scratch_shapes=buffers + list(scratch) + [pltpu.SemaphoreType.DMA((n_in + n_out,))],
        compiler_params=pltpu.CompilerParams(vmem_limit_bytes=limit * MIB),
        cost_estimate=cost_of(name),
        name=name,
    )(
        *scalars,
        *[a if n in free else pltpu.with_memory_space_constraint(a, pltpu.HBM) for n, a in ins.items()],
        *[pltpu.with_memory_space_constraint(a, pltpu.HBM) for a in far.values()],
        *after_args,
        *filled.values(),
    )
    Chain.token = list(outs).index(token), token in kept
    return Result(zip(outs, results))


class Result(dict):
    def __getattr__(self, name):
        return self[name]


def self_forward(item, dec_len, prefix, x, bias, qkv_w, out_w, q2_w, vecs, after):
    _, length, width = x.shape
    outs = {
        "n1t": ((width, length), BF16),
        "qkv": ((length, 3 * width), BF16),
        "e": ((H, length, length), BF16),
        "inv": ((16, length), F32),
        "mixed": ((length, width), F32),
        "z1t": ((width, length), BF16),
        "x2": ((length, width), F32),
        "n2t": ((width, length), BF16),
        "q2": ((length, width), BF16),
    }
    ins = dict(x=x, bias=bias, qkv_w=qkv_w, out_w=out_w, q2_w=q2_w, vecs=vecs)
    return stream_call(
        functools.partial(self_forward_kernel, item), "self_forward", ins, outs, after=after,
        scalars=(dec_len, prefix), limit=40, token="inv",
    )


def sums_of(names, rows, parts, width):
    outs = {}
    for name, count in zip(names, rows):
        outs.update({f"{side}{name}": ((parts // 2, count, width), BF16) for side in ("sent", "kept")})
    return outs


def operand_pair(rows, depth, columns):
    return [pltpu.VMEM((rows, depth), BF16), pltpu.VMEM((depth, columns), BF16)]


def cross_forward(item, earlier, order, mem_len, dec_len, x2, q2, mem, cot, kv_w, out_w, in_w, ffn_w, vecs, wides, after):
    length, width = x2.shape
    items = cot.shape[0]
    last = item == items - 1
    mem_tokens = mem.shape[0]
    ff = in_w.shape[1]
    parts = order.shape[0] // 2
    outs = {
        "out": ((length, width), BF16),
        "kv": ((mem_tokens, 2 * width), BF16),
        "e": ((H, mem_tokens, length), BF16),
        "inv": ((16, length), F32),
        "mixed": ((length, width), F32),
        "memt": ((width, mem_tokens), BF16),
        "z2t": ((width, length), BF16),
        "gx3": ((length, width), F32),
        "branch": ((length, width), BF16),
        "vg": ((VEC_ROWS, width), F32),
    }
    operands = {
        "n3t": ((width, length), BF16),
        "hid": ((length, ff), BF16),
        "midt": ((ff, length), BF16),
        "cot_low": ((length, width), BF16),
    }
    ins = dict(
        x2=x2, q2=q2, mem=mem, cot=cot, kv_w=kv_w, out_w=out_w, in_w=in_w, ffn_w=ffn_w, vecs=vecs, wides=wides
    )
    scratch = [pltpu.VMEM((length, ff), F32)] + [pltpu.VMEM((length, ff), BF16)] * 3
    scalars, far, sums = (mem_len, dec_len), {}, {}
    if last:
        sums = sums_of("AC", (ff // parts, ff // parts), parts, width)
        outs.update(sums)
        scalars += (order,)
        far = {f"{n}{i}": earlier[i][n] for i in range(item) for n in operands}
        scratch = (
            operand_pair(ff, items * length, width)
            + operand_pair(width, items * length, ff)
            + [pltpu.SemaphoreType.DMA((item * (2 * parts + 2),))]
            + scratch
        )
    else:
        outs.update(operands)
    return stream_call(
        functools.partial(cross_forward_kernel, item, last), "cross_forward", ins, outs,
        scratch=scratch, after=after, scalars=scalars, limit=58 if last else 50, free=("mem",),
        gathered=dict(out=(items, earlier[item - 1].out if item else None)), far=far, parted=("cot",),
    )


def cross_back(item, items, earlier, starts, ahead, order, kv_w, out_w, q2_w, vecs, after):
    a, x2, q2 = ahead[item], starts[item].x2, starts[item].q2
    last = item == items - 1
    length, width = x2.shape
    mem_tokens = a.kv.shape[0]
    parts = order.shape[0] // 2
    outs = {
        "gmem": ((mem_tokens, width), BF16),
        "gx2": ((length, width), F32),
        "branch2": ((length, width), BF16),
        "vg": ((VEC_ROWS, width), F32),
    }
    operands = {"dq": ((length, width), BF16), "dkv": ((mem_tokens, 2 * width), BF16)}
    ins = dict(
        branch=a.branch, gx3=a.gx3, mixed=a.mixed, kv=a.kv, inv=a.inv, q2=q2, x2=x2,
        kv_w=kv_w, out_w=out_w, q2_w=q2_w, vecs=vecs,
    )
    scratch = [
        pltpu.VMEM(a.e.shape, a.e.dtype),
        pltpu.SemaphoreType.DMA((PAIRS,)),
        pltpu.VMEM((length, width), BF16),
        pltpu.VMEM((length, width), F32),
    ]
    scalars, far, sums = (), dict(e=a.e), {}
    if last:
        quarter = width // parts
        sums = sums_of("DG", (2 * quarter, 3 * quarter), parts, width)
        outs.update(sums)
        scalars = (order,)
        for i in range(items):
            far.update({f"memt{i}": ahead[i].memt, f"z2t{i}": ahead[i].z2t, f"branch{i}": ahead[i].branch})
            far.update({f"n2t{i}": starts[i].n2t, f"z1t{i}": starts[i].z1t})
            if i < item:
                b = earlier[i]
                far.update({f"dkv{i}": b.dkv, f"dq{i}": b.dq, f"branch2{i}": b.branch2})
        scratch = (
            operand_pair(width, items * mem_tokens, 2 * width)
            + operand_pair(width, items * length, width) * 3
            + [pltpu.SemaphoreType.DMA((items * (4 * parts + 1) + item * 3,))]
            + scratch
        )
    else:
        outs.update(operands)
    return stream_call(
        functools.partial(cross_back_kernel, item, last), "cross_back", ins, outs, scratch=scratch, after=after,
        scalars=scalars, limit=50 if last else 34, far=far,
    )


def self_back(starts, ahead, behind, order, x, qkv_w, out_w, vecs, buckets, after):
    items, length, width = x.shape
    parts = order.shape[0] // 2
    ins = dict(x=x, qkv_w=qkv_w, out_w=out_w, vecs=vecs, buckets=buckets)
    far = {}
    for item in range(items):
        a, b = starts[item], behind[item]
        ins.update({f"{name}{item}": a[name] for name in ("mixed", "qkv", "e", "inv")})
        ins.update({f"branch{item}": b.branch2, f"gx2{item}": b.gx2})
        far.update({f"n1t{item}": a.n1t, f"vgf{item}": ahead[item].vg, f"vgb{item}": b.vg})
    sums = sums_of("EH", (width // parts + VEC_ROWS, 2 * width // parts), parts, width)
    outs = {"gx": (x.shape, BF16), **sums}
    scratch = operand_pair(width, items * length, 3 * width) + [
        pltpu.VMEM((3 * items, VEC_ROWS, width), F32),
        pltpu.SemaphoreType.DMA((items * (parts + 2),)),
        pltpu.VMEM((length, width), BF16),
        pltpu.VMEM((length, width), F32),
        pltpu.VMEM((16, 2 * length), F32),
    ]
    return stream_call(
        functools.partial(self_back_kernel, items), "self_back", ins, outs, scratch=scratch, after=after,
        scalars=(order,), limit=40, far=far, token="keptE",
    )


def prepare_kernel(narrow, wide, *refs):
    ins, (vec_ref, wide_ref) = refs[: narrow + wide], refs[narrow + wide :]
    vec_ref[...] = jnp.zeros_like(vec_ref)
    wide_ref[...] = jnp.zeros_like(wide_ref)
    for row in range(narrow):
        vec_ref[row, :] = ins[row][...].astype(F32)
    for row in range(wide):
        wide_ref[row, :] = ins[narrow + row][...].astype(F32)


def prepare(vectors, wides, after):
    count = len(vectors) + len(wides)
    shapes = [
        pltpu.HBM((24, vectors[0].shape[0]), F32), pltpu.HBM((8, wides[0].shape[0]), F32)
    ]

    after_specs, after_args = token_args(after)

    def body(*refs):
        prepare_kernel(len(vectors), len(wides), *refs[:count], *refs[count + len(after) :])

    Chain.token = 0, False
    return pl.pallas_call(
        body, out_shape=shapes, in_specs=[VMEM] * count + after_specs, out_specs=[VMEM] * 2,
        name="prepare",
    )(*vectors, *wides, *after_args)


def rel_bias_of(table, length):
    count = table.shape[0]
    positions = jnp.arange(length, dtype=jnp.int32)
    offset = jnp.clip(positions[:, None] - positions[None, :], -(count // 2), count // 2 - 1)
    one_hot = (offset + count // 2)[None] == jnp.arange(count, dtype=jnp.int32)[:, None, None]
    return lax.dot_general(
        table, one_hot.astype(BF16), (((0,), (0,)), ((), ())), preferred_element_type=F32
    ).astype(BF16)


def bucket_lanes(length, count):
    offset = length - 1 - jnp.arange(2 * length, dtype=jnp.int32)
    bucket = jnp.clip(offset, -(count // 2), count // 2 - 1) + count // 2
    return (bucket[:, None] == jnp.arange(128, dtype=jnp.int32)[None, :]).astype(F32)


def gather_kernel(slots_ref, memory_ref, out_ref, sems):
    copies = [
        pltpu.make_async_copy(memory_ref.at[slots_ref[i]], out_ref.at[i], sems.at[i])
        for i in range(out_ref.shape[0])
    ]
    for copy in copies:
        copy.start()
    for copy in copies:
        copy.wait()


def gather_items(memory, slots, after):
    count = slots.shape[0]
    return call(
        gather_kernel, "gather_items", (), [Stored((count,) + memory.shape[1:], memory.dtype)],
        scratch=[pltpu.SemaphoreType.DMA((count,))], after=after, scalars=(slots,), far=(memory,), limit=8,
    )


def scatter_kernel(items, slots_ref, *refs):
    parts, out_ref, sems = refs[:items], refs[items], refs[items + 1]
    copies = []
    for p in range(parts[0].shape[0]):
        for j in range(items):
            i = p * items + j
            copies.append(pltpu.make_async_copy(parts[j].at[p], out_ref.at[slots_ref[i]], sems.at[i]))
    for copy in copies:
        copy.start()
    for copy in copies:
        copy.wait()


def scatter_items(parts, slots, after):
    count = slots.shape[0]
    return call(
        functools.partial(scatter_kernel, len(parts)), "scatter_items", (),
        [Stored((count,) + parts[0].shape[1:], parts[0].dtype)],
        scratch=[pltpu.SemaphoreType.DMA((count,))], after=after, scalars=(slots,), far=tuple(parts), limit=8,
    )


class Bundle:
    def __init__(self, shapes, width, parts, vectors=False):
        self.shapes, self.width, self.parts, self.vectors = shapes, width, parts, vectors
        self.blocks = []
        row = 0
        for index, (rows, columns) in enumerate(shapes):
            size = rows // parts
            for column in range(columns // width):
                self.blocks.append((index, column, row, size))
                row += size
        self.vector_row = row
        self.rows = row + (VEC_ROWS if vectors else 0)

    def halves(self, mine_ref, got_ref, own_side):
        half = mine_ref.shape[0]

        def rows_of(start, size):
            pieces = []
            while size:
                part = start // half
                take = min(size, (part + 1) * half - start)
                rows = slice(start - part * half, start - part * half + take)
                value = mine_ref[rows, :].astype(F32)
                if own_side is not None:
                    value = jnp.where(own_side == part, value, got_ref[rows, :].astype(F32))
                pieces.append(value)
                start, size = start + take, size - take
            return pieces

        return rows_of


def finish_kernel(bundles, columns, place_ref, *refs):
    number = len(bundles)
    pairs, outs = refs[: 2 * number], refs[2 * number :]
    vec_ref = outs[-1]
    outs = list(outs)

    def store(out_ref, pieces, cols):
        done = 0
        for piece in pieces:
            out_ref[done : done + piece.shape[0], cols] = piece
            done += piece.shape[0]

    for b, bundle in enumerate(bundles):
        mine_ref, got_ref = pairs[2 * b], pairs[2 * b + 1]
        whole_rows = mine_ref.shape[0] == bundle.rows
        rows_of = bundle.halves(mine_ref, got_ref, None if whole_rows else place_ref[0])
        for index, column, row, size in bundle.blocks:
            first = columns[b] + column * bundle.width
            out_ref = outs[index]
            store(out_ref, rows_of(row, size), slice(first, first + bundle.width))
        if bundle.vectors:
            store(vec_ref, rows_of(bundle.vector_row, VEC_ROWS), slice(None))


def finish(bundles, sums, place, after):
    first = bundles[0]
    if len(bundles) == 1:
        shapes, columns = first.shapes, [0]
    else:
        widths = [bundle.shapes[0][1] for bundle in bundles]
        shapes = [(first.shapes[0][0], sum(widths))]
        columns = [sum(widths[:b]) for b in range(len(bundles))]
    outs = [Stored((rows // first.parts, cols), F32) for rows, cols in shapes]
    if any(bundle.vectors for bundle in bundles):
        outs.append(Kept((VEC_ROWS, first.width), F32))
    ins = []
    for mine, got in sums:
        ins += [mine, mine if got is None else got]
    return call(
        functools.partial(finish_kernel, bundles, columns), "finish", tuple(ins), outs,
        after=after, scalars=(place,), limit=12,
    )


def add_low(left, right):
    return left + right


def first_add_kernel(split, side_ref, left_ref, right_ref, *refs):
    refs = refs[-5:]
    sent_ref, kept_ref, near_left, near_right, sems = refs
    rows = near_left.shape[1]
    half = rows // 2
    copies = []
    for quarter in range(2):
        for part in range(2):
            place = pl.ds(part * half, half)
            if split:
                place = pl.ds(pl.multiple_of((part ^ 1 ^ side_ref[0]) * half, 16), half)
            for far, near in ((left_ref, near_left), (right_ref, near_right)):
                copies.append(
                    pltpu.make_async_copy(
                        far.at[quarter, place, :], near.at[quarter, pl.ds(part * half, half), :],
                        sems.at[len(copies)],
                    )
                )
    for copy in copies:
        copy.start()
    for quarter in range(2):
        for part in range(2):
            for copy in copies[:2]:
                copy.wait()
            copies = copies[2:]
            rows = slice(part * half, (part + 1) * half)
            value = add_low(near_left[quarter, rows, :], near_right[quarter, rows, :])
            if split:
                (sent_ref, kept_ref)[part][quarter] = value
            else:
                (sent_ref, kept_ref)[quarter][rows, :] = value


def first_add(left, right, side, split, after):
    shape = (2, left.shape[1] // 2, left.shape[2]) if split else left.shape[1:]
    after_specs, after_args = token_args(after)
    Chain.token = 1, True
    return pl.pallas_call(
        functools.partial(first_add_kernel, split),
        out_shape=[pltpu.VMEM(shape, BF16)] * 2,
        in_specs=[SMEM, HBM, ANY] + after_specs,
        out_specs=[VMEM] * 2,
        scratch_shapes=[pltpu.VMEM(left.shape, BF16)] * 2 + [pltpu.SemaphoreType.DMA((8,))],
        compiler_params=pltpu.CompilerParams(vmem_limit_bytes=10 * MIB),
        cost_estimate=cost_of("first_add"),
        name="first_add",
    )(side, pltpu.with_memory_space_constraint(left, pltpu.HBM), right, *after_args)


def core_add_kernel(left_ref, right_ref, sent_ref, kept_ref):
    sent_ref[...] = add_low(left_ref[0], right_ref[0])
    kept_ref[...] = add_low(left_ref[1], right_ref[1])


def core_add(left, right, after):
    shape = left.shape[1:]
    return call(core_add_kernel, "core_add", (left, right), [Kept(shape, BF16)] * 2, after=after, limit=8)


def split_add_kernel(side_ref, left_ref, right_ref, sent_ref, kept_ref):
    half = sent_ref.shape[0]
    mine = pl.ds(pl.multiple_of(side_ref[0] * half, 16), half)
    other = pl.ds(pl.multiple_of((1 - side_ref[0]) * half, 16), half)
    sent_ref[...] = add_low(left_ref[other, :], right_ref[other, :])
    kept_ref[...] = add_low(left_ref[mine, :], right_ref[mine, :])


def split_add(left, right, side, after):
    shape = (left.shape[0] // 2, left.shape[1])
    return call(
        split_add_kernel, "split_add", (left, right), [Kept(shape, BF16)] * 2,
        after=after, scalars=(side,), limit=8,
    )


def join_kernel(side_ref, mine_ref, got_ref, out_ref):
    half = mine_ref.shape[0]
    mine = pl.ds(pl.multiple_of(side_ref[0] * half, 16), half)
    other = pl.ds(pl.multiple_of((1 - side_ref[0]) * half, 16), half)
    out_ref[mine, :] = mine_ref[...]
    out_ref[other, :] = got_ref[...]


def join(mine, got, side, after):
    shape = (2 * mine.shape[0], mine.shape[1])
    return call(
        join_kernel, "join", (mine, got), [Kept(shape, BF16)], after=after, scalars=(side,), limit=4
    )


def add_kernel(left_ref, right_ref, out_ref):
    out_ref[...] = add_low(left_ref[...], right_ref[...])


def add(left, right, after):
    return call(add_kernel, "add", (left, right), [Kept(left.shape, BF16)], after=after, limit=4)


def pick_kernel(own_ref, mine_ref, got_ref, out_ref):
    @pl.when(own_ref[0] == 1)
    def _():
        out_ref[...] = mine_ref[...]

    @pl.when(own_ref[0] != 1)
    def _():
        out_ref[...] = got_ref[...]


def pick(mine, got, own, after):
    return call(
        pick_kernel, "pick", (mine, got), [Kept(mine.shape, BF16)], after=after, scalars=(own,), limit=4
    )


def vectors_kernel(parts, group_ref, vec_ref, *refs):
    outs, scratch = refs[:-1], refs[-1]
    group = group_ref[0]
    width = vec_ref.shape[1]
    size = width // parts
    values = vec_ref[...]
    rolled = pltpu.roll(values, lax.rem(width - size * group, width), 1)
    narrow = [row for row in range(FFN_OB + 1) if row not in (SELF_HEAD, CROSS_HEAD)]
    for out, row in zip(outs, narrow):
        out[...] = rolled[row, :size]
    outs = outs[len(narrow) :]
    tiles = outs[0].shape[0] * parts // width
    for out, row in zip(outs, (IN_BIAS, MID_GAIN, MID_SHIFT)):
        if tiles == parts:
            out[...] = vec_ref[pl.ds(row + group, 1), :][0]
    heads = H // parts
    lane = lax.broadcasted_iota(jnp.int32, (width, 128), 0) // HD
    one_hot = (lane == lax.broadcasted_iota(jnp.int32, (width, 128), 1)).astype(F32)
    sums = jnp.dot(values, one_hot, precision=lax.Precision.HIGHEST, preferred_element_type=F32)
    sums = pltpu.roll(sums, lax.rem(128 - heads * group, 128), 1)
    outs[3][...] = sums[SELF_HEAD, :heads]
    outs[4][...] = sums[CROSS_HEAD, :heads]
    scratch[...] = values[TABLE : TABLE + 16, :128].T
    buckets = outs[5].shape[0]
    outs[5][...] = scratch[pl.ds(pl.multiple_of(buckets * group, buckets), buckets), :][:, :H]


def vector_outputs(vec, group, parts, ff, buckets, after):
    width = vec.shape[1]
    outs = [Stored((width // parts,), F32)] * 17 + [Stored((ff // parts,), F32)] * 3
    outs += [Stored((H // parts,), F32)] * 2 + [Stored((buckets // parts, H), F32)]
    return call(
        functools.partial(vectors_kernel, parts), "vectors", (vec,), outs,
        scratch=[pltpu.VMEM((128, 16), F32)], after=after, scalars=(group,), limit=8,
    )


CORE_PAIRS = [(0, 1), (1, 0), (2, 3), (3, 2)]
Y_PAIRS = [(0, 2), (2, 0), (1, 3), (3, 1)]
X_PAIRS = [(0, 1), (1, 0), (2, 3), (3, 2), (4, 5), (5, 4), (6, 7), (7, 6)]
Z_IN = [(0, 2), (1, 3), (6, 4), (7, 5)]
Z_MID = [(2, 4), (4, 2), (3, 5), (5, 3)]
Z_OUT = [(2, 0), (3, 1), (4, 6), (5, 7)]
Z_NEAR = [(0, 2), (2, 0), (1, 3), (3, 1), (4, 6), (6, 4), (5, 7), (7, 5)]
Z_FAR = [(0, 4), (4, 0), (1, 5), (5, 1), (2, 6), (6, 2), (3, 7), (7, 3)]


ROUTE = dict(A="YH", C="XH", D="XH", G="YH", E="XH", H="YH")
STEPS = [
    ("F0", 30), ("B0", 30), ("F1", 0), ("A1", 3), ("C1", 0), ("B1", 13), ("A2", 2), ("C2", 20), ("S", 5),
    ("C3", 1), ("G1", 2), ("D1", 1), ("A3", 3), ("C4", 1), ("SC", 5), ("E1", 0.2), ("A4", 1), ("H1", 0.5),
    ("D2", 1), ("G2", 1), ("C5", 3), ("E2", 3), ("H2", 0), ("G3", 0), ("A5", 1), ("E3", 0.5), ("C6", 0),
    ("G4", 1), ("H3", 2), ("A6", 0.2), ("D3", 0.5), ("D4", 0), ("G5", 0.5), ("H4", 0), ("C7", 1), ("D5", 1),
    ("G6", 1), ("E4", 0.2), ("A7", 1), ("H5", 2), ("D6", 0.2), ("E5", 3), ("G7", 0.5), ("H6", 1), ("D7", 0.2),
    ("E6", 0), ("E7", 0),
]


class Chain:
    def __init__(self):
        self.last = ()

    def run(self, function, *args, also=(), cost=None):
        Chain.cost = cost
        result = function(*args, after=self.last + tuple(also))
        Chain.cost = None
        index, near = Chain.token
        arrays = Chain.flat(result)
        self.last = (Token(arrays[index], near),)
        return result

    @staticmethod
    def flat(result):
        return jax.tree.leaves(list(result.values()) if isinstance(result, dict) else result)

    cost = None
    token = None


def cost_of(name):
    us = COST.get(name, 1) if Chain.cost is None else Chain.cost
    return pl.CostEstimate(flops=int(us * 1_000_000_000), bytes_accessed=1000, transcendentals=0)


def local(
    dec_in,
    memory,
    cotangent,
    dec_len,
    task_prefix,
    owner,
    mem_len,
    self_norm_gain,
    self_norm_shift,
    self_qkv,
    self_q_bias,
    self_v_bias,
    rel_bias_table,
    self_head_gain,
    self_mix_gain,
    self_mix_shift,
    self_out,
    self_out_bias,
    cross_norm_gain,
    cross_norm_shift,
    cross_q,
    cross_q_bias,
    cross_kv,
    cross_v_bias,
    cross_head_gain,
    cross_mix_gain,
    cross_mix_shift,
    cross_out,
    cross_out_bias,
    ffn_norm_gain,
    ffn_norm_shift,
    ffn_in,
    ffn_in_bias,
    ffn_mid_gain,
    ffn_mid_shift,
    ffn_out,
    ffn_out_bias,
):
    items, length, width = dec_in.shape
    items_grp = owner.shape[1]
    shard_tokens = memory.shape[1]
    seq_size = lax.axis_size("seq")
    parts = lax.axis_size("grp")
    mem_tokens = shard_tokens * seq_size
    ff = ffn_in.shape[1]
    group = lax.axis_index("grp")
    seq_index = lax.axis_index("seq")
    paired = seq_size == 8 and parts == 4 and items == 2

    owner_row = lax.dynamic_index_in_dim(owner, group, 0, keepdims=False)
    slots = jnp.arange(items_grp, dtype=jnp.int32)
    inverse = jnp.sum(jnp.where(owner_row[None, :] == slots[:, None], slots[None, :], 0), axis=1)
    mine = lax.dynamic_slice_in_dim(inverse, seq_index * items, items)
    my_mem_len = jnp.take(mem_len, group * items_grp + mine)

    def exchange(sent):
        return lax.all_to_all(sent, "seq", split_axis=0, concat_axis=0, tiled=True)

    chain = Chain()
    by_item = inverse.reshape(seq_size, items)
    memories = []

    def gather(item):
        sent = chain.run(gather_items, memory, by_item[:, item])[0]
        memories.append(exchange(sent).reshape(mem_tokens, width))

    gather(0)

    def spread(gain):
        return jnp.repeat(gain, HD)

    vectors = [
        self_norm_gain, self_norm_shift, self_q_bias, self_v_bias, spread(self_head_gain),
        self_mix_gain, self_mix_shift, self_out_bias, cross_norm_gain, cross_norm_shift,
        cross_q_bias, cross_v_bias, spread(cross_head_gain), cross_mix_gain, cross_mix_shift,
        cross_out_bias, ffn_norm_gain, ffn_norm_shift, ffn_out_bias,
    ]
    vecs, wides = chain.run(prepare, vectors, [ffn_in_bias, ffn_mid_gain, ffn_mid_shift])
    bias = rel_bias_of(rel_bias_table, length)
    buckets = bucket_lanes(length, rel_bias_table.shape[0])

    starts = [
        chain.run(
            self_forward, item, dec_len, task_prefix, dec_in, bias, self_qkv, self_out, cross_q, vecs
        )
        for item in range(items)
    ]
    for item in range(1, items):
        gather(item)

    core, y = group % 2, group // 2
    x, z = seq_index % 2, seq_index // 2
    if paired:
        order = jnp.stack([(1 - y) * 2 + 1 - core, y * 2 + 1 - core, (1 - y) * 2 + core, y * 2 + core])
        places = jnp.sum(jnp.where(order[None, :] == jnp.arange(parts)[:, None], jnp.arange(parts)[None, :], 0), axis=1)
    else:
        order = places = jnp.arange(parts)
    order = jnp.concatenate([order, places]).astype(jnp.int32)

    bundles = dict(
        A=Bundle([ffn_out.shape], width, parts),
        C=Bundle([ffn_in.shape], width, parts),
        D=Bundle([cross_kv.shape], width, parts),
        G=Bundle([cross_out.shape, cross_q.shape, self_out.shape], width, parts),
        E=Bundle([(width, width)], width, parts, vectors=True),
        H=Bundle([(width, 2 * width)], width, parts),
    )
    ahead, behind, returned, ends, state, done = {}, {}, {}, {}, {}, {}

    def start_sums(result, names):
        for name in names:
            sent, kept = result[f"sent{name}"], result[f"kept{name}"]
            state[name] = (kept, lax.ppermute(sent, "grp", CORE_PAIRS)) if paired else (sent, kept)

    def forward(item, **how):
        ahead[item] = chain.run(
            cross_forward, item, ahead, order, my_mem_len, dec_len, starts[item].x2, starts[item].q2,
            memories[item], cotangent, cross_kv, cross_out, ffn_in, ffn_out, vecs, wides, **how,
        )
        if item == items - 1:
            start_sums(ahead[item], "AC")

    def backward(item, **how):
        behind[item] = chain.run(
            cross_back, item, items, behind, starts, ahead, order, cross_kv, cross_out, cross_q, vecs, **how
        )
        returned[item] = exchange(behind[item].gmem.reshape(seq_size, shard_tokens, width))
        if item == items - 1:
            start_sums(behind[item], "DG")

    def self_backward(**how):
        ends.update(
            chain.run(
                self_back, starts, ahead, behind, order, dec_in, self_qkv, self_out, vecs, buckets, **how
            )
        )
        start_sums(ends, "EH")

    def scatter_memory(**how):
        return chain.run(scatter_items, [returned[i] for i in range(items)], inverse, **how)[0]

    if paired:
        side, z_side = x.reshape(1), (z % 2).reshape(1)
        inner = ((z == 1) | (z == 2)).astype(jnp.int32).reshape(1)

        def reduce_step(name, step, **how):
            along_y = step == (1 if ROUTE[name][0] == "Y" else 2)
            if step == 1:
                sent, kept = chain.run(first_add, *state[name], side, not along_y, **how)
                axis, pairs = ("grp", Y_PAIRS) if along_y else ("seq", X_PAIRS)
            elif step == 2:
                if along_y:
                    sent, kept = chain.run(core_add, *state[name], **how)
                else:
                    sent, kept = chain.run(split_add, *state[name], side, **how)
                axis, pairs = ("grp", Y_PAIRS) if along_y else ("seq", X_PAIRS)
            elif step == 3 and ROUTE[name][1] == "H":
                sent, kept = chain.run(split_add, *state[name], z_side, **how)
                axis, pairs = "seq", Z_NEAR
            elif step in (4, 5) and ROUTE[name][1] == "H":
                sent = kept = chain.run(add, *state[name], **how)[0]
                axis, pairs = "seq", Z_FAR if step == 4 else Z_NEAR
            elif step == 6 and ROUTE[name][1] == "H":
                sent = kept = chain.run(join, *state[name], z_side, **how)[0]
                axis, pairs = "seq", X_PAIRS
            elif step in (3, 4, 5):
                sent = kept = chain.run(add, *state[name], **how)[0]
                axis, pairs = "seq", (Z_IN, Z_MID, Z_OUT)[step - 3]
            elif step == 6:
                sent = kept = chain.run(pick, *state[name], inner, **how)[0]
                axis, pairs = "seq", X_PAIRS
            else:
                names = "EH" if name == "E" else name
                done[name] = chain.run(
                    finish, [bundles[n] for n in names], [state[n] for n in names], side, **how
                )
                return
            state[name] = kept, lax.ppermute(sent, axis, pairs)

        for step, cost in STEPS:
            if step[0] == "F":
                forward(int(step[1]), cost=cost)
            elif step[0] == "B":
                backward(int(step[1]), cost=cost)
            elif step == "S":
                self_backward(cost=cost)
            elif step == "SC":
                grad_memory = scatter_memory(cost=cost)
            else:
                reduce_step(step[0], int(step[1]), cost=cost)
    else:
        for item in range(items):
            forward(item)
            backward(item)
        self_backward()
        none = jnp.zeros((1,), jnp.int32)
        for name in ROUTE:
            share = lax.psum_scatter(jnp.concatenate(state[name]), "grp", scatter_dimension=0, tiled=True)[0]
            state[name] = lax.psum(share, "seq"), None
        for names in ("A", "C", "D", "G", "EH"):
            done[names[0]] = chain.run(finish, [bundles[n] for n in names], [state[n] for n in names], none)
        grad_memory = scatter_memory()

    out, gx = ahead[items - 1].out, ends["gx"]
    g_ffn_out, g_ffn_in, g_cross_kv = (done[name][0] for name in ("A", "C", "D"))
    g_cross_out, g_cross_q, g_self_out = done["G"]
    g_self_qkv, vec = done["E"]
    (
        g_self_norm_gain, g_self_norm_shift, g_self_q_bias, g_self_v_bias, g_self_mix_gain,
        g_self_mix_shift, g_self_out_bias, g_cross_norm_gain, g_cross_norm_shift, g_cross_q_bias,
        g_cross_v_bias, g_cross_mix_gain, g_cross_mix_shift, g_cross_out_bias, g_ffn_norm_gain,
        g_ffn_norm_shift, g_ffn_out_bias, g_ffn_in_bias, g_ffn_mid_gain, g_ffn_mid_shift,
        g_self_head, g_cross_head, g_table,
    ) = chain.run(
        vector_outputs, vec, group.reshape(1), parts, ff, rel_bias_table.shape[0]
    )
    return (
        out,
        gx,
        grad_memory,
        g_self_norm_gain,
        g_self_norm_shift,
        g_self_qkv,
        g_self_q_bias,
        g_self_v_bias,
        g_table,
        g_self_head,
        g_self_mix_gain,
        g_self_mix_shift,
        g_self_out,
        g_self_out_bias,
        g_cross_norm_gain,
        g_cross_norm_shift,
        g_cross_q,
        g_cross_q_bias,
        g_cross_kv,
        g_cross_v_bias,
        g_cross_head,
        g_cross_mix_gain,
        g_cross_mix_shift,
        g_cross_out,
        g_cross_out_bias,
        g_ffn_norm_gain,
        g_ffn_norm_shift,
        g_ffn_in,
        g_ffn_in_bias,
        g_ffn_mid_gain,
        g_ffn_mid_shift,
        g_ffn_out,
        g_ffn_out_bias,
    )


def solution(mesh):
    rows = P(("seq", "grp"), None, None)
    matrix, vector = P("grp", None), P("grp")
    in_specs = (rows, P("grp", "seq", None), rows, P(("seq", "grp")), P(("seq", "grp"))) + (P(),) * 32
    out_specs = (
        rows, rows, P("grp", "seq", None),
        vector, vector, matrix, vector, vector, matrix, vector, vector, vector, matrix, vector,
        vector, vector, matrix, vector, matrix, vector, vector, vector, vector, matrix, vector,
        vector, vector, matrix, vector, vector, vector, matrix, vector,
    )
    return jax.shard_map(local, mesh=mesh, in_specs=in_specs, out_specs=out_specs, check_vma=False)
```

```python
import functools
import math

import jax
import jax.numpy as jnp
from jax import lax
from jax.experimental import pallas as pl
from jax.experimental.pallas import tpu as pltpu
from jax.sharding import PartitionSpec as P

H = 12
HD = 64
EPSILON = 1e-05
FACTOR = 1.0 / math.sqrt(HD)
MASKED = -1000000000.0
F32 = jnp.float32
BF16 = jnp.bfloat16
PAIR = 2 * HD
PAIRS = H // 2

(
    SELF_GAIN,
    SELF_SHIFT,
    SELF_QB,
    SELF_VB,
    SELF_HEAD,
    SELF_MIX_GAIN,
    SELF_MIX_SHIFT,
    SELF_OB,
    CROSS_GAIN,
    CROSS_SHIFT,
    CROSS_QB,
    CROSS_VB,
    CROSS_HEAD,
    CROSS_MIX_GAIN,
    CROSS_MIX_SHIFT,
    CROSS_OB,
    FFN_GAIN,
    FFN_SHIFT,
    FFN_OB,
) = range(19)
IN_BIAS, MID_GAIN, MID_SHIFT, TABLE = 20, 24, 28, 32
VEC_ROWS = 64


def dot(left, right):
    return jnp.dot(left, right, preferred_element_type=F32)


def dot_rows(left, right):
    return lax.dot_general(left, right, (((1,), (1,)), ((), ())), preferred_element_type=F32)


def dot_cols(left, right):
    return lax.dot_general(left, right, (((0,), (0,)), ((), ())), preferred_element_type=F32)


def normalize(values):
    average = jnp.mean(values, axis=-1, keepdims=True)
    centered = values - average
    spread = jnp.mean(centered * centered, axis=-1, keepdims=True)
    scale = lax.rsqrt(spread + EPSILON)
    return centered * scale, scale


def normalize_back(grad, normed, scale):
    mean_grad = jnp.mean(grad, axis=-1, keepdims=True)
    mean_both = jnp.mean(grad * normed, axis=-1, keepdims=True)
    return scale * (grad - mean_grad - normed * mean_both)


def total(values):
    return jnp.sum(values.astype(F32), axis=0, keepdims=True)


def lanes(start, size):
    return pl.ds(pl.multiple_of(start, 128), size)


def pick_head(values, half, axis):
    place = lax.broadcasted_iota(jnp.int32, values.shape, axis)
    inside = (place < HD) if half == 0 else (place >= HD)
    return jnp.where(inside, values, jnp.zeros_like(values))


def attend_pair(queries, keys, values, score_fn, e_ref, inv_ref, first):
    values_t = values.T
    ones = jnp.ones((16, values.shape[0]), BF16)
    scores = [score_fn(dot_rows(keys, pick_head(queries, half, 1)), first + half) for half in range(2)]
    parts = []
    for half in range(2):
        peak = jnp.max(scores[half], axis=0, keepdims=True)
        low = jnp.exp(scores[half] - peak).astype(BF16)
        e_ref[first + half] = low
        mixed = dot(jnp.concatenate([values_t[half * HD : (half + 1) * HD], ones], axis=0), low)
        inverse = 1.0 / mixed[HD : HD + 1]
        inv_ref[pl.ds(first + half, 1), :] = inverse
        parts.append(mixed[:HD] * inverse)
    return jnp.concatenate(parts, axis=0).T


def attend_pair_back(queries, keys, values, grad, prod, e_ref, inv_ref, first, keep_scores):
    keys_t = keys.T
    grad_t = grad.astype(F32).T
    prod_t = prod.T
    grads, deltas, grad_probs = [], [], []
    for half in range(2):
        rows = slice(half * HD, (half + 1) * HD)
        inverse = inv_ref[pl.ds(first + half, 1), :]
        deltas.append(jnp.sum(prod_t[rows], axis=0, keepdims=True) * inverse)
        grads.append(pick_head((grad_t * inverse).astype(BF16), half, 0))
        grad_probs.append(dot(values, grads[half]))
    lows = [e_ref[first + half] for half in range(2)]
    dv = dot_rows(jnp.concatenate(lows, axis=1), jnp.concatenate(grads, axis=1))
    scores = []
    for half in range(2):
        scores.append((lows[half].astype(F32) * (grad_probs[half] - deltas[half])).astype(BF16))
        if keep_scores is not None:
            keep_scores(scores[half], first + half)
    heads = jnp.concatenate([pick_head(queries, half, 1) for half in range(2)], axis=0)
    dk = dot(jnp.concatenate(scores, axis=1), heads)
    dq = [dot(keys_t[half * HD : (half + 1) * HD], scores[half]) for half in range(2)]
    return jnp.concatenate(dq, axis=0).T * FACTOR, dk, dv


class Gradients:
    def __init__(self, order_ref, sems, width):
        self.order_ref, self.sems, self.width = order_ref, sems, width
        self.parts = order_ref.shape[0] // 2
        self.used, self.copies = 0, []

    def load(self, far, near):
        copy = pltpu.make_async_copy(far, near, self.sems.at[self.used])
        copy.start()
        self.copies.append(copy)
        self.used += 1

    def load_left(self, far, near, item):
        size, depth = far.shape[0] // self.parts, far.shape[1]
        for j in range(self.parts):
            rows = pl.ds(pl.multiple_of(self.order_ref[j] * size, 16), size)
            self.load(far.at[rows, :], near.at[pl.ds(j * size, size), pl.ds(item * depth, depth)])

    def load_right(self, far, near, item):
        depth = far.shape[0]
        self.load(far, near.at[pl.ds(item * depth, depth), :])

    def wait(self):
        for copy in self.copies:
            copy.wait()
        self.copies = []

    def place(self, quarter, size):
        return pl.ds(pl.multiple_of(self.order_ref[self.parts + quarter] * size, 16), size)

    def put_left(self, value, near, item):
        size, depth = value.shape[0] // self.parts, value.shape[1]
        for quarter in range(self.parts):
            near[self.place(quarter, size), item * depth : (item + 1) * depth] = value[
                quarter * size : (quarter + 1) * size
            ]

    def put(self, outs, quarter, place, value):
        half = self.parts // 2
        outs[quarter // half][quarter % half, place, :] = value.astype(BF16)

    def store(self, io, name, row, size):
        rows = pl.ds(row, size)
        for side in ("sent", "kept"):
            near, far = io.near[side + name].at[:, rows, :], io.far[side + name].at[:, rows, :]
            copy = pltpu.make_async_copy(near, far, self.sems.at[self.used])
            copy.start()
            io.storing.append(copy)
            self.used += 1

    def sum(self, io, name, left, right, row):
        outs = io.near["sent" + name], io.near["kept" + name]
        size = left.shape[0] // self.parts
        span = min(left.shape[0], self.width)
        for column in range(right.shape[1] // self.width):
            cols = slice(column * self.width, (column + 1) * self.width)
            for top in range(0, left.shape[0], span):
                value = dot(left[top : top + span, :], right[:, cols])
                for quarter in range(top // size, (top + span - 1) // size + 1):
                    low, high = max(top, quarter * size), min(top + span, (quarter + 1) * size)
                    place = slice(row + low - quarter * size, row + high - quarter * size)
                    self.put(outs, quarter, place, value[low - top : high - top])
            self.store(io, name, row, size)
            row += size
        return row


def item_rows(ref, item, depth):
    return ref.at[pl.ds(item * depth, depth), :]


def self_forward_kernel(item, io, len_ref, prefix_ref, *_):
    io.load("x", "vecs", "qkv_w", "bias", "out_w", "q2_w")
    _, length, width = io.x.shape
    vec_ref = io.vecs

    def vec(row):
        return vec_ref[row : row + 1, :]

    io.need("x", "vecs")
    x = io.x[item].astype(F32)
    normed, _ = normalize(x)
    low = (normed * vec(SELF_GAIN) + vec(SELF_SHIFT)).astype(BF16)
    io.n1t[...] = low.T
    io.store("n1t")
    io.need("qkv_w")
    queries = dot(low, io.qkv_w[:, :width]) + vec(SELF_QB)
    io.qkv[:, :width] = queries.astype(BF16) * jnp.asarray(FACTOR, BF16)
    io.qkv[:, width : 2 * width] = dot(low, io.qkv_w[:, width : 2 * width]).astype(BF16)
    values = dot(low, io.qkv_w[:, 2 * width :]) + vec(SELF_VB)
    io.qkv[:, 2 * width :] = values.astype(BF16)
    io.store("qkv")
    key_pos = lax.broadcasted_iota(jnp.int32, (length, length), 0)
    query_pos = lax.broadcasted_iota(jnp.int32, (length, length), 1)
    allowed = (key_pos < len_ref[item]) & ((key_pos <= query_pos) | (key_pos < prefix_ref[item]))
    io.inv[...] = jnp.zeros_like(io.inv)
    io.need("bias")

    def scores_of(scores, head):
        row = jnp.broadcast_to(io.bias[pl.ds(head, 1), :], (length, 2 * length))
        bias = pltpu.roll(row, 0, 1, stride=1, stride_axis=0)[:, :length]
        return jnp.where(allowed, scores + bias, MASKED)

    def one_pair(pair, _):
        base = pair * PAIR
        io.mixed[:, lanes(base, PAIR)] = attend_pair(
            io.qkv[:, lanes(base, PAIR)],
            io.qkv[:, lanes(base + width, PAIR)],
            io.qkv[:, lanes(base + 2 * width, PAIR)],
            scores_of, io.e, io.inv, 2 * pair,
        )
        return 0

    lax.fori_loop(0, PAIRS, one_pair, 0, unroll=2)
    io.store("e", "inv", "mixed")
    normed, _ = normalize(io.mixed[...] * vec(SELF_HEAD))
    low = (normed * vec(SELF_MIX_GAIN) + vec(SELF_MIX_SHIFT)).astype(BF16)
    io.z1t[...] = low.T
    io.store("z1t")
    io.need("out_w")
    x2 = x + dot(low, io.out_w[...]) + vec(SELF_OB)
    io.x2[...] = x2
    io.store("x2")
    normed, _ = normalize(x2)
    low = (normed * vec(CROSS_GAIN) + vec(CROSS_SHIFT)).astype(BF16)
    io.n2t[...] = low.T
    io.need("q2_w")
    queries = dot(low, io.q2_w[...]) + vec(CROSS_QB)
    io.q2[...] = queries.astype(BF16) * jnp.asarray(FACTOR, BF16)
    io.store("n2t", "q2")


def gelu_parts(hidden):
    gate = 0.5 * (1.0 + lax.erf(hidden * math.sqrt(0.5)))
    slope = hidden * (jnp.exp(-0.5 * hidden * hidden) * (1.0 / math.sqrt(2.0 * math.pi)))
    return hidden * gate, gate + slope


def cross_forward_kernel(item, last, io, mem_len_ref, dec_len_ref, *refs):
    act_ref, grad_ref, slope_ref, mid_ref = refs[-4:]
    io.load("mem", "kv_w", "vecs")
    length, width = io.x2.shape
    mem_tokens = io.mem.shape[0]
    ff = io.in_w.shape[1]
    tiles = ff // width
    mem_ref, kv_ref, kv_w, vec_ref, wide_ref = io.mem, io.kv, io.kv_w, io.vecs, io.wides
    e_ref, inv_ref, mixed_ref, q2_ref, vg_ref = io.e, io.inv, io.mixed, io.q2, io.vg
    out_w, in_w, ffn_w = io.out_w, io.in_w, io.ffn_w
    if last:
        order_ref, left_out, right_out, left_in, right_in, sems = refs[:-4]
        grads = Gradients(order_ref, sems, width)
        hid_ref, cot_low_ref = item_rows(right_in, item, length), item_rows(right_out, item, length)
    else:
        hid_ref, cot_low_ref = io.hid, io.cot_low

    def vec(row):
        return vec_ref[row : row + 1, :]

    io.need("mem", "kv_w", "vecs")
    io.load("q2", "x2", "out_w", "in_w", "wides")
    io.load("cot", at=item)
    io.load("ffn_w")
    if last:
        for i in range(item):
            grads.load_left(io.far[f"midt{i}"], left_out, i)
            grads.load_right(io.far[f"cot_low{i}"], right_out, i)
            grads.load_left(io.far[f"n3t{i}"], left_in, i)
            grads.load_right(io.far[f"hid{i}"], right_in, i)
    io.memt[...] = mem_ref[...].T
    io.store("memt")
    kv_ref[:, :width] = dot(mem_ref[...], kv_w[:, :width]).astype(BF16)
    kv_ref[:, width:] = (dot(mem_ref[...], kv_w[:, width:]) + vec(CROSS_VB)).astype(BF16)
    io.store("kv")
    io.need("q2")
    mem_len = mem_len_ref[item]
    inv_ref[...] = jnp.zeros_like(inv_ref)

    def scores_of(scores, head):
        del head
        key_pos = lax.broadcasted_iota(jnp.int32, (mem_tokens, length), 0)
        return jnp.where(key_pos < mem_len, scores, MASKED)

    def one_pair(pair, _):
        base = pair * PAIR
        mixed_ref[:, lanes(base, PAIR)] = attend_pair(
            q2_ref[:, lanes(base, PAIR)],
            kv_ref[:, lanes(base, PAIR)],
            kv_ref[:, lanes(base + width, PAIR)],
            scores_of, e_ref, inv_ref, 2 * pair,
        )
        return 0

    lax.fori_loop(0, PAIRS, one_pair, 0, unroll=2)
    io.store("e", "inv", "mixed")
    normed, _ = normalize(mixed_ref[...] * vec(CROSS_HEAD))
    low = (normed * vec(CROSS_MIX_GAIN) + vec(CROSS_MIX_SHIFT)).astype(BF16)
    io.z2t[...] = low.T
    io.store("z2t")
    io.need("x2", "out_w")
    x3 = io.x2[...] + dot(low, out_w[...]) + vec(CROSS_OB)
    norm3, scale3 = normalize(x3)
    n3 = (norm3 * vec(FFN_GAIN) + vec(FFN_SHIFT)).astype(BF16)
    if last:
        grads.put_left(n3.T, left_in, item)
    else:
        io.n3t[...] = n3.T
        io.store("n3t")
    io.need("in_w", "wides")

    def hidden_tile(tile, sums):
        cols = lanes(tile * width, width)
        hidden = dot(n3, in_w[:, cols]) + wide_ref[0:1, cols]
        act, slope = gelu_parts(hidden)
        act_ref[:, cols] = act
        slope_ref[:, cols] = slope.astype(BF16)
        return sums + jnp.sum(act, axis=-1, keepdims=True)

    sums = lax.fori_loop(0, tiles, hidden_tile, jnp.zeros((length, 1), F32), unroll=True)
    average = sums / ff

    def spread_tile(tile, sums):
        centered = act_ref[:, lanes(tile * width, width)] - average
        return sums + jnp.sum(centered * centered, axis=-1, keepdims=True)

    sums = lax.fori_loop(0, tiles, spread_tile, jnp.zeros((length, 1), F32), unroll=True)
    scale = lax.rsqrt(sums / ff + EPSILON)

    def middle_tile(tile, _):
        cols = lanes(tile * width, width)
        normed = (act_ref[:, cols] - average) * scale
        act_ref[:, cols] = normed
        low = (normed * wide_ref[1:2, cols] + wide_ref[2:3, cols]).astype(BF16)
        mid_ref[:, cols] = low
        if last:
            left_out[grads.place(tile, width), item * length : (item + 1) * length] = low.T
        else:
            io.midt[pl.ds(pl.multiple_of(tile * width, 128), width), :] = low.T
        return 0

    lax.fori_loop(0, tiles, middle_tile, 0, unroll=True)
    if not last:
        io.store("midt")
    io.need("ffn_w", "cot")
    result = x3 + dot(mid_ref[...], ffn_w[...]) + vec(FFN_OB)
    io.out[...] = result.astype(BF16)
    io.store("out", at=item)

    valid = lax.broadcasted_iota(jnp.int32, (length, 1), 0) < dec_len_ref[item]
    cot = jnp.where(valid, io.cot[...].astype(F32), 0.0)
    cot_low_ref[...] = cot.astype(BF16)
    if not last:
        io.store("cot_low")
    vg_ref[...] = jnp.zeros_like(vg_ref)

    def grad_mid_tile(tile, sums):
        cols = lanes(tile * width, width)
        grad_mid = dot_rows(cot_low_ref[...], ffn_w[cols, :])
        normed = act_ref[:, cols]
        vg_ref[pl.ds(MID_GAIN + tile, 1), :] = total(grad_mid * normed)
        vg_ref[pl.ds(MID_SHIFT + tile, 1), :] = total(grad_mid)
        grad = grad_mid * wide_ref[1:2, cols]
        grad_ref[:, cols] = grad.astype(BF16)
        return (
            sums[0] + jnp.sum(grad, axis=-1, keepdims=True),
            sums[1] + jnp.sum(grad * normed, axis=-1, keepdims=True),
        )

    zero = jnp.zeros((length, 1), F32)
    sum_grad, sum_both = lax.fori_loop(0, tiles, grad_mid_tile, (zero, zero), unroll=True)
    mean_grad, mean_both = sum_grad / ff, sum_both / ff

    def hidden_back_tile(tile, _):
        cols = lanes(tile * width, width)
        grad = scale * (grad_ref[:, cols].astype(F32) - mean_grad - act_ref[:, cols] * mean_both)
        low = (grad * slope_ref[:, cols].astype(F32)).astype(BF16)
        hid_ref[:, cols] = low
        vg_ref[pl.ds(IN_BIAS + tile, 1), :] = total(low)
        return 0

    lax.fori_loop(0, tiles, hidden_back_tile, 0, unroll=True)
    if not last:
        io.store("hid")
    grad_n3 = dot_rows(hid_ref[...], in_w[...])
    vg_ref[FFN_GAIN : FFN_GAIN + 1, :] = total(grad_n3 * norm3)
    vg_ref[FFN_SHIFT : FFN_SHIFT + 1, :] = total(grad_n3)
    vg_ref[FFN_OB : FFN_OB + 1, :] = total(cot_low_ref[...])
    gx3 = normalize_back(grad_n3 * vec(FFN_GAIN), norm3, scale3) + cot
    io.gx3[...] = gx3
    io.branch[...] = gx3.astype(BF16)
    io.store("gx3", "branch")
    vg_ref[CROSS_OB : CROSS_OB + 1, :] = total(io.branch[...])
    io.store("vg")
    if last:
        grads.wait()
        grads.sum(io, "A", left_out, right_out, 0)
        grads.sum(io, "C", left_in, right_in, 0)


def cross_back_kernel(item, last, io, *refs):
    e_ref, _, grad_ref, prod_ref = refs[-4:]
    length, width = io.x2.shape
    mem_tokens = io.kv.shape[0]
    vec_ref, vg_ref = io.vecs, io.vg
    if last:
        order_ref, left_mem, right_mem, left_z, right_z, left_n, right_n, left_s, right_s, sems = refs[:-4]
        grads = Gradients(order_ref, sems, width)
        dkv_ref, dq_ref = item_rows(right_mem, item, mem_tokens), item_rows(right_n, item, length)
    else:
        dkv_ref, dq_ref = io.dkv, io.dq
    io.load("vecs", "mixed", "branch", "out_w", "q2", "inv", "kv")
    pair_sems = refs[-3]
    pair_copies = [
        pltpu.make_async_copy(io.far["e"].at[pl.ds(2 * p, 2)], e_ref.at[pl.ds(2 * p, 2)], pair_sems.at[p])
        for p in range(PAIRS)
    ]
    for copy in pair_copies:
        copy.start()

    def load_later():
        io.load("kv_w", "x2", "q2_w", "gx3")
        if not last:
            return
        for i in range(item + 1):
            grads.load_left(io.far[f"memt{i}"], left_mem, i)
            if i < item:
                grads.load_right(io.far[f"dkv{i}"], right_mem, i)
        for i in range(item + 1):
            grads.load_left(io.far[f"z2t{i}"], left_z, i)
            grads.load_left(io.far[f"n2t{i}"], left_n, i)
            grads.load_left(io.far[f"z1t{i}"], left_s, i)
            grads.load_right(io.far[f"branch{i}"], right_z, i)
            if i < item:
                grads.load_right(io.far[f"dq{i}"], right_n, i)
                grads.load_right(io.far[f"branch2{i}"], right_s, i)

    def vec(row):
        return vec_ref[row : row + 1, :]

    def put(row, value):
        vg_ref[row : row + 1, :] = value

    if not last:
        load_later()
    vg_ref[...] = jnp.zeros_like(vg_ref)
    io.need("vecs", "mixed")
    mixed = io.mixed[...]
    normed, scale = normalize(mixed * vec(CROSS_HEAD))
    io.need("branch", "out_w")
    grad = dot_rows(io.branch[...], io.out_w[...])
    put(CROSS_MIX_GAIN, total(grad * normed))
    put(CROSS_MIX_SHIFT, total(grad))
    grad = normalize_back(grad * vec(CROSS_MIX_GAIN), normed, scale)
    put(CROSS_HEAD, total(grad * mixed))
    grad = (grad * vec(CROSS_HEAD)).astype(BF16)
    grad_ref[...] = grad
    prod_ref[...] = grad.astype(F32) * mixed
    for pair in range(PAIRS):
        if pair == 0:
            io.need("q2", "inv", "kv")
        pair_copies[pair].wait()
        if pair == 1 and last:
            load_later()
        base = pair * PAIR
        cols = slice(base, base + PAIR)
        dq, dk, dv = attend_pair_back(
            io.q2[:, cols], io.kv[:, cols], io.kv[:, base + width : base + width + PAIR],
            grad_ref[:, cols], prod_ref[:, cols], e_ref, io.inv, 2 * pair, None,
        )
        dq_ref[:, cols] = dq.astype(BF16)
        dkv_ref[:, cols] = dk.astype(BF16)
        dkv_ref[:, base + width : base + width + PAIR] = dv.astype(BF16)

    if not last:
        io.store("dkv", "dq")
    put(CROSS_VB, total(dkv_ref[:, width:]))
    step = 256
    io.need("kv_w")

    def memory_tile(tile, _):
        cols = lanes(tile * step, step)
        io.gmem[:, cols] = dot_rows(dkv_ref[...], io.kv_w[cols, :]).astype(BF16)
        return 0

    lax.fori_loop(0, width // step, memory_tile, 0, unroll=True)
    io.store("gmem")
    put(CROSS_QB, total(dq_ref[...]))
    io.need("x2", "q2_w", "gx3")
    normed, scale = normalize(io.x2[...])
    grad = dot_rows(dq_ref[...], io.q2_w[...])
    put(CROSS_GAIN, total(grad * normed))
    put(CROSS_SHIFT, total(grad))
    gx2 = normalize_back(grad * vec(CROSS_GAIN), normed, scale) + io.gx3[...]
    io.gx2[...] = gx2
    io.branch2[...] = gx2.astype(BF16)
    io.store("gx2", "branch2")
    put(SELF_OB, total(io.branch2[...]))
    io.store("vg")
    if last:
        right_s[item * length : (item + 1) * length, :] = io.branch2[...]
        grads.wait()
        grads.sum(io, "D", left_mem, right_mem, 0)
        row = 0
        for left, right in ((left_z, right_z), (left_n, right_n), (left_s, right_s)):
            row = grads.sum(io, "G", left, right, row)


def self_back_kernel(items, io, order_ref, left, right, vg_refs, sems, grad_ref, prod_ref, diag_ref):
    _, length, width = io.x.shape
    shared = ("mixed", "branch", "qkv", "inv", "e")
    io.load("vecs", "mixed0", "branch0", "out_w", "qkv0", "inv0", "e0")
    grads = Gradients(order_ref, sems, width)

    def load_later():
        io.load("buckets", "x", "qkv_w", "gx20")
        for item in range(1, items):
            io.load(*[f"{name}{item}" for name in shared + ("gx2",)])
        for item in range(items):
            grads.load_left(io.far[f"n1t{item}"], left, item)
            for i, name in enumerate(("vgf", "vgb")):
                grads.load(io.far[f"{name}{item}"], vg_refs.at[2 * item + i])

    own = 2 * items
    for item in range(items):
        self_back_item(
            item, io, item_rows(right, item, length), vg_refs.at[own + item], grad_ref, prod_ref, diag_ref,
            load_later if item == 0 else None,
        )
    grads.wait()
    outs = (io.sentE, io.keptE)
    grads.sum(io, "H", left, right.at[:, pl.ds(width, 2 * width)], 0)
    row = grads.sum(io, "E", left, right.at[:, pl.ds(0, width)], 0)
    value = vg_refs[0]
    for i in range(1, 3 * items):
        value = value + vg_refs[i]
    for quarter in range(grads.parts):
        grads.put(outs, quarter, slice(row, row + VEC_ROWS), value)
    grads.store(io, "E", row, VEC_ROWS)


def self_back_item(item, io, dqkv_ref, vg_ref, grad_ref, prod_ref, diag_ref, load_later):
    _, length, width = io.x.shape
    vec_ref = io.vecs
    near = {name: io.near[f"{name}{item}"] for name in ("mixed", "branch", "qkv", "inv", "e", "gx2")}
    qkv_ref = near["qkv"]

    def vec(row):
        return vec_ref[row : row + 1, :]

    def put(row, value):
        vg_ref[row : row + 1, :] = value

    vg_ref[...] = jnp.zeros_like(vg_ref)
    diag_ref[...] = jnp.zeros_like(diag_ref)
    if item == 0:
        io.need("vecs")
    io.need(f"mixed{item}")
    mixed = near["mixed"][...]
    normed, scale = normalize(mixed * vec(SELF_HEAD))
    io.need(f"branch{item}")
    if item == 0:
        io.need("out_w")
    grad = dot_rows(near["branch"][...], io.out_w[...])
    put(SELF_MIX_GAIN, total(grad * normed))
    put(SELF_MIX_SHIFT, total(grad))
    grad = normalize_back(grad * vec(SELF_MIX_GAIN), normed, scale)
    put(SELF_HEAD, total(grad * mixed))
    grad = (grad * vec(SELF_HEAD)).astype(BF16)
    grad_ref[...] = grad
    prod_ref[...] = grad.astype(F32) * mixed
    io.need(f"qkv{item}", f"inv{item}", f"e{item}")
    if load_later is not None:
        load_later()
    backwards = (
        lax.broadcasted_iota(jnp.int32, (length, length), 0)
        + lax.broadcasted_iota(jnp.int32, (length, length), 1)
        == length - 1
    ).astype(F32).astype(BF16)

    def keep_scores(scores, head):
        flipped = dot(backwards, scores)
        padded = jnp.concatenate([flipped, jnp.zeros_like(flipped)], axis=1)
        rolled = pltpu.roll(padded, 0, 1, stride=1, stride_axis=0)
        diag_ref[pl.ds(head, 1), :] = jnp.sum(rolled, axis=0, keepdims=True)

    def one_pair(pair, _):
        base = pair * PAIR
        cols = lanes(base, PAIR)
        dq, dk, dv = attend_pair_back(
            qkv_ref[:, cols], qkv_ref[:, lanes(base + width, PAIR)],
            qkv_ref[:, lanes(base + 2 * width, PAIR)],
            grad_ref[:, cols], prod_ref[:, cols], near["e"], near["inv"], 2 * pair, keep_scores,
        )
        dqkv_ref[:, cols] = dq.astype(BF16)
        dqkv_ref[:, lanes(base + width, PAIR)] = dk.astype(BF16)
        dqkv_ref[:, lanes(base + 2 * width, PAIR)] = dv.astype(BF16)
        return 0

    lax.fori_loop(0, PAIRS, one_pair, 0, unroll=2)
    if item == 0:
        io.need("buckets", "x", "qkv_w")
    table = jnp.dot(
        diag_ref[...], io.buckets[...], precision=lax.Precision.HIGHEST, preferred_element_type=F32
    )
    vg_ref[TABLE : TABLE + 16, : table.shape[1]] = table
    put(SELF_QB, total(dqkv_ref[:, :width]))
    put(SELF_VB, total(dqkv_ref[:, 2 * width :]))
    normed, scale = normalize(io.x[item].astype(F32))
    grad = dot_rows(dqkv_ref[...], io.qkv_w[...])
    put(SELF_GAIN, total(grad * normed))
    put(SELF_SHIFT, total(grad))
    io.need(f"gx2{item}")
    gx = normalize_back(grad * vec(SELF_GAIN), normed, scale) + near["gx2"][...]
    io.gx[item] = gx.astype(BF16)
    if item == io.gx.shape[0] - 1:
        io.store("gx")


SMEM = pl.BlockSpec(memory_space=pltpu.SMEM)
VMEM = pl.BlockSpec(memory_space=pltpu.VMEM)
ANY = pl.BlockSpec(memory_space=pl.ANY)
HBM = pl.BlockSpec(memory_space=pltpu.HBM)
MIB = 1024 * 1024


COST = dict(
    self_forward=11, cross_forward=28, cross_back=18, self_back=10, weight_grads=5, finish=2, split_add=1, core_add=1, first_add=2, join=1,
    gather_items=3, scatter_items=4, add=1, pick=1, vectors=1,
)
COST_SCALE = 3_000_000


class Kept:
    def __init__(self, shape, dtype):
        self.shape, self.dtype = tuple(shape), dtype


class Stored(Kept):
    pass


class Token:
    def __init__(self, array, near):
        self.space = pltpu.VMEM if near else pltpu.HBM
        self.spec = VMEM if near else HBM
        self.array = array

    def operand(self):
        return pltpu.with_memory_space_constraint(self.array, self.space)


def token_args(after):
    return [t.spec for t in after], [t.operand() for t in after]


def call(kernel, name, ins, outs, scratch=(), after=(), limit=16, scalars=(), far=()):
    after_specs, after_args = token_args(after)
    first = len(scalars) + len(far) + len(ins)
    last = first + len(after)

    def body(*refs):
        kernel(*refs[:first], *refs[last:])

    ins = [pltpu.with_memory_space_constraint(a, pltpu.VMEM) for a in ins]
    far = [pltpu.with_memory_space_constraint(a, pltpu.HBM) for a in far]
    shapes = [(pltpu.HBM if isinstance(o, Stored) else pltpu.VMEM)(o.shape, o.dtype) for o in outs]
    Chain.token = 0, not isinstance(outs[0], Stored)
    return pl.pallas_call(
        body,
        out_shape=shapes,
        in_specs=[SMEM] * len(scalars) + [HBM] * len(far) + [VMEM] * len(ins) + after_specs,
        out_specs=[VMEM] * len(shapes),
        scratch_shapes=list(scratch),
        compiler_params=pltpu.CompilerParams(vmem_limit_bytes=limit * MIB),
        cost_estimate=cost_of(name),
        name=name,
    )(*scalars, *far, *ins, *after_args)


class Stream:
    def __init__(self, ins, outs, far, near, sems):
        self.names = list(ins) + list(outs)
        self.far, self.near = dict(zip(self.names, far)), dict(zip(self.names, near))
        self.sems = dict(zip(self.names, range(len(self.names))))
        self.sem_refs = sems
        self.loading, self.storing = {}, []

    def __getattr__(self, name):
        return self.near[name]

    def load(self, *names, at=None):
        for name in names:
            far = self.far[name] if at is None else self.far[name].at[at]
            copy = pltpu.make_async_copy(far, self.near[name], self.sem_refs.at[self.sems[name]])
            copy.start()
            self.loading[name] = copy

    def need(self, *names):
        for name in names:
            self.loading.pop(name).wait()

    def store(self, *names, at=None):
        for name in names:
            far = self.far[name] if at is None else self.far[name].at[at]
            copy = pltpu.make_async_copy(self.near[name], far, self.sem_refs.at[self.sems[name]])
            copy.start()
            self.storing.append(copy)

    def drain(self):
        assert not self.loading
        for copy in self.storing:
            copy.wait()


def stream_call(kernel, name, ins, outs, scratch=(), after=(), scalars=(), limit=16, kept=(), free=(), token="vg", gathered={}, far=None, parted=()):
    far = far or {}
    after_specs, after_args = token_args(after)
    n_in, n_out = len(ins), len(outs)
    far_outs = [n for n in outs if n not in kept]

    def body(*refs):
        refs = list(refs)

        def take(count):
            taken, refs[:] = refs[:count], refs[count:]
            return taken

        scalar_refs, far_in = take(len(scalars)), take(n_in)
        far_only = dict(zip(far, take(len(far))))
        take(len(after) + len(filled))
        out_refs = dict(zip(outs, take(n_out)))
        near_in = take(n_in)
        near_out = dict(zip(far_outs, take(len(far_outs))))
        sems = refs.pop()
        near_out.update({n: out_refs[n] for n in kept})
        io = Stream(
            ins, outs, far_in + [out_refs[n] for n in outs], near_in + [near_out[n] for n in outs], sems
        )
        io.far.update(far_only)
        kernel(io, *scalar_refs, *refs)
        io.drain()

    filled = {n: array for n, (_, array) in gathered.items() if array is not None}
    before = len(scalars) + n_in + len(far) + len(after)
    aliases = {before + i: list(outs).index(n) for i, n in enumerate(filled)}
    shapes = [
        pltpu.VMEM(s, d) if n in kept else pltpu.HBM((gathered[n][0],) + s if n in gathered else s, d)
        for n, (s, d) in outs.items()
    ]
    buffers = [pltpu.VMEM(a.shape[1:] if n in parted else a.shape, a.dtype) for n, a in ins.items()]
    buffers += [pltpu.VMEM(*outs[n]) for n in far_outs]
    results = pl.pallas_call(
        body,
        out_shape=shapes,
        in_specs=[SMEM] * len(scalars)
        + [ANY if n in free else HBM for n in ins]
        + [HBM] * len(far)
        + after_specs
        + [HBM] * len(filled),
        input_output_aliases=aliases,
        out_specs=[VMEM if n in kept else HBM for n in outs],
        scratch_shapes=buffers + list(scratch) + [pltpu.SemaphoreType.DMA((n_in + n_out,))],
        compiler_params=pltpu.CompilerParams(vmem_limit_bytes=limit * MIB),
        cost_estimate=cost_of(name),
        name=name,
    )(
        *scalars,
        *[a if n in free else pltpu.with_memory_space_constraint(a, pltpu.HBM) for n, a in ins.items()],
        *[pltpu.with_memory_space_constraint(a, pltpu.HBM) for a in far.values()],
        *after_args,
        *filled.values(),
    )
    Chain.token = list(outs).index(token), token in kept
    return Result(zip(outs, results))


class Result(dict):
    def __getattr__(self, name):
        return self[name]


def self_forward(item, dec_len, prefix, mem_len, order, x, bias, qkv_w, out_w, q2_w, vecs, after):
    _, length, width = x.shape
    outs = {
        "n1t": ((width, length), BF16),
        "qkv": ((length, 3 * width), BF16),
        "e": ((H, length, length), BF16),
        "inv": ((16, length), F32),
        "mixed": ((length, width), F32),
        "z1t": ((width, length), BF16),
        "x2": ((length, width), F32),
        "n2t": ((width, length), BF16),
        "q2": ((length, width), BF16),
    }
    ins = dict(x=x, bias=bias, qkv_w=qkv_w, out_w=out_w, q2_w=q2_w, vecs=vecs)
    return stream_call(
        functools.partial(self_forward_kernel, item), "self_forward", ins, outs, after=after,
        scalars=(dec_len, prefix, mem_len, order), limit=40, token="inv",
    )


def sums_of(names, rows, parts, width):
    outs = {}
    for name, count in zip(names, rows):
        outs.update({f"{side}{name}": ((parts // 2, count, width), BF16) for side in ("sent", "kept")})
    return outs


def operand_pair(rows, depth, columns):
    return [pltpu.VMEM((rows, depth), BF16), pltpu.VMEM((depth, columns), BF16)]


def cross_forward(item, earlier, order, mem_len, dec_len, x2, q2, mem, cot, kv_w, out_w, in_w, ffn_w, vecs, wides, after):
    length, width = x2.shape
    items = cot.shape[0]
    last = item == items - 1
    mem_tokens = mem.shape[0]
    ff = in_w.shape[1]
    parts = order.shape[0] // 2
    outs = {
        "out": ((length, width), BF16),
        "kv": ((mem_tokens, 2 * width), BF16),
        "e": ((H, mem_tokens, length), BF16),
        "inv": ((16, length), F32),
        "mixed": ((length, width), F32),
        "memt": ((width, mem_tokens), BF16),
        "z2t": ((width, length), BF16),
        "gx3": ((length, width), F32),
        "branch": ((length, width), BF16),
        "vg": ((VEC_ROWS, width), F32),
    }
    operands = {
        "n3t": ((width, length), BF16),
        "hid": ((length, ff), BF16),
        "midt": ((ff, length), BF16),
        "cot_low": ((length, width), BF16),
    }
    ins = dict(
        x2=x2, q2=q2, mem=mem, cot=cot, kv_w=kv_w, out_w=out_w, in_w=in_w, ffn_w=ffn_w, vecs=vecs, wides=wides
    )
    scratch = [pltpu.VMEM((length, ff), F32)] + [pltpu.VMEM((length, ff), BF16)] * 3
    scalars, far, sums = (mem_len, dec_len), {}, {}
    if last:
        sums = sums_of("AC", (ff // parts, ff // parts), parts, width)
        outs.update(sums)
        scalars += (order,)
        far = {f"{n}{i}": earlier[i][n] for i in range(item) for n in operands}
        scratch = (
            operand_pair(ff, items * length, width)
            + operand_pair(width, items * length, ff)
            + [pltpu.SemaphoreType.DMA((item * (2 * parts + 2) + 2 * (1 + ff // width),))]
            + scratch
        )
    else:
        outs.update(operands)
    return stream_call(
        functools.partial(cross_forward_kernel, item, last), "cross_forward", ins, outs,
        scratch=scratch, after=after, scalars=scalars, limit=58 if last else 50, free=("mem",),
        gathered=dict(out=(items, earlier[item - 1].out if item else None)), far=far, parted=("cot",),
    )


def cross_back(item, items, earlier, starts, ahead, order, kv_w, out_w, q2_w, vecs, after):
    a, x2, q2 = ahead[item], starts[item].x2, starts[item].q2
    last = item == items - 1
    length, width = x2.shape
    mem_tokens = a.kv.shape[0]
    parts = order.shape[0] // 2
    outs = {
        "gmem": ((mem_tokens, width), BF16),
        "gx2": ((length, width), F32),
        "branch2": ((length, width), BF16),
        "vg": ((VEC_ROWS, width), F32),
    }
    operands = {"dq": ((length, width), BF16), "dkv": ((mem_tokens, 2 * width), BF16)}
    ins = dict(
        branch=a.branch, gx3=a.gx3, mixed=a.mixed, kv=a.kv, inv=a.inv, q2=q2, x2=x2,
        kv_w=kv_w, out_w=out_w, q2_w=q2_w, vecs=vecs,
    )
    scratch = [
        pltpu.VMEM(a.e.shape, a.e.dtype),
        pltpu.SemaphoreType.DMA((PAIRS,)),
        pltpu.VMEM((length, width), BF16),
        pltpu.VMEM((length, width), F32),
    ]
    scalars, far, sums = (), dict(e=a.e), {}
    if last:
        quarter = width // parts
        sums = sums_of("DG", (2 * quarter, 3 * quarter), parts, width)
        outs.update(sums)
        scalars = (order,)
        for i in range(items):
            far.update({f"memt{i}": ahead[i].memt, f"z2t{i}": ahead[i].z2t, f"branch{i}": ahead[i].branch})
            far.update({f"n2t{i}": starts[i].n2t, f"z1t{i}": starts[i].z1t})
            if i < item:
                b = earlier[i]
                far.update({f"dkv{i}": b.dkv, f"dq{i}": b.dq, f"branch2{i}": b.branch2})
        scratch = (
            operand_pair(width, items * mem_tokens, 2 * width)
            + operand_pair(width, items * length, width) * 3
            + [pltpu.SemaphoreType.DMA((items * (4 * parts + 1) + item * 3 + 2 * 5,))]
            + scratch
        )
    else:
        outs.update(operands)
    return stream_call(
        functools.partial(cross_back_kernel, item, last), "cross_back", ins, outs, scratch=scratch, after=after,
        scalars=scalars, limit=50 if last else 34, far=far,
    )


def self_back(starts, ahead, behind, order, x, qkv_w, out_w, vecs, buckets, after):
    items, length, width = x.shape
    parts = order.shape[0] // 2
    ins = dict(x=x, qkv_w=qkv_w, out_w=out_w, vecs=vecs, buckets=buckets)
    far = {}
    for item in range(items):
        a, b = starts[item], behind[item]
        ins.update({f"{name}{item}": a[name] for name in ("mixed", "qkv", "e", "inv")})
        ins.update({f"branch{item}": b.branch2, f"gx2{item}": b.gx2})
        far.update({f"n1t{item}": a.n1t, f"vgf{item}": ahead[item].vg, f"vgb{item}": b.vg})
    sums = sums_of("EH", (width // parts + VEC_ROWS, 2 * width // parts), parts, width)
    outs = {"gx": (x.shape, BF16), **sums}
    scratch = operand_pair(width, items * length, 3 * width) + [
        pltpu.VMEM((3 * items, VEC_ROWS, width), F32),
        pltpu.SemaphoreType.DMA((items * (parts + 2) + 2 * 4,)),
        pltpu.VMEM((length, width), BF16),
        pltpu.VMEM((length, width), F32),
        pltpu.VMEM((16, 2 * length), F32),
    ]
    return stream_call(
        functools.partial(self_back_kernel, items), "self_back", ins, outs, scratch=scratch, after=after,
        scalars=(order,), limit=40, far=far, token="keptE",
    )


def prepare_kernel(narrow, wide, *refs):
    ins, (vec_ref, wide_ref) = refs[: narrow + wide], refs[narrow + wide :]
    vec_ref[...] = jnp.zeros_like(vec_ref)
    wide_ref[...] = jnp.zeros_like(wide_ref)
    for row in range(narrow):
        vec_ref[row, :] = ins[row][...].astype(F32)
    for row in range(wide):
        wide_ref[row, :] = ins[narrow + row][...].astype(F32)


def prepare(vectors, wides, after):
    count = len(vectors) + len(wides)
    shapes = [
        pltpu.HBM((24, vectors[0].shape[0]), F32), pltpu.HBM((8, wides[0].shape[0]), F32)
    ]

    after_specs, after_args = token_args(after)

    def body(*refs):
        prepare_kernel(len(vectors), len(wides), *refs[:count], *refs[count + len(after) :])

    Chain.token = 0, False
    return pl.pallas_call(
        body, out_shape=shapes, in_specs=[VMEM] * count + after_specs, out_specs=[VMEM] * 2,
        name="prepare",
    )(*vectors, *wides, *after_args)


def rel_bias_rows(table, length):
    count, heads = table.shape
    place = jnp.arange(2 * length, dtype=jnp.int32)
    offset = jnp.where(place < length, -place, 2 * length - place)
    bucket = jnp.clip(offset, -(count // 2), count // 2 - 1) + count // 2
    one_hot = (jnp.arange(count, dtype=jnp.int32)[:, None] == bucket[None, :]).astype(F32)
    rows = jnp.dot(table.T.astype(F32), one_hot, precision=lax.Precision.HIGHEST)
    return jnp.pad(rows, ((0, 16 - heads), (0, 0)))


def bucket_lanes(length, count):
    offset = length - 1 - jnp.arange(2 * length, dtype=jnp.int32)
    bucket = jnp.clip(offset, -(count // 2), count // 2 - 1) + count // 2
    return (bucket[:, None] == jnp.arange(128, dtype=jnp.int32)[None, :]).astype(F32)


def gather_kernel(slots_ref, memory_ref, out_ref, sems):
    copies = [
        pltpu.make_async_copy(memory_ref.at[slots_ref[i]], out_ref.at[i], sems.at[i])
        for i in range(out_ref.shape[0])
    ]
    for copy in copies:
        copy.start()
    for copy in copies:
        copy.wait()


def gather_items(memory, slots, after):
    count = slots.shape[0]
    return call(
        gather_kernel, "gather_items", (), [Stored((count,) + memory.shape[1:], memory.dtype)],
        scratch=[pltpu.SemaphoreType.DMA((count,))], after=after, scalars=(slots,), far=(memory,), limit=8,
    )


def scatter_kernel(items, slots_ref, *refs):
    parts, out_ref, sems = refs[:items], refs[items], refs[items + 1]
    copies = []
    for p in range(parts[0].shape[0]):
        for j in range(items):
            i = p * items + j
            copies.append(pltpu.make_async_copy(parts[j].at[p], out_ref.at[slots_ref[i]], sems.at[i]))
    for copy in copies:
        copy.start()
    for copy in copies:
        copy.wait()


def scatter_items(parts, slots, after):
    count = slots.shape[0]
    return call(
        functools.partial(scatter_kernel, len(parts)), "scatter_items", (),
        [Stored((count,) + parts[0].shape[1:], parts[0].dtype)],
        scratch=[pltpu.SemaphoreType.DMA((count,))], after=after, scalars=(slots,), far=tuple(parts), limit=8,
    )


class Bundle:
    def __init__(self, shapes, width, parts, vectors=False):
        self.shapes, self.width, self.parts, self.vectors = shapes, width, parts, vectors
        self.blocks = []
        row = 0
        for index, (rows, columns) in enumerate(shapes):
            size = rows // parts
            for column in range(columns // width):
                self.blocks.append((index, column, row, size))
                row += size
        self.vector_row = row
        self.rows = row + (VEC_ROWS if vectors else 0)

    def halves(self, mine_ref, got_ref, own_side):
        half = mine_ref.shape[0]

        def rows_of(start, size):
            pieces = []
            while size:
                part = start // half
                take = min(size, (part + 1) * half - start)
                rows = slice(start - part * half, start - part * half + take)
                value = mine_ref[rows, :].astype(F32)
                if own_side is not None:
                    value = jnp.where(own_side == part, value, got_ref[rows, :].astype(F32))
                pieces.append(value)
                start, size = start + take, size - take
            return pieces

        return rows_of


def finish_kernel(bundles, columns, place_ref, *refs):
    number = len(bundles)
    pairs, outs = refs[: 2 * number], refs[2 * number :]
    vec_ref = outs[-1]
    outs = list(outs)

    def store(out_ref, pieces, cols):
        done = 0
        for piece in pieces:
            out_ref[done : done + piece.shape[0], cols] = piece
            done += piece.shape[0]

    for b, bundle in enumerate(bundles):
        mine_ref, got_ref = pairs[2 * b], pairs[2 * b + 1]
        whole_rows = mine_ref.shape[0] == bundle.rows
        rows_of = bundle.halves(mine_ref, got_ref, None if whole_rows else place_ref[0])
        for index, column, row, size in bundle.blocks:
            first = columns[b] + column * bundle.width
            out_ref = outs[index]
            store(out_ref, rows_of(row, size), slice(first, first + bundle.width))
        if bundle.vectors:
            store(vec_ref, rows_of(bundle.vector_row, VEC_ROWS), slice(None))


def finish(bundles, sums, place, after):
    first = bundles[0]
    if len(bundles) == 1:
        shapes, columns = first.shapes, [0]
    else:
        widths = [bundle.shapes[0][1] for bundle in bundles]
        shapes = [(first.shapes[0][0], sum(widths))]
        columns = [sum(widths[:b]) for b in range(len(bundles))]
    outs = [Stored((rows // first.parts, cols), F32) for rows, cols in shapes]
    if any(bundle.vectors for bundle in bundles):
        outs.append(Kept((VEC_ROWS, first.width), F32))
    ins = []
    for mine, got in sums:
        ins += [mine, mine if got is None else got]
    return call(
        functools.partial(finish_kernel, bundles, columns), "finish", tuple(ins), outs,
        after=after, scalars=(place,), limit=12,
    )


def add_low(left, right):
    return left + right


def first_add_kernel(split, side_ref, left_ref, right_ref, *refs):
    refs = refs[-5:]
    sent_ref, kept_ref, near_left, near_right, sems = refs
    rows = near_left.shape[1]
    half = rows // 2
    copies = []
    for quarter in range(2):
        for part in range(2):
            place = pl.ds(part * half, half)
            if split:
                place = pl.ds(pl.multiple_of((part ^ 1 ^ side_ref[0]) * half, 16), half)
            for far, near in ((left_ref, near_left), (right_ref, near_right)):
                copies.append(
                    pltpu.make_async_copy(
                        far.at[quarter, place, :], near.at[quarter, pl.ds(part * half, half), :],
                        sems.at[len(copies)],
                    )
                )
    for copy in copies:
        copy.start()
    for quarter in range(2):
        for part in range(2):
            for copy in copies[:2]:
                copy.wait()
            copies = copies[2:]
            rows = slice(part * half, (part + 1) * half)
            value = add_low(near_left[quarter, rows, :], near_right[quarter, rows, :])
            if split:
                (sent_ref, kept_ref)[part][quarter] = value
            else:
                (sent_ref, kept_ref)[quarter][rows, :] = value


def first_add(left, right, side, split, after):
    shape = (2, left.shape[1] // 2, left.shape[2]) if split else left.shape[1:]
    after_specs, after_args = token_args(after)
    Chain.token = 1, True
    return pl.pallas_call(
        functools.partial(first_add_kernel, split),
        out_shape=[pltpu.VMEM(shape, BF16)] * 2,
        in_specs=[SMEM, HBM, ANY] + after_specs,
        out_specs=[VMEM] * 2,
        scratch_shapes=[pltpu.VMEM(left.shape, BF16)] * 2 + [pltpu.SemaphoreType.DMA((8,))],
        compiler_params=pltpu.CompilerParams(vmem_limit_bytes=10 * MIB),
        cost_estimate=cost_of("first_add"),
        name="first_add",
    )(side, pltpu.with_memory_space_constraint(left, pltpu.HBM), right, *after_args)


def core_add_kernel(left_ref, right_ref, sent_ref, kept_ref):
    sent_ref[...] = add_low(left_ref[0], right_ref[0])
    kept_ref[...] = add_low(left_ref[1], right_ref[1])


def core_add(left, right, after):
    shape = left.shape[1:]
    return call(core_add_kernel, "core_add", (left, right), [Kept(shape, BF16)] * 2, after=after, limit=8)


def split_add_kernel(side_ref, left_ref, right_ref, sent_ref, kept_ref):
    half = sent_ref.shape[0]
    mine = pl.ds(pl.multiple_of(side_ref[0] * half, 16), half)
    other = pl.ds(pl.multiple_of((1 - side_ref[0]) * half, 16), half)
    sent_ref[...] = add_low(left_ref[other, :], right_ref[other, :])
    kept_ref[...] = add_low(left_ref[mine, :], right_ref[mine, :])


def split_add(left, right, side, after):
    shape = (left.shape[0] // 2, left.shape[1])
    return call(
        split_add_kernel, "split_add", (left, right), [Kept(shape, BF16)] * 2,
        after=after, scalars=(side,), limit=8,
    )


def join_kernel(side_ref, mine_ref, got_ref, out_ref):
    half = mine_ref.shape[0]
    mine = pl.ds(pl.multiple_of(side_ref[0] * half, 16), half)
    other = pl.ds(pl.multiple_of((1 - side_ref[0]) * half, 16), half)
    out_ref[mine, :] = mine_ref[...]
    out_ref[other, :] = got_ref[...]


def join(mine, got, side, after):
    shape = (2 * mine.shape[0], mine.shape[1])
    return call(
        join_kernel, "join", (mine, got), [Kept(shape, BF16)], after=after, scalars=(side,), limit=4
    )


def add_kernel(left_ref, right_ref, out_ref):
    out_ref[...] = add_low(left_ref[...], right_ref[...])


def add(left, right, after):
    return call(add_kernel, "add", (left, right), [Kept(left.shape, BF16)], after=after, limit=4)


def pick_kernel(own_ref, mine_ref, got_ref, out_ref):
    @pl.when(own_ref[0] == 1)
    def _():
        out_ref[...] = mine_ref[...]

    @pl.when(own_ref[0] != 1)
    def _():
        out_ref[...] = got_ref[...]


def pick(mine, got, own, after):
    return call(
        pick_kernel, "pick", (mine, got), [Kept(mine.shape, BF16)], after=after, scalars=(own,), limit=4
    )


def vectors_kernel(parts, group_ref, vec_ref, *refs):
    outs, scratch = refs[:-1], refs[-1]
    group = group_ref[0]
    width = vec_ref.shape[1]
    size = width // parts
    values = vec_ref[...]
    rolled = pltpu.roll(values, lax.rem(width - size * group, width), 1)
    narrow = [row for row in range(FFN_OB + 1) if row not in (SELF_HEAD, CROSS_HEAD)]
    for out, row in zip(outs, narrow):
        out[...] = rolled[row, :size]
    outs = outs[len(narrow) :]
    tiles = outs[0].shape[0] * parts // width
    for out, row in zip(outs, (IN_BIAS, MID_GAIN, MID_SHIFT)):
        if tiles == parts:
            out[...] = vec_ref[pl.ds(row + group, 1), :][0]
    heads = H // parts
    lane = lax.broadcasted_iota(jnp.int32, (width, 128), 0) // HD
    one_hot = (lane == lax.broadcasted_iota(jnp.int32, (width, 128), 1)).astype(F32)
    sums = jnp.dot(values, one_hot, precision=lax.Precision.HIGHEST, preferred_element_type=F32)
    sums = pltpu.roll(sums, lax.rem(128 - heads * group, 128), 1)
    outs[3][...] = sums[SELF_HEAD, :heads]
    outs[4][...] = sums[CROSS_HEAD, :heads]
    scratch[...] = values[TABLE : TABLE + 16, :128].T
    buckets = outs[5].shape[0]
    outs[5][...] = scratch[pl.ds(pl.multiple_of(buckets * group, buckets), buckets), :][:, :H]


def vector_outputs(vec, group, parts, ff, buckets, after):
    width = vec.shape[1]
    outs = [Stored((width // parts,), F32)] * 17 + [Stored((ff // parts,), F32)] * 3
    outs += [Stored((H // parts,), F32)] * 2 + [Stored((buckets // parts, H), F32)]
    return call(
        functools.partial(vectors_kernel, parts), "vectors", (vec,), outs,
        scratch=[pltpu.VMEM((128, 16), F32)], after=after, scalars=(group,), limit=8,
    )


CORE_PAIRS = [(0, 1), (1, 0), (2, 3), (3, 2)]
Y_PAIRS = [(0, 2), (2, 0), (1, 3), (3, 1)]
X_PAIRS = [(0, 1), (1, 0), (2, 3), (3, 2), (4, 5), (5, 4), (6, 7), (7, 6)]
Z_IN = [(0, 2), (1, 3), (6, 4), (7, 5)]
Z_MID = [(2, 4), (4, 2), (3, 5), (5, 3)]
Z_OUT = [(2, 0), (3, 1), (4, 6), (5, 7)]
Z_NEAR = [(0, 2), (2, 0), (1, 3), (3, 1), (4, 6), (6, 4), (5, 7), (7, 5)]
Z_FAR = [(0, 4), (4, 0), (1, 5), (5, 1), (2, 6), (6, 2), (3, 7), (7, 3)]


ROUTE = dict(A="YH", C="XH", D="XH", G="YH", E="XH", H="YH")
STEPS = [
    ("F0", 30), ("B0", 30), ("F1", 0), ("A1", 3), ("C1", 0), ("B1", 13), ("A2", 2), ("C2", 20), ("S", 5),
    ("C3", 1), ("G1", 2), ("D1", 1), ("A3", 3), ("C4", 1), ("SC", 5), ("E1", 0.2), ("A4", 1), ("H1", 0.5),
    ("D2", 1), ("G2", 1), ("C5", 3), ("E2", 3), ("H2", 0), ("G3", 0), ("A5", 1), ("E3", 0.5), ("C6", 0),
    ("G4", 1), ("H3", 2), ("A6", 0.2), ("D3", 0.5), ("D4", 0), ("G5", 0.5), ("H4", 0), ("C7", 1), ("D5", 1),
    ("G6", 1), ("E4", 0.2), ("A7", 1), ("H5", 2), ("D6", 0.2), ("E5", 3), ("G7", 0.5), ("H6", 1), ("D7", 0.2),
    ("E6", 0), ("E7", 0),
]


class Chain:
    def __init__(self):
        self.last = ()

    def run(self, function, *args, also=(), cost=None):
        Chain.cost = cost
        result = function(*args, after=self.last + tuple(also))
        Chain.cost = None
        index, near = Chain.token
        arrays = Chain.flat(result)
        self.last = (Token(arrays[index], near),)
        return result

    @staticmethod
    def flat(result):
        return jax.tree.leaves(list(result.values()) if isinstance(result, dict) else result)

    cost = None
    token = None


def cost_of(name):
    us = COST.get(name, 1) if Chain.cost is None else Chain.cost
    return pl.CostEstimate(flops=int(us * 1_000_000_000), bytes_accessed=1000, transcendentals=0)


def local(
    dec_in,
    memory,
    cotangent,
    dec_len,
    task_prefix,
    owner,
    mem_len,
    self_norm_gain,
    self_norm_shift,
    self_qkv,
    self_q_bias,
    self_v_bias,
    rel_bias_table,
    self_head_gain,
    self_mix_gain,
    self_mix_shift,
    self_out,
    self_out_bias,
    cross_norm_gain,
    cross_norm_shift,
    cross_q,
    cross_q_bias,
    cross_kv,
    cross_v_bias,
    cross_head_gain,
    cross_mix_gain,
    cross_mix_shift,
    cross_out,
    cross_out_bias,
    ffn_norm_gain,
    ffn_norm_shift,
    ffn_in,
    ffn_in_bias,
    ffn_mid_gain,
    ffn_mid_shift,
    ffn_out,
    ffn_out_bias,
):
    items, length, width = dec_in.shape
    items_grp = owner.shape[1]
    shard_tokens = memory.shape[1]
    seq_size = lax.axis_size("seq")
    parts = lax.axis_size("grp")
    mem_tokens = shard_tokens * seq_size
    ff = ffn_in.shape[1]
    group = lax.axis_index("grp")
    seq_index = lax.axis_index("seq")
    paired = seq_size == 8 and parts == 4 and items == 2

    owner_row = lax.dynamic_index_in_dim(owner, group, 0, keepdims=False)
    slots = jnp.arange(items_grp, dtype=jnp.int32)
    inverse = jnp.sum(jnp.where(owner_row[None, :] == slots[:, None], slots[None, :], 0), axis=1)
    mine = lax.dynamic_slice_in_dim(inverse, seq_index * items, items)
    my_mem_len = jnp.take(mem_len, group * items_grp + mine)

    def exchange(sent):
        return lax.all_to_all(sent, "seq", split_axis=0, concat_axis=0, tiled=True)

    chain = Chain()
    by_item = inverse.reshape(seq_size, items)
    memories = []

    def gather(item):
        sent = chain.run(gather_items, memory, by_item[:, item])[0]
        memories.append(exchange(sent).reshape(mem_tokens, width))

    gather(0)

    def spread(gain):
        return jnp.repeat(gain, HD)

    vectors = [
        self_norm_gain, self_norm_shift, self_q_bias, self_v_bias, spread(self_head_gain),
        self_mix_gain, self_mix_shift, self_out_bias, cross_norm_gain, cross_norm_shift,
        cross_q_bias, cross_v_bias, spread(cross_head_gain), cross_mix_gain, cross_mix_shift,
        cross_out_bias, ffn_norm_gain, ffn_norm_shift, ffn_out_bias,
    ]
    vecs, wides = chain.run(prepare, vectors, [ffn_in_bias, ffn_mid_gain, ffn_mid_shift])
    bias = rel_bias_rows(rel_bias_table, length)
    buckets = bucket_lanes(length, rel_bias_table.shape[0])

    core, y = group % 2, group // 2
    x, z = seq_index % 2, seq_index // 2
    if paired:
        order = jnp.stack([(1 - y) * 2 + 1 - core, y * 2 + 1 - core, (1 - y) * 2 + core, y * 2 + core])
        places = jnp.sum(jnp.where(order[None, :] == jnp.arange(parts)[:, None], jnp.arange(parts)[None, :], 0), axis=1)
    else:
        order = places = jnp.arange(parts)
    order = jnp.concatenate([order, places]).astype(jnp.int32)

    starts = [
        chain.run(
            self_forward, item, dec_len, task_prefix, my_mem_len, order, dec_in, bias, self_qkv, self_out,
            cross_q, vecs,
        )
        for item in range(items)
    ]
    for item in range(1, items):
        gather(item)

    bundles = dict(
        A=Bundle([ffn_out.shape], width, parts),
        C=Bundle([ffn_in.shape], width, parts),
        D=Bundle([cross_kv.shape], width, parts),
        G=Bundle([cross_out.shape, cross_q.shape, self_out.shape], width, parts),
        E=Bundle([(width, width)], width, parts, vectors=True),
        H=Bundle([(width, 2 * width)], width, parts),
    )
    ahead, behind, returned, ends, state, done = {}, {}, {}, {}, {}, {}

    def start_sums(result, names):
        for name in names:
            sent, kept = result[f"sent{name}"], result[f"kept{name}"]
            state[name] = (kept, lax.ppermute(sent, "grp", CORE_PAIRS)) if paired else (sent, kept)

    def forward(item, **how):
        ahead[item] = chain.run(
            cross_forward, item, ahead, order, my_mem_len, dec_len, starts[item].x2, starts[item].q2,
            memories[item], cotangent, cross_kv, cross_out, ffn_in, ffn_out, vecs, wides, **how,
        )
        if item == items - 1:
            start_sums(ahead[item], "AC")

    def backward(item, **how):
        behind[item] = chain.run(
            cross_back, item, items, behind, starts, ahead, order, cross_kv, cross_out, cross_q, vecs, **how
        )
        returned[item] = exchange(behind[item].gmem.reshape(seq_size, shard_tokens, width))
        if item == items - 1:
            start_sums(behind[item], "DG")

    def self_backward(**how):
        ends.update(
            chain.run(
                self_back, starts, ahead, behind, order, dec_in, self_qkv, self_out, vecs, buckets, **how
            )
        )
        start_sums(ends, "EH")

    def scatter_memory(**how):
        return chain.run(scatter_items, [returned[i] for i in range(items)], inverse, **how)[0]

    if paired:
        side, z_side = x.reshape(1), (z % 2).reshape(1)
        inner = ((z == 1) | (z == 2)).astype(jnp.int32).reshape(1)

        def reduce_step(name, step, **how):
            along_y = step == (1 if ROUTE[name][0] == "Y" else 2)
            if step == 1:
                sent, kept = chain.run(first_add, *state[name], side, not along_y, **how)
                axis, pairs = ("grp", Y_PAIRS) if along_y else ("seq", X_PAIRS)
            elif step == 2:
                if along_y:
                    sent, kept = chain.run(core_add, *state[name], **how)
                else:
                    sent, kept = chain.run(split_add, *state[name], side, **how)
                axis, pairs = ("grp", Y_PAIRS) if along_y else ("seq", X_PAIRS)
            elif step == 3 and ROUTE[name][1] == "H":
                sent, kept = chain.run(split_add, *state[name], z_side, **how)
                axis, pairs = "seq", Z_NEAR
            elif step in (4, 5) and ROUTE[name][1] == "H":
                sent = kept = chain.run(add, *state[name], **how)[0]
                axis, pairs = "seq", Z_FAR if step == 4 else Z_NEAR
            elif step == 6 and ROUTE[name][1] == "H":
                sent = kept = chain.run(join, *state[name], z_side, **how)[0]
                axis, pairs = "seq", X_PAIRS
            elif step in (3, 4, 5):
                sent = kept = chain.run(add, *state[name], **how)[0]
                axis, pairs = "seq", (Z_IN, Z_MID, Z_OUT)[step - 3]
            elif step == 6:
                sent = kept = chain.run(pick, *state[name], inner, **how)[0]
                axis, pairs = "seq", X_PAIRS
            else:
                names = "EH" if name == "E" else name
                done[name] = chain.run(
                    finish, [bundles[n] for n in names], [state[n] for n in names], side, **how
                )
                return
            state[name] = kept, lax.ppermute(sent, axis, pairs)

        for step, cost in STEPS:
            if step[0] == "F":
                forward(int(step[1]), cost=cost)
            elif step[0] == "B":
                backward(int(step[1]), cost=cost)
            elif step == "S":
                self_backward(cost=cost)
            elif step == "SC":
                grad_memory = scatter_memory(cost=cost)
            else:
                reduce_step(step[0], int(step[1]), cost=cost)
    else:
        for item in range(items):
            forward(item)
            backward(item)
        self_backward()
        none = jnp.zeros((1,), jnp.int32)
        for name in ROUTE:
            share = lax.psum_scatter(jnp.concatenate(state[name]), "grp", scatter_dimension=0, tiled=True)[0]
            state[name] = lax.psum(share, "seq"), None
        for names in ("A", "C", "D", "G", "EH"):
            done[names[0]] = chain.run(finish, [bundles[n] for n in names], [state[n] for n in names], none)
        grad_memory = scatter_memory()

    out, gx = ahead[items - 1].out, ends["gx"]
    g_ffn_out, g_ffn_in, g_cross_kv = (done[name][0] for name in ("A", "C", "D"))
    g_cross_out, g_cross_q, g_self_out = done["G"]
    g_self_qkv, vec = done["E"]
    (
        g_self_norm_gain, g_self_norm_shift, g_self_q_bias, g_self_v_bias, g_self_mix_gain,
        g_self_mix_shift, g_self_out_bias, g_cross_norm_gain, g_cross_norm_shift, g_cross_q_bias,
        g_cross_v_bias, g_cross_mix_gain, g_cross_mix_shift, g_cross_out_bias, g_ffn_norm_gain,
        g_ffn_norm_shift, g_ffn_out_bias, g_ffn_in_bias, g_ffn_mid_gain, g_ffn_mid_shift,
        g_self_head, g_cross_head, g_table,
    ) = chain.run(
        vector_outputs, vec, group.reshape(1), parts, ff, rel_bias_table.shape[0]
    )
    return (
        out,
        gx,
        grad_memory,
        g_self_norm_gain,
        g_self_norm_shift,
        g_self_qkv,
        g_self_q_bias,
        g_self_v_bias,
        g_table,
        g_self_head,
        g_self_mix_gain,
        g_self_mix_shift,
        g_self_out,
        g_self_out_bias,
        g_cross_norm_gain,
        g_cross_norm_shift,
        g_cross_q,
        g_cross_q_bias,
        g_cross_kv,
        g_cross_v_bias,
        g_cross_head,
        g_cross_mix_gain,
        g_cross_mix_shift,
        g_cross_out,
        g_cross_out_bias,
        g_ffn_norm_gain,
        g_ffn_norm_shift,
        g_ffn_in,
        g_ffn_in_bias,
        g_ffn_mid_gain,
        g_ffn_mid_shift,
        g_ffn_out,
        g_ffn_out_bias,
    )


def solution(mesh):
    rows = P(("seq", "grp"), None, None)
    matrix, vector = P("grp", None), P("grp")
    in_specs = (rows, P("grp", "seq", None), rows, P(("seq", "grp")), P(("seq", "grp"))) + (P(),) * 32
    out_specs = (
        rows, rows, P("grp", "seq", None),
        vector, vector, matrix, vector, vector, matrix, vector, vector, vector, matrix, vector,
        vector, vector, matrix, vector, matrix, vector, vector, vector, vector, matrix, vector,
        vector, vector, matrix, vector, vector, vector, matrix, vector,
    )
    return jax.shard_map(local, mesh=mesh, in_specs=in_specs, out_specs=out_specs, check_vma=False)
```

```python
import functools
import math

import jax
import jax.numpy as jnp
from jax import lax
from jax.experimental import pallas as pl
from jax.experimental.pallas import tpu as pltpu
from jax.sharding import PartitionSpec as P

H = 12
HD = 64
EPSILON = 1e-05
FACTOR = 1.0 / math.sqrt(HD)
MASKED = -1000000000.0
F32 = jnp.float32
BF16 = jnp.bfloat16
PAIR = 2 * HD
PAIRS = H // 2

(
    SELF_GAIN,
    SELF_SHIFT,
    SELF_QB,
    SELF_VB,
    SELF_HEAD,
    SELF_MIX_GAIN,
    SELF_MIX_SHIFT,
    SELF_OB,
    CROSS_GAIN,
    CROSS_SHIFT,
    CROSS_QB,
    CROSS_VB,
    CROSS_HEAD,
    CROSS_MIX_GAIN,
    CROSS_MIX_SHIFT,
    CROSS_OB,
    FFN_GAIN,
    FFN_SHIFT,
    FFN_OB,
) = range(19)
IN_BIAS, MID_GAIN, MID_SHIFT, TABLE = 20, 24, 28, 32
VEC_ROWS = 64


def dot(left, right):
    return jnp.dot(left, right, preferred_element_type=F32)


def dot_rows(left, right):
    return lax.dot_general(left, right, (((1,), (1,)), ((), ())), preferred_element_type=F32)


def dot_cols(left, right):
    return lax.dot_general(left, right, (((0,), (0,)), ((), ())), preferred_element_type=F32)


def normalize(values):
    average = jnp.mean(values, axis=-1, keepdims=True)
    centered = values - average
    spread = jnp.mean(centered * centered, axis=-1, keepdims=True)
    scale = lax.rsqrt(spread + EPSILON)
    return centered * scale, scale


def normalize_back(grad, normed, scale):
    mean_grad = jnp.mean(grad, axis=-1, keepdims=True)
    mean_both = jnp.mean(grad * normed, axis=-1, keepdims=True)
    return scale * (grad - mean_grad - normed * mean_both)


def total(values):
    return jnp.sum(values.astype(F32), axis=0, keepdims=True)


def lanes(start, size):
    return pl.ds(pl.multiple_of(start, 128), size)


def pick_head(values, half, axis):
    place = lax.broadcasted_iota(jnp.int32, values.shape, axis)
    inside = (place < HD) if half == 0 else (place >= HD)
    return jnp.where(inside, values, jnp.zeros_like(values))


def attend_pair(queries, keys, values, score_fn, e_ref, inv_ref, first):
    values_t = values.T
    ones = jnp.ones((16, values.shape[0]), BF16)
    scores = [score_fn(dot_rows(keys, pick_head(queries, half, 1)), first + half) for half in range(2)]
    parts = []
    for half in range(2):
        peak = jnp.max(scores[half], axis=0, keepdims=True)
        low = jnp.exp(scores[half] - peak).astype(BF16)
        e_ref[first + half] = low
        mixed = dot(jnp.concatenate([values_t[half * HD : (half + 1) * HD], ones], axis=0), low)
        inverse = 1.0 / mixed[HD : HD + 1]
        inv_ref[pl.ds(first + half, 1), :] = inverse
        parts.append(mixed[:HD] * inverse)
    return jnp.concatenate(parts, axis=0).T


def attend_pair_back(queries, keys, values, grad, prod, e_ref, inv_ref, first, keep_scores):
    keys_t = keys.T
    grad_t = grad.astype(F32).T
    prod_t = prod.T
    grads, deltas, grad_probs = [], [], []
    for half in range(2):
        rows = slice(half * HD, (half + 1) * HD)
        inverse = inv_ref[pl.ds(first + half, 1), :]
        deltas.append(jnp.sum(prod_t[rows], axis=0, keepdims=True) * inverse)
        grads.append(pick_head((grad_t * inverse).astype(BF16), half, 0))
        grad_probs.append(dot(values, grads[half]))
    lows = [e_ref[first + half] for half in range(2)]
    dv = dot_rows(jnp.concatenate(lows, axis=1), jnp.concatenate(grads, axis=1))
    scores = []
    for half in range(2):
        scores.append((lows[half].astype(F32) * (grad_probs[half] - deltas[half])).astype(BF16))
        if keep_scores is not None:
            keep_scores(scores[half], first + half)
    heads = jnp.concatenate([pick_head(queries, half, 1) for half in range(2)], axis=0)
    dk = dot(jnp.concatenate(scores, axis=1), heads)
    dq = [dot(keys_t[half * HD : (half + 1) * HD], scores[half]) for half in range(2)]
    return jnp.concatenate(dq, axis=0).T * FACTOR, dk, dv


class Gradients:
    def __init__(self, order_ref, sems, width):
        self.order_ref, self.sems, self.width = order_ref, sems, width
        self.parts = order_ref.shape[0] // 2
        self.used, self.copies = 0, []

    def load(self, far, near):
        copy = pltpu.make_async_copy(far, near, self.sems.at[self.used])
        copy.start()
        self.copies.append(copy)
        self.used += 1

    def load_left(self, far, near, item):
        size, depth = far.shape[0] // self.parts, far.shape[1]
        for j in range(self.parts):
            rows = pl.ds(pl.multiple_of(self.order_ref[j] * size, 16), size)
            self.load(far.at[rows, :], near.at[pl.ds(j * size, size), pl.ds(item * depth, depth)])

    def load_right(self, far, near, item):
        depth = far.shape[0]
        self.load(far, near.at[pl.ds(item * depth, depth), :])

    def wait(self):
        for copy in self.copies:
            copy.wait()
        self.copies = []

    def place(self, quarter, size):
        return pl.ds(pl.multiple_of(self.order_ref[self.parts + quarter] * size, 16), size)

    def put_left(self, value, near, item):
        size, depth = value.shape[0] // self.parts, value.shape[1]
        for quarter in range(self.parts):
            near[self.place(quarter, size), item * depth : (item + 1) * depth] = value[
                quarter * size : (quarter + 1) * size
            ]

    def put(self, outs, quarter, place, value):
        half = self.parts // 2
        outs[quarter // half][quarter % half, place, :] = value.astype(BF16)

    def store(self, io, name, row, size):
        rows = pl.ds(row, size)
        for side in ("sent", "kept"):
            near, far = io.near[side + name].at[:, rows, :], io.far[side + name].at[:, rows, :]
            copy = pltpu.make_async_copy(near, far, self.sems.at[self.used])
            copy.start()
            io.storing.append(copy)
            self.used += 1

    def sum(self, io, name, left, right, row):
        outs = io.near["sent" + name], io.near["kept" + name]
        size = left.shape[0] // self.parts
        span = min(left.shape[0], self.width)
        for column in range(right.shape[1] // self.width):
            cols = slice(column * self.width, (column + 1) * self.width)
            for top in range(0, left.shape[0], span):
                value = dot(left[top : top + span, :], right[:, cols])
                for quarter in range(top // size, (top + span - 1) // size + 1):
                    low, high = max(top, quarter * size), min(top + span, (quarter + 1) * size)
                    place = slice(row + low - quarter * size, row + high - quarter * size)
                    self.put(outs, quarter, place, value[low - top : high - top])
            self.store(io, name, row, size)
            row += size
        return row


def item_rows(ref, item, depth):
    return ref.at[pl.ds(item * depth, depth), :]


def self_forward_kernel(item, io, len_ref, prefix_ref, *_):
    io.load("x", "vecs", "qkv_w", "bias", "out_w", "q2_w")
    _, length, width = io.x.shape
    vec_ref = io.vecs

    def vec(row):
        return vec_ref[row : row + 1, :]

    io.need("x", "vecs")
    x = io.x[item].astype(F32)
    normed, _ = normalize(x)
    low = (normed * vec(SELF_GAIN) + vec(SELF_SHIFT)).astype(BF16)
    io.n1t[...] = low.T
    io.store("n1t")
    io.need("qkv_w")
    queries = dot(low, io.qkv_w[:, :width]) + vec(SELF_QB)
    io.qkv[:, :width] = queries.astype(BF16) * jnp.asarray(FACTOR, BF16)
    io.qkv[:, width : 2 * width] = dot(low, io.qkv_w[:, width : 2 * width]).astype(BF16)
    values = dot(low, io.qkv_w[:, 2 * width :]) + vec(SELF_VB)
    io.qkv[:, 2 * width :] = values.astype(BF16)
    io.store("qkv")
    key_pos = lax.broadcasted_iota(jnp.int32, (length, length), 0)
    query_pos = lax.broadcasted_iota(jnp.int32, (length, length), 1)
    allowed = (key_pos < len_ref[item]) & ((key_pos <= query_pos) | (key_pos < prefix_ref[item]))
    io.inv[...] = jnp.zeros_like(io.inv)
    io.need("bias")

    def scores_of(scores, head):
        row = jnp.broadcast_to(io.bias[pl.ds(head, 1), :], (length, 2 * length))
        bias = pltpu.roll(row, 0, 1, stride=1, stride_axis=0)[:, :length]
        return jnp.where(allowed, scores + bias, MASKED)

    def one_pair(pair, _):
        base = pair * PAIR
        io.mixed[:, lanes(base, PAIR)] = attend_pair(
            io.qkv[:, lanes(base, PAIR)],
            io.qkv[:, lanes(base + width, PAIR)],
            io.qkv[:, lanes(base + 2 * width, PAIR)],
            scores_of, io.e, io.inv, 2 * pair,
        )
        return 0

    lax.fori_loop(0, PAIRS, one_pair, 0, unroll=2)
    io.store("e", "inv", "mixed")
    normed, _ = normalize(io.mixed[...] * vec(SELF_HEAD))
    low = (normed * vec(SELF_MIX_GAIN) + vec(SELF_MIX_SHIFT)).astype(BF16)
    io.z1t[...] = low.T
    io.store("z1t")
    io.need("out_w")
    x2 = x + dot(low, io.out_w[...]) + vec(SELF_OB)
    io.x2[...] = x2
    io.store("x2")
    normed, _ = normalize(x2)
    low = (normed * vec(CROSS_GAIN) + vec(CROSS_SHIFT)).astype(BF16)
    io.n2t[...] = low.T
    io.need("q2_w")
    queries = dot(low, io.q2_w[...]) + vec(CROSS_QB)
    io.q2[...] = queries.astype(BF16) * jnp.asarray(FACTOR, BF16)
    io.store("n2t", "q2")


def gelu_parts(hidden):
    gate = 0.5 * (1.0 + lax.erf(hidden * math.sqrt(0.5)))
    slope = hidden * (jnp.exp(-0.5 * hidden * hidden) * (1.0 / math.sqrt(2.0 * math.pi)))
    return hidden * gate, gate + slope


def cross_forward_kernel(item, last, io, mem_len_ref, dec_len_ref, *refs):
    act_ref, grad_ref, slope_ref, mid_ref = refs[-4:]
    io.load("mem", "kv_w", "vecs")
    length, width = io.x2.shape
    mem_tokens = io.mem.shape[0]
    ff = io.in_w.shape[1]
    tiles = ff // width
    mem_ref, kv_ref, kv_w, vec_ref, wide_ref = io.mem, io.kv, io.kv_w, io.vecs, io.wides
    e_ref, inv_ref, mixed_ref, q2_ref, vg_ref = io.e, io.inv, io.mixed, io.q2, io.vg
    out_w, in_w, ffn_w = io.out_w, io.in_w, io.ffn_w
    if last:
        order_ref, left_out, right_out, left_in, right_in, sems = refs[:-4]
        grads = Gradients(order_ref, sems, width)
        hid_ref, cot_low_ref = item_rows(right_in, item, length), item_rows(right_out, item, length)
    else:
        hid_ref, cot_low_ref = io.hid, io.cot_low

    def vec(row):
        return vec_ref[row : row + 1, :]

    io.need("mem", "kv_w", "vecs")
    io.load("q2", "x2", "out_w", "in_w", "wides")
    io.load("cot", at=item)
    io.load("ffn_w")
    if last:
        for i in range(item):
            grads.load_left(io.far[f"midt{i}"], left_out, i)
            grads.load_right(io.far[f"cot_low{i}"], right_out, i)
            grads.load_left(io.far[f"n3t{i}"], left_in, i)
            grads.load_right(io.far[f"hid{i}"], right_in, i)
    io.memt[...] = mem_ref[...].T
    io.store("memt")
    kv_ref[:, :width] = dot(mem_ref[...], kv_w[:, :width]).astype(BF16)
    kv_ref[:, width:] = (dot(mem_ref[...], kv_w[:, width:]) + vec(CROSS_VB)).astype(BF16)
    io.store("kv")
    io.need("q2")
    mem_len = mem_len_ref[item]
    inv_ref[...] = jnp.zeros_like(inv_ref)

    def scores_of(scores, head):
        del head
        key_pos = lax.broadcasted_iota(jnp.int32, (mem_tokens, length), 0)
        return jnp.where(key_pos < mem_len, scores, MASKED)

    def one_pair(pair, _):
        base = pair * PAIR
        mixed_ref[:, lanes(base, PAIR)] = attend_pair(
            q2_ref[:, lanes(base, PAIR)],
            kv_ref[:, lanes(base, PAIR)],
            kv_ref[:, lanes(base + width, PAIR)],
            scores_of, e_ref, inv_ref, 2 * pair,
        )
        return 0

    lax.fori_loop(0, PAIRS, one_pair, 0, unroll=2)
    io.store("e", "inv", "mixed")
    normed, _ = normalize(mixed_ref[...] * vec(CROSS_HEAD))
    low = (normed * vec(CROSS_MIX_GAIN) + vec(CROSS_MIX_SHIFT)).astype(BF16)
    io.z2t[...] = low.T
    io.store("z2t")
    io.need("x2", "out_w")
    x3 = io.x2[...] + dot(low, out_w[...]) + vec(CROSS_OB)
    norm3, scale3 = normalize(x3)
    n3 = (norm3 * vec(FFN_GAIN) + vec(FFN_SHIFT)).astype(BF16)
    if last:
        grads.put_left(n3.T, left_in, item)
    else:
        io.n3t[...] = n3.T
        io.store("n3t")
    io.need("in_w", "wides")

    def hidden_tile(tile, sums):
        cols = lanes(tile * width, width)
        hidden = dot(n3, in_w[:, cols]) + wide_ref[0:1, cols]
        act, slope = gelu_parts(hidden)
        act_ref[:, cols] = act
        slope_ref[:, cols] = slope.astype(BF16)
        return sums + jnp.sum(act, axis=-1, keepdims=True)

    sums = lax.fori_loop(0, tiles, hidden_tile, jnp.zeros((length, 1), F32), unroll=True)
    average = sums / ff

    def spread_tile(tile, sums):
        centered = act_ref[:, lanes(tile * width, width)] - average
        return sums + jnp.sum(centered * centered, axis=-1, keepdims=True)

    sums = lax.fori_loop(0, tiles, spread_tile, jnp.zeros((length, 1), F32), unroll=True)
    scale = lax.rsqrt(sums / ff + EPSILON)

    def middle_tile(tile, _):
        cols = lanes(tile * width, width)
        normed = (act_ref[:, cols] - average) * scale
        act_ref[:, cols] = normed
        low = (normed * wide_ref[1:2, cols] + wide_ref[2:3, cols]).astype(BF16)
        mid_ref[:, cols] = low
        if last:
            left_out[grads.place(tile, width), item * length : (item + 1) * length] = low.T
        else:
            io.midt[pl.ds(pl.multiple_of(tile * width, 128), width), :] = low.T
        return 0

    lax.fori_loop(0, tiles, middle_tile, 0, unroll=True)
    if not last:
        io.store("midt")
    io.need("ffn_w", "cot")
    result = x3 + dot(mid_ref[...], ffn_w[...]) + vec(FFN_OB)
    io.out[...] = result.astype(BF16)
    io.store("out", at=item)

    valid = lax.broadcasted_iota(jnp.int32, (length, 1), 0) < dec_len_ref[item]
    cot = jnp.where(valid, io.cot[...].astype(F32), 0.0)
    cot_low_ref[...] = cot.astype(BF16)
    if not last:
        io.store("cot_low")
    vg_ref[...] = jnp.zeros_like(vg_ref)

    def grad_mid_tile(tile, sums):
        cols = lanes(tile * width, width)
        grad_mid = dot_rows(cot_low_ref[...], ffn_w[cols, :])
        normed = act_ref[:, cols]
        vg_ref[pl.ds(MID_GAIN + tile, 1), :] = total(grad_mid * normed)
        vg_ref[pl.ds(MID_SHIFT + tile, 1), :] = total(grad_mid)
        grad = grad_mid * wide_ref[1:2, cols]
        grad_ref[:, cols] = grad.astype(BF16)
        return (
            sums[0] + jnp.sum(grad, axis=-1, keepdims=True),
            sums[1] + jnp.sum(grad * normed, axis=-1, keepdims=True),
        )

    zero = jnp.zeros((length, 1), F32)
    sum_grad, sum_both = lax.fori_loop(0, tiles, grad_mid_tile, (zero, zero), unroll=True)
    mean_grad, mean_both = sum_grad / ff, sum_both / ff

    def hidden_back_tile(tile, _):
        cols = lanes(tile * width, width)
        grad = scale * (grad_ref[:, cols].astype(F32) - mean_grad - act_ref[:, cols] * mean_both)
        low = (grad * slope_ref[:, cols].astype(F32)).astype(BF16)
        hid_ref[:, cols] = low
        vg_ref[pl.ds(IN_BIAS + tile, 1), :] = total(low)
        return 0

    lax.fori_loop(0, tiles, hidden_back_tile, 0, unroll=True)
    if not last:
        io.store("hid")
    grad_n3 = dot_rows(hid_ref[...], in_w[...])
    vg_ref[FFN_GAIN : FFN_GAIN + 1, :] = total(grad_n3 * norm3)
    vg_ref[FFN_SHIFT : FFN_SHIFT + 1, :] = total(grad_n3)
    vg_ref[FFN_OB : FFN_OB + 1, :] = total(cot_low_ref[...])
    gx3 = normalize_back(grad_n3 * vec(FFN_GAIN), norm3, scale3) + cot
    io.gx3[...] = gx3
    io.branch[...] = gx3.astype(BF16)
    io.store("gx3", "branch")
    vg_ref[CROSS_OB : CROSS_OB + 1, :] = total(io.branch[...])
    io.store("vg")
    if last:
        grads.wait()
        grads.sum(io, "A", left_out, right_out, 0)
        grads.sum(io, "C", left_in, right_in, 0)


def cross_back_kernel(item, last, io, *refs):
    e_ref, _, grad_ref, prod_ref = refs[-4:]
    length, width = io.x2.shape
    mem_tokens = io.kv.shape[0]
    vec_ref, vg_ref = io.vecs, io.vg
    if last:
        order_ref, left_mem, right_mem, left_z, right_z, left_n, right_n, left_s, right_s, sems = refs[:-4]
        grads = Gradients(order_ref, sems, width)
        dkv_ref, dq_ref = item_rows(right_mem, item, mem_tokens), item_rows(right_n, item, length)
    else:
        dkv_ref, dq_ref = io.dkv, io.dq
    io.load("vecs", "mixed", "branch", "out_w", "q2", "inv", "kv")
    pair_sems = refs[-3]
    pair_copies = [
        pltpu.make_async_copy(io.far["e"].at[pl.ds(2 * p, 2)], e_ref.at[pl.ds(2 * p, 2)], pair_sems.at[p])
        for p in range(PAIRS)
    ]
    for copy in pair_copies:
        copy.start()

    def load_later():
        io.load("kv_w", "x2", "q2_w", "gx3")
        if not last:
            return
        for i in range(item + 1):
            grads.load_left(io.far[f"memt{i}"], left_mem, i)
            if i < item:
                grads.load_right(io.far[f"dkv{i}"], right_mem, i)
        for i in range(item + 1):
            grads.load_left(io.far[f"z2t{i}"], left_z, i)
            grads.load_left(io.far[f"n2t{i}"], left_n, i)
            grads.load_left(io.far[f"z1t{i}"], left_s, i)
            grads.load_right(io.far[f"branch{i}"], right_z, i)
            if i < item:
                grads.load_right(io.far[f"dq{i}"], right_n, i)
                grads.load_right(io.far[f"branch2{i}"], right_s, i)

    def vec(row):
        return vec_ref[row : row + 1, :]

    def put(row, value):
        vg_ref[row : row + 1, :] = value

    if not last:
        load_later()
    vg_ref[...] = jnp.zeros_like(vg_ref)
    io.need("vecs", "mixed")
    mixed = io.mixed[...]
    normed, scale = normalize(mixed * vec(CROSS_HEAD))
    io.need("branch", "out_w")
    grad = dot_rows(io.branch[...], io.out_w[...])
    put(CROSS_MIX_GAIN, total(grad * normed))
    put(CROSS_MIX_SHIFT, total(grad))
    grad = normalize_back(grad * vec(CROSS_MIX_GAIN), normed, scale)
    put(CROSS_HEAD, total(grad * mixed))
    grad = (grad * vec(CROSS_HEAD)).astype(BF16)
    grad_ref[...] = grad
    prod_ref[...] = grad.astype(F32) * mixed
    for pair in range(PAIRS):
        if pair == 0:
            io.need("q2", "inv", "kv")
        pair_copies[pair].wait()
        if pair == 1 and last:
            load_later()
        base = pair * PAIR
        cols = slice(base, base + PAIR)
        dq, dk, dv = attend_pair_back(
            io.q2[:, cols], io.kv[:, cols], io.kv[:, base + width : base + width + PAIR],
            grad_ref[:, cols], prod_ref[:, cols], e_ref, io.inv, 2 * pair, None,
        )
        dq_ref[:, cols] = dq.astype(BF16)
        dkv_ref[:, cols] = dk.astype(BF16)
        dkv_ref[:, base + width : base + width + PAIR] = dv.astype(BF16)

    if not last:
        io.store("dkv", "dq")
    put(CROSS_VB, total(dkv_ref[:, width:]))
    step = 256
    io.need("kv_w")

    def memory_tile(tile, _):
        cols = lanes(tile * step, step)
        io.gmem[:, cols] = dot_rows(dkv_ref[...], io.kv_w[cols, :]).astype(BF16)
        return 0

    lax.fori_loop(0, width // step, memory_tile, 0, unroll=True)
    io.store("gmem")
    put(CROSS_QB, total(dq_ref[...]))
    io.need("x2", "q2_w", "gx3")
    normed, scale = normalize(io.x2[...])
    grad = dot_rows(dq_ref[...], io.q2_w[...])
    put(CROSS_GAIN, total(grad * normed))
    put(CROSS_SHIFT, total(grad))
    gx2 = normalize_back(grad * vec(CROSS_GAIN), normed, scale) + io.gx3[...]
    io.gx2[...] = gx2
    io.branch2[...] = gx2.astype(BF16)
    io.store("gx2", "branch2")
    put(SELF_OB, total(io.branch2[...]))
    io.store("vg")
    if last:
        right_s[item * length : (item + 1) * length, :] = io.branch2[...]
        grads.wait()
        grads.sum(io, "D", left_mem, right_mem, 0)
        row = 0
        for left, right in ((left_z, right_z), (left_n, right_n), (left_s, right_s)):
            row = grads.sum(io, "G", left, right, row)


def self_back_kernel(items, io, order_ref, left, right, vg_refs, sems, grad_ref, prod_ref, diag_ref):
    _, length, width = io.x.shape
    shared = ("mixed", "branch", "qkv", "inv", "e")
    io.load("vecs", "mixed0", "branch0", "out_w", "qkv0", "inv0", "e0")
    grads = Gradients(order_ref, sems, width)

    def load_later():
        io.load("buckets", "x", "qkv_w", "gx20")
        for item in range(1, items):
            io.load(*[f"{name}{item}" for name in shared + ("gx2",)])
        for item in range(items):
            grads.load_left(io.far[f"n1t{item}"], left, item)
            for i, name in enumerate(("vgf", "vgb")):
                grads.load(io.far[f"{name}{item}"], vg_refs.at[2 * item + i])

    own = 2 * items
    for item in range(items):
        self_back_item(
            item, io, item_rows(right, item, length), vg_refs.at[own + item], grad_ref, prod_ref, diag_ref,
            load_later if item == 0 else None,
        )
    grads.wait()
    outs = (io.sentE, io.keptE)
    grads.sum(io, "H", left, right.at[:, pl.ds(width, 2 * width)], 0)
    row = grads.sum(io, "E", left, right.at[:, pl.ds(0, width)], 0)
    value = vg_refs[0]
    for i in range(1, 3 * items):
        value = value + vg_refs[i]
    for quarter in range(grads.parts):
        grads.put(outs, quarter, slice(row, row + VEC_ROWS), value)
    grads.store(io, "E", row, VEC_ROWS)


def self_back_item(item, io, dqkv_ref, vg_ref, grad_ref, prod_ref, diag_ref, load_later):
    _, length, width = io.x.shape
    vec_ref = io.vecs
    near = {name: io.near[f"{name}{item}"] for name in ("mixed", "branch", "qkv", "inv", "e", "gx2")}
    qkv_ref = near["qkv"]

    def vec(row):
        return vec_ref[row : row + 1, :]

    def put(row, value):
        vg_ref[row : row + 1, :] = value

    vg_ref[...] = jnp.zeros_like(vg_ref)
    diag_ref[...] = jnp.zeros_like(diag_ref)
    if item == 0:
        io.need("vecs")
    io.need(f"mixed{item}")
    mixed = near["mixed"][...]
    normed, scale = normalize(mixed * vec(SELF_HEAD))
    io.need(f"branch{item}")
    if item == 0:
        io.need("out_w")
    grad = dot_rows(near["branch"][...], io.out_w[...])
    put(SELF_MIX_GAIN, total(grad * normed))
    put(SELF_MIX_SHIFT, total(grad))
    grad = normalize_back(grad * vec(SELF_MIX_GAIN), normed, scale)
    put(SELF_HEAD, total(grad * mixed))
    grad = (grad * vec(SELF_HEAD)).astype(BF16)
    grad_ref[...] = grad
    prod_ref[...] = grad.astype(F32) * mixed
    io.need(f"qkv{item}", f"inv{item}", f"e{item}")
    if load_later is not None:
        load_later()
    backwards = (
        lax.broadcasted_iota(jnp.int32, (length, length), 0)
        + lax.broadcasted_iota(jnp.int32, (length, length), 1)
        == length - 1
    ).astype(F32).astype(BF16)

    def keep_scores(scores, head):
        flipped = dot(backwards, scores)
        padded = jnp.concatenate([flipped, jnp.zeros_like(flipped)], axis=1)
        rolled = pltpu.roll(padded, 0, 1, stride=1, stride_axis=0)
        diag_ref[pl.ds(head, 1), :] = jnp.sum(rolled, axis=0, keepdims=True)

    def one_pair(pair, _):
        base = pair * PAIR
        cols = lanes(base, PAIR)
        dq, dk, dv = attend_pair_back(
            qkv_ref[:, cols], qkv_ref[:, lanes(base + width, PAIR)],
            qkv_ref[:, lanes(base + 2 * width, PAIR)],
            grad_ref[:, cols], prod_ref[:, cols], near["e"], near["inv"], 2 * pair, keep_scores,
        )
        dqkv_ref[:, cols] = dq.astype(BF16)
        dqkv_ref[:, lanes(base + width, PAIR)] = dk.astype(BF16)
        dqkv_ref[:, lanes(base + 2 * width, PAIR)] = dv.astype(BF16)
        return 0

    lax.fori_loop(0, PAIRS, one_pair, 0, unroll=2)
    if item == 0:
        io.need("buckets", "x", "qkv_w")
    table = jnp.dot(
        diag_ref[...], io.buckets[...], precision=lax.Precision.HIGHEST, preferred_element_type=F32
    )
    vg_ref[TABLE : TABLE + 16, : table.shape[1]] = table
    put(SELF_QB, total(dqkv_ref[:, :width]))
    put(SELF_VB, total(dqkv_ref[:, 2 * width :]))
    normed, scale = normalize(io.x[item].astype(F32))
    grad = dot_rows(dqkv_ref[...], io.qkv_w[...])
    put(SELF_GAIN, total(grad * normed))
    put(SELF_SHIFT, total(grad))
    io.need(f"gx2{item}")
    gx = normalize_back(grad * vec(SELF_GAIN), normed, scale) + near["gx2"][...]
    io.gx[item] = gx.astype(BF16)
    if item == io.gx.shape[0] - 1:
        io.store("gx")


SMEM = pl.BlockSpec(memory_space=pltpu.SMEM)
VMEM = pl.BlockSpec(memory_space=pltpu.VMEM)
ANY = pl.BlockSpec(memory_space=pl.ANY)
HBM = pl.BlockSpec(memory_space=pltpu.HBM)
MIB = 1024 * 1024


COST = dict(
    self_forward=11, cross_forward=28, cross_back=18, self_back=10, weight_grads=5, finish=2, split_add=1, core_add=1, first_add=2, join=1,
    gather_items=3, scatter_items=4, add=1, pick=1, vectors=1,
)
COST_SCALE = 3_000_000


class Kept:
    def __init__(self, shape, dtype):
        self.shape, self.dtype = tuple(shape), dtype


class Stored(Kept):
    pass


class Token:
    def __init__(self, array, near):
        self.space = pltpu.VMEM if near else pltpu.HBM
        self.spec = VMEM if near else HBM
        self.array = array

    def operand(self):
        return pltpu.with_memory_space_constraint(self.array, self.space)


def token_args(after):
    return [t.spec for t in after], [t.operand() for t in after]


def call(kernel, name, ins, outs, scratch=(), after=(), limit=16, scalars=(), far=()):
    after_specs, after_args = token_args(after)
    first = len(scalars) + len(far) + len(ins)
    last = first + len(after)

    def body(*refs):
        kernel(*refs[:first], *refs[last:])

    ins = [pltpu.with_memory_space_constraint(a, pltpu.VMEM) for a in ins]
    far = [pltpu.with_memory_space_constraint(a, pltpu.HBM) for a in far]
    shapes = [(pltpu.HBM if isinstance(o, Stored) else pltpu.VMEM)(o.shape, o.dtype) for o in outs]
    Chain.token = 0, not isinstance(outs[0], Stored)
    return pl.pallas_call(
        body,
        out_shape=shapes,
        in_specs=[SMEM] * len(scalars) + [HBM] * len(far) + [VMEM] * len(ins) + after_specs,
        out_specs=[VMEM] * len(shapes),
        scratch_shapes=list(scratch),
        compiler_params=pltpu.CompilerParams(vmem_limit_bytes=limit * MIB),
        cost_estimate=cost_of(name),
        name=name,
    )(*scalars, *far, *ins, *after_args)


class Stream:
    def __init__(self, ins, outs, far, near, sems):
        self.names = list(ins) + list(outs)
        self.far, self.near = dict(zip(self.names, far)), dict(zip(self.names, near))
        self.sems = dict(zip(self.names, range(len(self.names))))
        self.sem_refs = sems
        self.loading, self.storing = {}, []

    def __getattr__(self, name):
        return self.near[name]

    def load(self, *names, at=None):
        for name in names:
            far = self.far[name] if at is None else self.far[name].at[at]
            copy = pltpu.make_async_copy(far, self.near[name], self.sem_refs.at[self.sems[name]])
            copy.start()
            self.loading[name] = copy

    def need(self, *names):
        for name in names:
            self.loading.pop(name).wait()

    def store(self, *names, at=None):
        for name in names:
            far = self.far[name] if at is None else self.far[name].at[at]
            copy = pltpu.make_async_copy(self.near[name], far, self.sem_refs.at[self.sems[name]])
            copy.start()
            self.storing.append(copy)

    def drain(self):
        assert not self.loading
        for copy in self.storing:
            copy.wait()


def stream_call(kernel, name, ins, outs, scratch=(), after=(), scalars=(), limit=16, kept=(), free=(), token="vg", gathered={}, far=None, parted=()):
    far = far or {}
    after_specs, after_args = token_args(after)
    n_in, n_out = len(ins), len(outs)
    far_outs = [n for n in outs if n not in kept]

    def body(*refs):
        refs = list(refs)

        def take(count):
            taken, refs[:] = refs[:count], refs[count:]
            return taken

        scalar_refs, far_in = take(len(scalars)), take(n_in)
        far_only = dict(zip(far, take(len(far))))
        take(len(after) + len(filled))
        out_refs = dict(zip(outs, take(n_out)))
        near_in = take(n_in)
        near_out = dict(zip(far_outs, take(len(far_outs))))
        sems = refs.pop()
        near_out.update({n: out_refs[n] for n in kept})
        io = Stream(
            ins, outs, far_in + [out_refs[n] for n in outs], near_in + [near_out[n] for n in outs], sems
        )
        io.far.update(far_only)
        kernel(io, *scalar_refs, *refs)
        io.drain()

    filled = {n: array for n, (_, array) in gathered.items() if array is not None}
    before = len(scalars) + n_in + len(far) + len(after)
    aliases = {before + i: list(outs).index(n) for i, n in enumerate(filled)}
    shapes = [
        pltpu.VMEM(s, d) if n in kept else pltpu.HBM((gathered[n][0],) + s if n in gathered else s, d)
        for n, (s, d) in outs.items()
    ]
    buffers = [pltpu.VMEM(a.shape[1:] if n in parted else a.shape, a.dtype) for n, a in ins.items()]
    buffers += [pltpu.VMEM(*outs[n]) for n in far_outs]
    results = pl.pallas_call(
        body,
        out_shape=shapes,
        in_specs=[SMEM] * len(scalars)
        + [ANY if n in free else HBM for n in ins]
        + [HBM] * len(far)
        + after_specs
        + [HBM] * len(filled),
        input_output_aliases=aliases,
        out_specs=[VMEM if n in kept else HBM for n in outs],
        scratch_shapes=buffers + list(scratch) + [pltpu.SemaphoreType.DMA((n_in + n_out,))],
        compiler_params=pltpu.CompilerParams(vmem_limit_bytes=limit * MIB),
        cost_estimate=cost_of(name),
        name=name,
    )(
        *scalars,
        *[a if n in free else pltpu.with_memory_space_constraint(a, pltpu.HBM) for n, a in ins.items()],
        *[pltpu.with_memory_space_constraint(a, pltpu.HBM) for a in far.values()],
        *after_args,
        *filled.values(),
    )
    Chain.token = list(outs).index(token), token in kept
    return Result(zip(outs, results))


class Result(dict):
    def __getattr__(self, name):
        return self[name]


def self_forward(item, dec_len, prefix, mem_len, order, x, bias, qkv_w, out_w, q2_w, vecs, after):
    _, length, width = x.shape
    outs = {
        "n1t": ((width, length), BF16),
        "qkv": ((length, 3 * width), BF16),
        "e": ((H, length, length), BF16),
        "inv": ((16, length), F32),
        "mixed": ((length, width), F32),
        "z1t": ((width, length), BF16),
        "x2": ((length, width), F32),
        "n2t": ((width, length), BF16),
        "q2": ((length, width), BF16),
    }
    ins = dict(x=x, bias=bias, qkv_w=qkv_w, out_w=out_w, q2_w=q2_w, vecs=vecs)
    return stream_call(
        functools.partial(self_forward_kernel, item), "self_forward", ins, outs, after=after,
        scalars=(dec_len, prefix, mem_len, order), limit=40, token="inv",
    )


def sums_of(names, rows, parts, width):
    outs = {}
    for name, count in zip(names, rows):
        outs.update({f"{side}{name}": ((parts // 2, count, width), BF16) for side in ("sent", "kept")})
    return outs


def operand_pair(rows, depth, columns):
    return [pltpu.VMEM((rows, depth), BF16), pltpu.VMEM((depth, columns), BF16)]


def cross_forward(item, earlier, order, mem_len, dec_len, x2, q2, mem, cot, kv_w, out_w, in_w, ffn_w, vecs, wides, after):
    length, width = x2.shape
    items = cot.shape[0]
    last = item == items - 1
    mem_tokens = mem.shape[0]
    ff = in_w.shape[1]
    parts = order.shape[0] // 2
    outs = {
        "out": ((length, width), BF16),
        "kv": ((mem_tokens, 2 * width), BF16),
        "e": ((H, mem_tokens, length), BF16),
        "inv": ((16, length), F32),
        "mixed": ((length, width), F32),
        "memt": ((width, mem_tokens), BF16),
        "z2t": ((width, length), BF16),
        "gx3": ((length, width), F32),
        "branch": ((length, width), BF16),
        "vg": ((VEC_ROWS, width), F32),
    }
    operands = {
        "n3t": ((width, length), BF16),
        "hid": ((length, ff), BF16),
        "midt": ((ff, length), BF16),
        "cot_low": ((length, width), BF16),
    }
    ins = dict(
        x2=x2, q2=q2, mem=mem, cot=cot, kv_w=kv_w, out_w=out_w, in_w=in_w, ffn_w=ffn_w, vecs=vecs, wides=wides
    )
    scratch = [pltpu.VMEM((length, ff), F32)] + [pltpu.VMEM((length, ff), BF16)] * 3
    scalars, far, sums = (mem_len, dec_len), {}, {}
    if last:
        sums = sums_of("AC", (ff // parts, ff // parts), parts, width)
        outs.update(sums)
        scalars += (order,)
        far = {f"{n}{i}": earlier[i][n] for i in range(item) for n in operands}
        scratch = (
            operand_pair(ff, items * length, width)
            + operand_pair(width, items * length, ff)
            + [pltpu.SemaphoreType.DMA((item * (2 * parts + 2) + 2 * (1 + ff // width),))]
            + scratch
        )
    else:
        outs.update(operands)
    return stream_call(
        functools.partial(cross_forward_kernel, item, last), "cross_forward", ins, outs,
        scratch=scratch, after=after, scalars=scalars, limit=58 if last else 50, free=("mem",),
        gathered=dict(out=(items, earlier[item - 1].out if item else None)), far=far, parted=("cot",),
    )


def cross_back(item, items, earlier, starts, ahead, order, kv_w, out_w, q2_w, vecs, after):
    a, x2, q2 = ahead[item], starts[item].x2, starts[item].q2
    last = item == items - 1
    length, width = x2.shape
    mem_tokens = a.kv.shape[0]
    parts = order.shape[0] // 2
    outs = {
        "gmem": ((mem_tokens, width), BF16),
        "gx2": ((length, width), F32),
        "branch2": ((length, width), BF16),
        "vg": ((VEC_ROWS, width), F32),
    }
    operands = {"dq": ((length, width), BF16), "dkv": ((mem_tokens, 2 * width), BF16)}
    ins = dict(
        branch=a.branch, gx3=a.gx3, mixed=a.mixed, kv=a.kv, inv=a.inv, q2=q2, x2=x2,
        kv_w=kv_w, out_w=out_w, q2_w=q2_w, vecs=vecs,
    )
    scratch = [
        pltpu.VMEM(a.e.shape, a.e.dtype),
        pltpu.SemaphoreType.DMA((PAIRS,)),
        pltpu.VMEM((length, width), BF16),
        pltpu.VMEM((length, width), F32),
    ]
    scalars, far, sums = (), dict(e=a.e), {}
    if last:
        quarter = width // parts
        sums = sums_of("DG", (2 * quarter, 3 * quarter), parts, width)
        outs.update(sums)
        scalars = (order,)
        for i in range(items):
            far.update({f"memt{i}": ahead[i].memt, f"z2t{i}": ahead[i].z2t, f"branch{i}": ahead[i].branch})
            far.update({f"n2t{i}": starts[i].n2t, f"z1t{i}": starts[i].z1t})
            if i < item:
                b = earlier[i]
                far.update({f"dkv{i}": b.dkv, f"dq{i}": b.dq, f"branch2{i}": b.branch2})
        scratch = (
            operand_pair(width, items * mem_tokens, 2 * width)
            + operand_pair(width, items * length, width) * 3
            + [pltpu.SemaphoreType.DMA((items * (4 * parts + 1) + item * 3 + 2 * 5,))]
            + scratch
        )
    else:
        outs.update(operands)
    return stream_call(
        functools.partial(cross_back_kernel, item, last), "cross_back", ins, outs, scratch=scratch, after=after,
        scalars=scalars, limit=50 if last else 34, far=far,
    )


def self_back(starts, ahead, behind, order, x, qkv_w, out_w, vecs, buckets, after):
    items, length, width = x.shape
    parts = order.shape[0] // 2
    ins = dict(x=x, qkv_w=qkv_w, out_w=out_w, vecs=vecs, buckets=buckets)
    far = {}
    for item in range(items):
        a, b = starts[item], behind[item]
        ins.update({f"{name}{item}": a[name] for name in ("mixed", "qkv", "e", "inv")})
        ins.update({f"branch{item}": b.branch2, f"gx2{item}": b.gx2})
        far.update({f"n1t{item}": a.n1t, f"vgf{item}": ahead[item].vg, f"vgb{item}": b.vg})
    sums = sums_of("EH", (width // parts + VEC_ROWS, 2 * width // parts), parts, width)
    outs = {"gx": (x.shape, BF16), **sums}
    scratch = operand_pair(width, items * length, 3 * width) + [
        pltpu.VMEM((3 * items, VEC_ROWS, width), F32),
        pltpu.SemaphoreType.DMA((items * (parts + 2) + 2 * 4,)),
        pltpu.VMEM((length, width), BF16),
        pltpu.VMEM((length, width), F32),
        pltpu.VMEM((16, 2 * length), F32),
    ]
    return stream_call(
        functools.partial(self_back_kernel, items), "self_back", ins, outs, scratch=scratch, after=after,
        scalars=(order,), limit=40, far=far, token="keptE",
    )


def prepare_kernel(narrow, wide, *refs):
    ins, (vec_ref, wide_ref) = refs[: narrow + wide], refs[narrow + wide :]
    vec_ref[...] = jnp.zeros_like(vec_ref)
    wide_ref[...] = jnp.zeros_like(wide_ref)
    for row in range(narrow):
        vec_ref[row, :] = ins[row][...].astype(F32)
    for row in range(wide):
        wide_ref[row, :] = ins[narrow + row][...].astype(F32)


def prepare(vectors, wides, after):
    count = len(vectors) + len(wides)
    shapes = [
        pltpu.HBM((24, vectors[0].shape[0]), F32), pltpu.HBM((8, wides[0].shape[0]), F32)
    ]

    after_specs, after_args = token_args(after)

    def body(*refs):
        prepare_kernel(len(vectors), len(wides), *refs[:count], *refs[count + len(after) :])

    Chain.token = 0, False
    return pl.pallas_call(
        body, out_shape=shapes, in_specs=[VMEM] * count + after_specs, out_specs=[VMEM] * 2,
        name="prepare",
    )(*vectors, *wides, *after_args)


def rel_bias_rows(table, length):
    count, heads = table.shape
    place = jnp.arange(2 * length, dtype=jnp.int32)
    offset = jnp.where(place < length, -place, 2 * length - place)
    bucket = jnp.clip(offset, -(count // 2), count // 2 - 1) + count // 2
    one_hot = (jnp.arange(count, dtype=jnp.int32)[:, None] == bucket[None, :]).astype(F32)
    rows = jnp.dot(table.T.astype(F32), one_hot, precision=lax.Precision.HIGHEST)
    return jnp.pad(rows, ((0, 16 - heads), (0, 0)))


def bucket_lanes(length, count):
    offset = length - 1 - jnp.arange(2 * length, dtype=jnp.int32)
    bucket = jnp.clip(offset, -(count // 2), count // 2 - 1) + count // 2
    return (bucket[:, None] == jnp.arange(128, dtype=jnp.int32)[None, :]).astype(F32)


def gather_kernel(slots_ref, memory_ref, out_ref, sems):
    copies = [
        pltpu.make_async_copy(memory_ref.at[slots_ref[i]], out_ref.at[i], sems.at[i])
        for i in range(out_ref.shape[0])
    ]
    for copy in copies:
        copy.start()
    for copy in copies:
        copy.wait()


def gather_items(memory, slots, after):
    count = slots.shape[0]
    return call(
        gather_kernel, "gather_items", (), [Stored((count,) + memory.shape[1:], memory.dtype)],
        scratch=[pltpu.SemaphoreType.DMA((count,))], after=after, scalars=(slots,), far=(memory,), limit=8,
    )


def scatter_kernel(items, slots_ref, *refs):
    parts, out_ref, sems = refs[:items], refs[items], refs[items + 1]
    copies = []
    for p in range(parts[0].shape[0]):
        for j in range(items):
            i = p * items + j
            copies.append(pltpu.make_async_copy(parts[j].at[p], out_ref.at[slots_ref[i]], sems.at[i]))
    for copy in copies:
        copy.start()
    for copy in copies:
        copy.wait()


def scatter_items(parts, slots, after):
    count = slots.shape[0]
    return call(
        functools.partial(scatter_kernel, len(parts)), "scatter_items", (),
        [Stored((count,) + parts[0].shape[1:], parts[0].dtype)],
        scratch=[pltpu.SemaphoreType.DMA((count,))], after=after, scalars=(slots,), far=tuple(parts), limit=8,
    )


class Bundle:
    def __init__(self, shapes, width, parts, vectors=False):
        self.shapes, self.width, self.parts, self.vectors = shapes, width, parts, vectors
        self.blocks = []
        row = 0
        for index, (rows, columns) in enumerate(shapes):
            size = rows // parts
            for column in range(columns // width):
                self.blocks.append((index, column, row, size))
                row += size
        self.vector_row = row
        self.rows = row + (VEC_ROWS if vectors else 0)

    def halves(self, mine_ref, got_ref, own_side):
        half = mine_ref.shape[0]

        def rows_of(start, size):
            pieces = []
            while size:
                part = start // half
                take = min(size, (part + 1) * half - start)
                rows = slice(start - part * half, start - part * half + take)
                value = mine_ref[rows, :].astype(F32)
                if own_side is not None:
                    value = jnp.where(own_side == part, value, got_ref[rows, :].astype(F32))
                pieces.append(value)
                start, size = start + take, size - take
            return pieces

        return rows_of


def finish_kernel(bundles, columns, place_ref, *refs):
    number = len(bundles)
    has_vectors = any(bundle.vectors for bundle in bundles)
    if has_vectors:
        group_ref, refs = refs[0], refs[1:]
    pairs, outs = refs[: 2 * number], list(refs[2 * number :])
    if has_vectors:
        vec_ref, turned_ref = outs[-2:]

    def store(out_ref, pieces, cols):
        done = 0
        for piece in pieces:
            out_ref[done : done + piece.shape[0], cols] = piece
            done += piece.shape[0]

    for b, bundle in enumerate(bundles):
        mine_ref, got_ref = pairs[2 * b], pairs[2 * b + 1]
        whole_rows = mine_ref.shape[0] == bundle.rows
        rows_of = bundle.halves(mine_ref, got_ref, None if whole_rows else place_ref[0])
        for index, column, row, size in bundle.blocks:
            first = columns[b] + column * bundle.width
            out_ref = outs[index]
            store(out_ref, rows_of(row, size), slice(first, first + bundle.width))
        if bundle.vectors:
            store(vec_ref, rows_of(bundle.vector_row, VEC_ROWS), slice(None))
    if has_vectors:
        vectors_kernel(bundles[0].parts, group_ref, vec_ref, *outs[1:-2], turned_ref)


def finish(bundles, sums, place, vectors, after):
    first = bundles[0]
    if len(bundles) == 1:
        shapes, columns = first.shapes, [0]
    else:
        widths = [bundle.shapes[0][1] for bundle in bundles]
        shapes = [(first.shapes[0][0], sum(widths))]
        columns = [sum(widths[:b]) for b in range(len(bundles))]
    outs = [Stored((rows // first.parts, cols), F32) for rows, cols in shapes]
    scalars, scratch = (place,), ()
    if any(bundle.vectors for bundle in bundles):
        group, ff, buckets = vectors
        parts = first.parts
        outs += [Stored((first.width // parts,), F32)] * 17 + [Stored((ff // parts,), F32)] * 3
        outs += [Stored((H // parts,), F32)] * 2 + [Stored((buckets // parts, H), F32)]
        scalars += (group,)
        scratch = [pltpu.VMEM((VEC_ROWS, first.width), F32), pltpu.VMEM((128, 16), F32)]
    ins = []
    for mine, got in sums:
        ins += [mine, mine if got is None else got]
    return call(
        functools.partial(finish_kernel, bundles, columns), "finish", tuple(ins), outs,
        scratch=scratch, after=after, scalars=scalars, limit=14,
    )


def add_low(left, right):
    return left + right


def first_add_kernel(split, side_ref, left_ref, right_ref, *refs):
    refs = refs[-5:]
    sent_ref, kept_ref, near_left, near_right, sems = refs
    rows = near_left.shape[1]
    half = rows // 2
    copies = []
    for quarter in range(2):
        for part in range(2):
            place = pl.ds(part * half, half)
            if split:
                place = pl.ds(pl.multiple_of((part ^ 1 ^ side_ref[0]) * half, 16), half)
            for far, near in ((left_ref, near_left), (right_ref, near_right)):
                copies.append(
                    pltpu.make_async_copy(
                        far.at[quarter, place, :], near.at[quarter, pl.ds(part * half, half), :],
                        sems.at[len(copies)],
                    )
                )
    for copy in copies:
        copy.start()
    for quarter in range(2):
        for part in range(2):
            for copy in copies[:2]:
                copy.wait()
            copies = copies[2:]
            rows = slice(part * half, (part + 1) * half)
            value = add_low(near_left[quarter, rows, :], near_right[quarter, rows, :])
            if split:
                (sent_ref, kept_ref)[part][quarter] = value
            else:
                (sent_ref, kept_ref)[quarter][rows, :] = value


def first_add(left, right, side, split, after):
    shape = (2, left.shape[1] // 2, left.shape[2]) if split else left.shape[1:]
    after_specs, after_args = token_args(after)
    Chain.token = 1, True
    return pl.pallas_call(
        functools.partial(first_add_kernel, split),
        out_shape=[pltpu.VMEM(shape, BF16)] * 2,
        in_specs=[SMEM, HBM, ANY] + after_specs,
        out_specs=[VMEM] * 2,
        scratch_shapes=[pltpu.VMEM(left.shape, BF16)] * 2 + [pltpu.SemaphoreType.DMA((8,))],
        compiler_params=pltpu.CompilerParams(vmem_limit_bytes=10 * MIB),
        cost_estimate=cost_of("first_add"),
        name="first_add",
    )(side, pltpu.with_memory_space_constraint(left, pltpu.HBM), right, *after_args)


def core_add_kernel(left_ref, right_ref, sent_ref, kept_ref):
    sent_ref[...] = add_low(left_ref[0], right_ref[0])
    kept_ref[...] = add_low(left_ref[1], right_ref[1])


def core_add(left, right, after):
    shape = left.shape[1:]
    return call(core_add_kernel, "core_add", (left, right), [Kept(shape, BF16)] * 2, after=after, limit=8)


def split_add_kernel(side_ref, left_ref, right_ref, sent_ref, kept_ref):
    half = sent_ref.shape[0]
    mine = pl.ds(pl.multiple_of(side_ref[0] * half, 16), half)
    other = pl.ds(pl.multiple_of((1 - side_ref[0]) * half, 16), half)
    sent_ref[...] = add_low(left_ref[other, :], right_ref[other, :])
    kept_ref[...] = add_low(left_ref[mine, :], right_ref[mine, :])


def split_add(left, right, side, after):
    shape = (left.shape[0] // 2, left.shape[1])
    return call(
        split_add_kernel, "split_add", (left, right), [Kept(shape, BF16)] * 2,
        after=after, scalars=(side,), limit=8,
    )


def join_kernel(side_ref, mine_ref, got_ref, out_ref):
    half = mine_ref.shape[0]
    mine = pl.ds(pl.multiple_of(side_ref[0] * half, 16), half)
    other = pl.ds(pl.multiple_of((1 - side_ref[0]) * half, 16), half)
    out_ref[mine, :] = mine_ref[...]
    out_ref[other, :] = got_ref[...]


def join(mine, got, side, after):
    shape = (2 * mine.shape[0], mine.shape[1])
    return call(
        join_kernel, "join", (mine, got), [Kept(shape, BF16)], after=after, scalars=(side,), limit=4
    )


def add_kernel(left_ref, right_ref, out_ref):
    out_ref[...] = add_low(left_ref[...], right_ref[...])


def add(left, right, after):
    return call(add_kernel, "add", (left, right), [Kept(left.shape, BF16)], after=after, limit=4)


def pick_kernel(own_ref, mine_ref, got_ref, out_ref):
    @pl.when(own_ref[0] == 1)
    def _():
        out_ref[...] = mine_ref[...]

    @pl.when(own_ref[0] != 1)
    def _():
        out_ref[...] = got_ref[...]


def pick(mine, got, own, after):
    return call(
        pick_kernel, "pick", (mine, got), [Kept(mine.shape, BF16)], after=after, scalars=(own,), limit=4
    )


def vectors_kernel(parts, group_ref, vec_ref, *refs):
    outs, scratch = refs[:-1], refs[-1]
    group = group_ref[0]
    width = vec_ref.shape[1]
    size = width // parts
    values = vec_ref[...]
    rolled = pltpu.roll(values, lax.rem(width - size * group, width), 1)
    narrow = [row for row in range(FFN_OB + 1) if row not in (SELF_HEAD, CROSS_HEAD)]
    for out, row in zip(outs, narrow):
        out[...] = rolled[row, :size]
    outs = outs[len(narrow) :]
    tiles = outs[0].shape[0] * parts // width
    for out, row in zip(outs, (IN_BIAS, MID_GAIN, MID_SHIFT)):
        if tiles == parts:
            out[...] = vec_ref[pl.ds(row + group, 1), :][0]
    heads = H // parts
    lane = lax.broadcasted_iota(jnp.int32, (width, 128), 0) // HD
    one_hot = (lane == lax.broadcasted_iota(jnp.int32, (width, 128), 1)).astype(F32)
    sums = jnp.dot(values, one_hot, precision=lax.Precision.HIGHEST, preferred_element_type=F32)
    sums = pltpu.roll(sums, lax.rem(128 - heads * group, 128), 1)
    outs[3][...] = sums[SELF_HEAD, :heads]
    outs[4][...] = sums[CROSS_HEAD, :heads]
    scratch[...] = values[TABLE : TABLE + 16, :128].T
    buckets = outs[5].shape[0]
    outs[5][...] = scratch[pl.ds(pl.multiple_of(buckets * group, buckets), buckets), :][:, :H]


CORE_PAIRS = [(0, 1), (1, 0), (2, 3), (3, 2)]
Y_PAIRS = [(0, 2), (2, 0), (1, 3), (3, 1)]
X_PAIRS = [(0, 1), (1, 0), (2, 3), (3, 2), (4, 5), (5, 4), (6, 7), (7, 6)]
Z_IN = [(0, 2), (1, 3), (6, 4), (7, 5)]
Z_MID = [(2, 4), (4, 2), (3, 5), (5, 3)]
Z_OUT = [(2, 0), (3, 1), (4, 6), (5, 7)]
Z_NEAR = [(0, 2), (2, 0), (1, 3), (3, 1), (4, 6), (6, 4), (5, 7), (7, 5)]
Z_FAR = [(0, 4), (4, 0), (1, 5), (5, 1), (2, 6), (6, 2), (3, 7), (7, 3)]


ROUTE = dict(A="YH", C="XH", D="XH", G="YH", E="XH", H="YH")
STEPS = [
    ("F0", 30), ("B0", 30), ("F1", 0), ("A1", 3), ("C1", 0), ("B1", 13), ("A2", 2), ("C2", 20), ("S", 5),
    ("C3", 1), ("G1", 2), ("D1", 1), ("A3", 3), ("C4", 1), ("SC", 5), ("E1", 0.2), ("A4", 1), ("H1", 0.5),
    ("D2", 1), ("G2", 1), ("C5", 3), ("E2", 3), ("H2", 0), ("G3", 0), ("A5", 1), ("E3", 0.5), ("C6", 0),
    ("G4", 1), ("H3", 2), ("A6", 0.2), ("D3", 0.5), ("D4", 0), ("G5", 0.5), ("H4", 0), ("C7", 1), ("D5", 1),
    ("G6", 1), ("E4", 0.2), ("A7", 1), ("H5", 2), ("D6", 0.2), ("E5", 3), ("G7", 0.5), ("H6", 1), ("D7", 0.2),
    ("E6", 0), ("E7", 0),
]


class Chain:
    def __init__(self):
        self.last = ()

    def run(self, function, *args, also=(), cost=None):
        Chain.cost = cost
        result = function(*args, after=self.last + tuple(also))
        Chain.cost = None
        index, near = Chain.token
        arrays = Chain.flat(result)
        self.last = (Token(arrays[index], near),)
        return result

    @staticmethod
    def flat(result):
        return jax.tree.leaves(list(result.values()) if isinstance(result, dict) else result)

    cost = None
    token = None


def cost_of(name):
    us = COST.get(name, 1) if Chain.cost is None else Chain.cost
    return pl.CostEstimate(flops=int(us * 1_000_000_000), bytes_accessed=1000, transcendentals=0)


def local(
    dec_in,
    memory,
    cotangent,
    dec_len,
    task_prefix,
    owner,
    mem_len,
    self_norm_gain,
    self_norm_shift,
    self_qkv,
    self_q_bias,
    self_v_bias,
    rel_bias_table,
    self_head_gain,
    self_mix_gain,
    self_mix_shift,
    self_out,
    self_out_bias,
    cross_norm_gain,
    cross_norm_shift,
    cross_q,
    cross_q_bias,
    cross_kv,
    cross_v_bias,
    cross_head_gain,
    cross_mix_gain,
    cross_mix_shift,
    cross_out,
    cross_out_bias,
    ffn_norm_gain,
    ffn_norm_shift,
    ffn_in,
    ffn_in_bias,
    ffn_mid_gain,
    ffn_mid_shift,
    ffn_out,
    ffn_out_bias,
):
    items, length, width = dec_in.shape
    items_grp = owner.shape[1]
    shard_tokens = memory.shape[1]
    seq_size = lax.axis_size("seq")
    parts = lax.axis_size("grp")
    mem_tokens = shard_tokens * seq_size
    ff = ffn_in.shape[1]
    group = lax.axis_index("grp")
    seq_index = lax.axis_index("seq")
    paired = seq_size == 8 and parts == 4 and items == 2

    owner_row = lax.dynamic_index_in_dim(owner, group, 0, keepdims=False)
    slots = jnp.arange(items_grp, dtype=jnp.int32)
    inverse = jnp.sum(jnp.where(owner_row[None, :] == slots[:, None], slots[None, :], 0), axis=1)
    mine = lax.dynamic_slice_in_dim(inverse, seq_index * items, items)
    my_mem_len = jnp.take(mem_len, group * items_grp + mine)

    def exchange(sent):
        return lax.all_to_all(sent, "seq", split_axis=0, concat_axis=0, tiled=True)

    chain = Chain()
    by_item = inverse.reshape(seq_size, items)
    memories = []

    def gather(item):
        sent = chain.run(gather_items, memory, by_item[:, item])[0]
        memories.append(exchange(sent).reshape(mem_tokens, width))

    gather(0)

    def spread(gain):
        return jnp.repeat(gain, HD)

    vectors = [
        self_norm_gain, self_norm_shift, self_q_bias, self_v_bias, spread(self_head_gain),
        self_mix_gain, self_mix_shift, self_out_bias, cross_norm_gain, cross_norm_shift,
        cross_q_bias, cross_v_bias, spread(cross_head_gain), cross_mix_gain, cross_mix_shift,
        cross_out_bias, ffn_norm_gain, ffn_norm_shift, ffn_out_bias,
    ]
    vecs, wides = chain.run(prepare, vectors, [ffn_in_bias, ffn_mid_gain, ffn_mid_shift])
    bias = rel_bias_rows(rel_bias_table, length)
    buckets = bucket_lanes(length, rel_bias_table.shape[0])

    core, y = group % 2, group // 2
    x, z = seq_index % 2, seq_index // 2
    if paired:
        order = jnp.stack([(1 - y) * 2 + 1 - core, y * 2 + 1 - core, (1 - y) * 2 + core, y * 2 + core])
        places = jnp.sum(jnp.where(order[None, :] == jnp.arange(parts)[:, None], jnp.arange(parts)[None, :], 0), axis=1)
    else:
        order = places = jnp.arange(parts)
    order = jnp.concatenate([order, places]).astype(jnp.int32)

    starts = [
        chain.run(
            self_forward, item, dec_len, task_prefix, my_mem_len, order, dec_in, bias, self_qkv, self_out,
            cross_q, vecs,
        )
        for item in range(items)
    ]
    for item in range(1, items):
        gather(item)

    bundles = dict(
        A=Bundle([ffn_out.shape], width, parts),
        C=Bundle([ffn_in.shape], width, parts),
        D=Bundle([cross_kv.shape], width, parts),
        G=Bundle([cross_out.shape, cross_q.shape, self_out.shape], width, parts),
        E=Bundle([(width, width)], width, parts, vectors=True),
        H=Bundle([(width, 2 * width)], width, parts),
    )
    ahead, behind, returned, ends, state, done = {}, {}, {}, {}, {}, {}

    def start_sums(result, names):
        for name in names:
            sent, kept = result[f"sent{name}"], result[f"kept{name}"]
            state[name] = (kept, lax.ppermute(sent, "grp", CORE_PAIRS)) if paired else (sent, kept)

    def forward(item, **how):
        ahead[item] = chain.run(
            cross_forward, item, ahead, order, my_mem_len, dec_len, starts[item].x2, starts[item].q2,
            memories[item], cotangent, cross_kv, cross_out, ffn_in, ffn_out, vecs, wides, **how,
        )
        if item == items - 1:
            start_sums(ahead[item], "AC")

    def backward(item, **how):
        behind[item] = chain.run(
            cross_back, item, items, behind, starts, ahead, order, cross_kv, cross_out, cross_q, vecs, **how
        )
        returned[item] = exchange(behind[item].gmem.reshape(seq_size, shard_tokens, width))
        if item == items - 1:
            start_sums(behind[item], "DG")

    def self_backward(**how):
        ends.update(
            chain.run(
                self_back, starts, ahead, behind, order, dec_in, self_qkv, self_out, vecs, buckets, **how
            )
        )
        start_sums(ends, "EH")

    def scatter_memory(**how):
        return chain.run(scatter_items, [returned[i] for i in range(items)], inverse, **how)[0]

    small = group.reshape(1), ff, rel_bias_table.shape[0]
    if paired:
        side, z_side = x.reshape(1), (z % 2).reshape(1)
        inner = ((z == 1) | (z == 2)).astype(jnp.int32).reshape(1)

        def reduce_step(name, step, **how):
            along_y = step == (1 if ROUTE[name][0] == "Y" else 2)
            if step == 1:
                sent, kept = chain.run(first_add, *state[name], side, not along_y, **how)
                axis, pairs = ("grp", Y_PAIRS) if along_y else ("seq", X_PAIRS)
            elif step == 2:
                if along_y:
                    sent, kept = chain.run(core_add, *state[name], **how)
                else:
                    sent, kept = chain.run(split_add, *state[name], side, **how)
                axis, pairs = ("grp", Y_PAIRS) if along_y else ("seq", X_PAIRS)
            elif step == 3 and ROUTE[name][1] == "H":
                sent, kept = chain.run(split_add, *state[name], z_side, **how)
                axis, pairs = "seq", Z_NEAR
            elif step in (4, 5) and ROUTE[name][1] == "H":
                sent = kept = chain.run(add, *state[name], **how)[0]
                axis, pairs = "seq", Z_FAR if step == 4 else Z_NEAR
            elif step == 6 and ROUTE[name][1] == "H":
                sent = kept = chain.run(join, *state[name], z_side, **how)[0]
                axis, pairs = "seq", X_PAIRS
            elif step in (3, 4, 5):
                sent = kept = chain.run(add, *state[name], **how)[0]
                axis, pairs = "seq", (Z_IN, Z_MID, Z_OUT)[step - 3]
            elif step == 6:
                sent = kept = chain.run(pick, *state[name], inner, **how)[0]
                axis, pairs = "seq", X_PAIRS
            else:
                names = "EH" if name == "E" else name
                done[name] = chain.run(
                    finish, [bundles[n] for n in names], [state[n] for n in names], side, small, **how
                )
                return
            state[name] = kept, lax.ppermute(sent, axis, pairs)

        for step, cost in STEPS:
            if step[0] == "F":
                forward(int(step[1]), cost=cost)
            elif step[0] == "B":
                backward(int(step[1]), cost=cost)
            elif step == "S":
                self_backward(cost=cost)
            elif step == "SC":
                grad_memory = scatter_memory(cost=cost)
            else:
                reduce_step(step[0], int(step[1]), cost=cost)
    else:
        for item in range(items):
            forward(item)
            backward(item)
        self_backward()
        none = jnp.zeros((1,), jnp.int32)
        for name in ROUTE:
            share = lax.psum_scatter(jnp.concatenate(state[name]), "grp", scatter_dimension=0, tiled=True)[0]
            state[name] = lax.psum(share, "seq"), None
        for names in ("A", "C", "D", "G", "EH"):
            done[names[0]] = chain.run(finish, [bundles[n] for n in names], [state[n] for n in names], none, small)
        grad_memory = scatter_memory()

    out, gx = ahead[items - 1].out, ends["gx"]
    g_ffn_out, g_ffn_in, g_cross_kv = (done[name][0] for name in ("A", "C", "D"))
    g_cross_out, g_cross_q, g_self_out = done["G"]
    g_self_qkv = done["E"][0]
    (
        g_self_norm_gain, g_self_norm_shift, g_self_q_bias, g_self_v_bias, g_self_mix_gain,
        g_self_mix_shift, g_self_out_bias, g_cross_norm_gain, g_cross_norm_shift, g_cross_q_bias,
        g_cross_v_bias, g_cross_mix_gain, g_cross_mix_shift, g_cross_out_bias, g_ffn_norm_gain,
        g_ffn_norm_shift, g_ffn_out_bias, g_ffn_in_bias, g_ffn_mid_gain, g_ffn_mid_shift,
        g_self_head, g_cross_head, g_table,
    ) = done["E"][1:]
    return (
        out,
        gx,
        grad_memory,
        g_self_norm_gain,
        g_self_norm_shift,
        g_self_qkv,
        g_self_q_bias,
        g_self_v_bias,
        g_table,
        g_self_head,
        g_self_mix_gain,
        g_self_mix_shift,
        g_self_out,
        g_self_out_bias,
        g_cross_norm_gain,
        g_cross_norm_shift,
        g_cross_q,
        g_cross_q_bias,
        g_cross_kv,
        g_cross_v_bias,
        g_cross_head,
        g_cross_mix_gain,
        g_cross_mix_shift,
        g_cross_out,
        g_cross_out_bias,
        g_ffn_norm_gain,
        g_ffn_norm_shift,
        g_ffn_in,
        g_ffn_in_bias,
        g_ffn_mid_gain,
        g_ffn_mid_shift,
        g_ffn_out,
        g_ffn_out_bias,
    )


def solution(mesh):
    rows = P(("seq", "grp"), None, None)
    matrix, vector = P("grp", None), P("grp")
    in_specs = (rows, P("grp", "seq", None), rows, P(("seq", "grp")), P(("seq", "grp"))) + (P(),) * 32
    out_specs = (
        rows, rows, P("grp", "seq", None),
        vector, vector, matrix, vector, vector, matrix, vector, vector, vector, matrix, vector,
        vector, vector, matrix, vector, matrix, vector, vector, vector, vector, matrix, vector,
        vector, vector, matrix, vector, vector, vector, matrix, vector,
    )
    return jax.shard_map(local, mesh=mesh, in_specs=in_specs, out_specs=out_specs, check_vma=False)
```
